256 devices in a mesh: leaf: 64 (over z, x, y_lo), sub: 4 (over y_hi, core).
Axes of the slice: x: 4, y: 4 (y_hi: 2, y_lo: 2; y = y_hi * 2 + y_lo), z: 8, core: 2. Of those that a mesh axis runs over, the one named last changes fastest.
Arguments:
- right_sides: bfloat16 [64, 262144], P(None, ('leaf', 'sub')), may hold values from -6 to 6
- leaf_basis: bfloat16 [64, 262144], P(None, ('leaf', 'sub')), may hold values from -0.75 to 0.75
- near_blocks: bfloat16 [4096, 8, 4096], P(('leaf', 'sub')), may hold values from -0.25 to 0.25
- near_list: int32 [4096, 8], P(('leaf', 'sub')), may hold values from 0 to 4095, as said below
- local_transfer: bfloat16 [7936, 4096], P(('leaf', 'sub')), may hold values from -0.5 to 0.5
- local_couple: bfloat16 [7936, 8, 4096], P(('leaf', 'sub')), may hold values from -0.375 to 0.375
- local_partner: int32 [7936, 8], P(('leaf', 'sub')), may hold values from 0 to 7935, as said below
- local_count: int32 [7936], P(('leaf', 'sub')), may hold values from 1 to 8, as said below
- group_transfer: bfloat16 [192, 4096], P('leaf'), may hold values from -0.5 to 0.5
- group_couple: bfloat16 [192, 4, 4096], P('leaf'), may hold values from -1 to 1
- group_partner: int32 [192, 4], P('leaf'), may hold values from 0 to 191, as said below
- group_count: int32 [192], P('leaf'), may hold values from 1 to 4, as said below
- top_transfer: bfloat16 [62, 4096], replicated, may hold values from -0.5 to 0.5
- top_couple: bfloat16 [63, 3, 4096], replicated, may hold values from -1 to 1
- top_partner: int32 [63, 3], replicated, may hold values from 0 to 62, as said below
- top_count: int32 [63], replicated, may hold values from 0 to 3, as said below
Outputs:
- product: float32 [64, 262144], P(None, ('leaf', 'sub'))
The draws below stay inside these ranges and needn't reach their ends.
Inputs may be any that keep to these rules, and one draw needn't show every extreme that they name: `near_list`: entry (t, k) names a leaf at most 8 places from leaf t in tree order. `local_partner`: entry (c, k) names a cluster of the same level as c, other than c, in c's own subtree or in the subtree just before or just after it. Only the first local_count slots of row c are used; in every subtree some cluster uses all 8. `group_partner`: entry (c, k) names a group cluster of the same level as c, other than c, in c's group or in the group just before or just after it. Only the first group_count slots of row c are used; some cluster uses all 4. `top_partner`: entry (c, k) names a top cluster of the same level as c, other than c; the root names itself. Only the first top_count slots of row c are used; a count is below the number of clusters on c's level, so the root has none; some cluster of the first top level uses all 3.
All inputs are finite; a program needn't handle non-finite values.
Results may differ from the reference program's by a relative error of at most 0.024.
Values may be sent and summed in bfloat16 or wider, within the bound.
A program may use at most 128 MiB of HBM per device.

```python
import jax
import jax.numpy as jnp
import numpy as np
from jax import lax

LEAF = 64
RANK = 64
RHS = 64
LEAF_DEV = 16
NEAR = 8
COUPLE = 8
GCOUPLE = 4
TCOUPLE = 3
NEARW = 8
NLEAVES = 4096
NPTS = 262144
LOCCL = 31
GROUPS = 64
TOPCL = 63
DEVICES = 256


def level_table(number):
    level_sizes = []
    level_starts = []
    offset = 0
    while number >= 1:
        level_sizes = level_sizes + [number] * number
        level_starts = level_starts + [offset] * number
        offset = offset + number
        number = number // 2
    return (np.array(level_sizes, np.int32), np.array(level_starts, np.int32))


def draw_near_list(key, part):
    key = jax.random.fold_in(key, 11)
    leaf_ids = jnp.arange(NLEAVES, dtype=jnp.int32)[:, None]
    offsets = jax.random.randint(key, (NLEAVES, NEAR), -NEARW, NEARW + 1, dtype=jnp.int32)
    return jnp.clip(leaf_ids + offsets, 0, NLEAVES - 1)


def draw_local_partner(key, part):
    key = jax.random.fold_in(key, 12)
    devices = NLEAVES // LEAF_DEV
    level_sizes, level_starts = level_table(LEAF_DEV)
    key_step, key_pick = jax.random.split(key)
    extent = (devices, LOCCL, COUPLE)
    device_ids = jnp.arange(devices, dtype=jnp.int32)[:, None, None]
    position = jnp.arange(LOCCL, dtype=jnp.int32)[None, :, None]
    span_size = jnp.asarray(level_sizes)[None, :, None]
    span_start = jnp.asarray(level_starts)[None, :, None]
    stride = jax.random.randint(key_step, extent, -1, 2, dtype=jnp.int32)
    stride = jnp.where((stride == 0) & (span_size == 1), 1, stride)
    target = device_ids + stride
    stride = jnp.where((target < 0) | (target >= devices), -stride, stride)
    choose = jax.random.randint(key_pick, extent, 0, 1 << 20, dtype=jnp.int32) % span_size
    own_place = position - span_start
    choose = jnp.where((stride == 0) & (choose == own_place), (choose + 1) % span_size, choose)
    return ((device_ids + stride) * LOCCL + span_start + choose).reshape(devices * LOCCL, COUPLE)


def draw_local_count(key, part):
    key = jax.random.fold_in(key, 13)
    devices = NLEAVES // LEAF_DEV
    key_count, key_full = jax.random.split(key)
    counts = jax.random.randint(key_count, (devices, LOCCL), 1, COUPLE + 1, dtype=jnp.int32)
    fullest = jax.random.randint(key_full, (devices, 1), 0, LOCCL, dtype=jnp.int32)
    position = jnp.arange(LOCCL, dtype=jnp.int32)[None, :]
    return jnp.where(position == fullest, COUPLE, counts).reshape(devices * LOCCL)


def draw_group_partner(key, part):
    key = jax.random.fold_in(key, 14)
    key_step, key_half = jax.random.split(key)
    extent = (GROUPS, 3, GCOUPLE)
    group_ids = jnp.arange(GROUPS, dtype=jnp.int32)[:, None, None]
    member = jnp.arange(3, dtype=jnp.int32)[None, :, None]
    stride = jax.random.randint(key_step, extent, -1, 2, dtype=jnp.int32)
    stride = jnp.where((stride == 0) & (member == 2), 1, stride)
    target = group_ids + stride
    stride = jnp.where((target < 0) | (target >= GROUPS), -stride, stride)
    halves = jax.random.randint(key_half, extent, 0, 2, dtype=jnp.int32)
    halves = jnp.where((stride == 0) & (halves == member), 1 - halves, halves)
    within = jnp.where(member == 2, 2, halves)
    return ((group_ids + stride) * 3 + within).reshape(GROUPS * 3, GCOUPLE)


def draw_group_count(key, part):
    key = jax.random.fold_in(key, 15)
    key_count, key_full = jax.random.split(key)
    counts = jax.random.randint(key_count, (3 * GROUPS,), 1, GCOUPLE + 1, dtype=jnp.int32)
    fullest = jax.random.randint(key_full, (), 0, 3 * GROUPS, dtype=jnp.int32)
    return jnp.where(jnp.arange(3 * GROUPS, dtype=jnp.int32) == fullest, GCOUPLE, counts)


def draw_top_partner(key, part):
    key = jax.random.fold_in(key, 16)
    level_sizes, level_starts = level_table(GROUPS // 2)
    span_size = jnp.asarray(level_sizes)[:, None]
    span_start = jnp.asarray(level_starts)[:, None]
    position = jnp.arange(TOPCL, dtype=jnp.int32)[:, None]
    jumps = jax.random.randint(key, (TOPCL, TCOUPLE), 0, 1 << 20, dtype=jnp.int32) % jnp.maximum(span_size - 1, 1) + 1
    return span_start + (position - span_start + jumps) % span_size


def draw_top_count(key, part):
    key = jax.random.fold_in(key, 17)
    level_sizes, level_starts = level_table(GROUPS // 2)
    key_count, key_full = jax.random.split(key)
    counts = jax.random.randint(key_count, (TOPCL,), 1, TCOUPLE + 1, dtype=jnp.int32)
    counts = jnp.minimum(counts, jnp.asarray(level_sizes) - 1)
    fullest = jax.random.randint(key_full, (), 0, GROUPS // 2, dtype=jnp.int32)
    return jnp.where(jnp.arange(TOPCL, dtype=jnp.int32) == fullest, TCOUPLE, counts)


def steps_of(stream_key, dims, cuts, low, largest):
    def one(dim, shards_of):
        heights = jax.random.uniform(jax.random.fold_in(jax.random.fold_in(stream_key, 6), dim), (shards_of,), jnp.float32, low / len(cuts), largest / len(cuts))
        return jnp.repeat(jnp.exp(heights), dims[dim] // shards_of).reshape((-1,) + (1,) * (len(dims) - dim - 1))

    loudness = one(*cuts[0])
    for cut in cuts[1:]:
        loudness = loudness * one(*cut)
    return loudness


def centred(rng, shape, spread, limit, cuts=(), held_as=jnp.bfloat16):
    factor_of = steps_of(rng, shape, cuts, -0.22, 0.18) if cuts else 1.0
    values = jax.random.normal(rng, shape, jnp.float32) * spread * factor_of
    return jnp.minimum(jnp.maximum(values, -limit), limit).astype(held_as)


def setup_inputs(seed: int = 0) -> dict:
    seeds = jax.random.split(jax.random.key(seed), 17)
    right_sides = centred(seeds[0], (RHS, NPTS), 1.0, 6.0, ((1, 256),))
    leaf_basis = centred(seeds[1], (RANK, NPTS), LEAF ** -0.5, 0.75, ((1, 256),))
    near_blocks = centred(seeds[2], (NLEAVES, NEAR, LEAF * LEAF), (LEAF * NEAR) ** -0.5, 0.25, ((0, 256),))
    near_list = draw_near_list(jax.random.fold_in(seeds[16], 71), 0)
    local_transfer = centred(seeds[4], (LOCCL * DEVICES, RANK * RANK), (2 * RANK) ** -0.5, 0.5, ((0, 256),))
    local_couple = centred(seeds[5], (LOCCL * DEVICES, COUPLE, RANK * RANK), (RANK * COUPLE // 2) ** -0.5, 0.375, ((0, 256),))
    local_partner = draw_local_partner(jax.random.fold_in(seeds[16], 71), 0)
    local_count = draw_local_count(jax.random.fold_in(seeds[16], 71), 0)
    group_transfer = centred(seeds[8], (3 * GROUPS, RANK * RANK), (2 * RANK) ** -0.5, 0.5, ((0, 64),))
    group_couple = centred(seeds[9], (3 * GROUPS, GCOUPLE, RANK * RANK), (RANK // 2) ** -0.5, 1.0, ((0, 64),))
    group_partner = draw_group_partner(jax.random.fold_in(seeds[16], 71), 0)
    group_count = draw_group_count(jax.random.fold_in(seeds[16], 71), 0)
    top_transfer = centred(seeds[12], (TOPCL - 1, RANK * RANK), (2 * RANK) ** -0.5, 0.5)
    top_couple = centred(seeds[13], (TOPCL, TCOUPLE, RANK * RANK), (RANK // 2) ** -0.5, 1.0)
    top_partner = draw_top_partner(jax.random.fold_in(seeds[16], 71), 0)
    top_count = draw_top_count(jax.random.fold_in(seeds[16], 71), 0)
    return dict(right_sides=right_sides, leaf_basis=leaf_basis, near_blocks=near_blocks, near_list=near_list, local_transfer=local_transfer, local_couple=local_couple, local_partner=local_partner, local_count=local_count, group_transfer=group_transfer, group_couple=group_couple, group_partner=group_partner, group_count=group_count, top_transfer=top_transfer, top_couple=top_couple, top_partner=top_partner, top_count=top_count)


def blocks(packed, height, across):
    return packed.reshape(packed.shape[:-1] + (height, across))


def ladder(number):
    pieces = []
    offset = 0
    while number >= 1:
        pieces.append((offset, number))
        offset = offset + number
        number = number // 2
    return pieces


def stored(values):
    return lax.optimization_barrier(values.astype(jnp.bfloat16))


def pair_sum(values):
    return values.reshape((values.shape[0] // 2, 2) + values.shape[1:]).sum(axis=1)


def couple_terms(source, couple, partner, counts):
    gathered = source[partner]
    slot_ids = lax.broadcasted_iota(jnp.int32, partner.shape, 1)
    active = slot_ids < counts[:, None]
    gathered = jnp.where(active[:, :, None, None], gathered, jnp.zeros_like(gathered))
    return jnp.einsum('nkab,nkbr->nar', blocks(couple, RANK, RANK).astype(jnp.float32), gathered.astype(jnp.float32))


def reference(right_sides, leaf_basis, near_blocks, near_list, local_transfer, local_couple, local_partner, local_count, group_transfer, group_couple, group_partner, group_count, top_transfer, top_couple, top_partner, top_count):
    devices = NLEAVES // LEAF_DEV
    basis_rows = leaf_basis.astype(jnp.float32).reshape(RANK, NLEAVES, LEAF)
    points = right_sides.astype(jnp.float32).reshape(RHS, NLEAVES, LEAF)
    leaf_coef = stored(jnp.einsum('klp,rlp->lkr', basis_rows, points))
    transfer = blocks(local_transfer, RANK, RANK).reshape(devices, LOCCL, RANK, RANK).astype(jnp.float32)
    level_spans = ladder(LEAF_DEV)
    levels = [leaf_coef.reshape(devices, LEAF_DEV, RANK, RHS)]
    for offset, amount in level_spans[:-1]:
        lifted = jnp.einsum('dnab,dnar->dnbr', transfer[:, offset:offset + amount], levels[-1].astype(jnp.float32))
        levels.append(stored(lifted.reshape(devices, amount // 2, 2, RANK, RHS).sum(axis=2)))
    source_table = jnp.concatenate(levels, axis=1).reshape(devices * LOCCL, RANK, RHS)

    def local_block(pieces):
        return couple_terms(source_table, pieces[0], pieces[1], pieces[2])

    local_far = lax.map(local_block, (local_couple.reshape(devices, LOCCL, COUPLE, RANK * RANK), local_partner.reshape(devices, LOCCL, COUPLE), local_count.reshape(devices, LOCCL)))

    root_terms = jnp.einsum('dab,dar->dbr', transfer[:, LOCCL - 1], levels[-1][:, 0].astype(jnp.float32))
    first_level = stored(pair_sum(root_terms)).reshape(GROUPS, 2, RANK, RHS)
    group_trans = blocks(group_transfer, RANK, RANK).reshape(GROUPS, 3, RANK, RANK).astype(jnp.float32)
    second_level = stored(jnp.einsum('ghab,ghar->gbr', group_trans[:, :2], first_level.astype(jnp.float32)))
    group_table = jnp.concatenate([first_level, second_level[:, None]], axis=1).reshape(3 * GROUPS, RANK, RHS)
    group_far = couple_terms(group_table, group_couple, group_partner, group_count).reshape(GROUPS, 3, RANK, RHS)
    upper_terms = jnp.einsum('gab,gar->gbr', group_trans[:, 2], second_level.astype(jnp.float32))

    top_trans = blocks(top_transfer, RANK, RANK).astype(jnp.float32)
    top_spans = ladder(GROUPS // 2)
    current = stored(pair_sum(upper_terms))
    top_levels = [current]
    for offset, amount in top_spans[:-1]:
        lifted = jnp.einsum('nab,nar->nbr', top_trans[offset:offset + amount], current.astype(jnp.float32))
        current = stored(pair_sum(lifted))
        top_levels.append(current)
    top_table = jnp.concatenate(top_levels, axis=0)
    top_far = couple_terms(top_table, top_couple, top_partner, top_count)

    root_offset = top_spans[-1][0]
    descend = top_far[root_offset:root_offset + 1]
    for offset, amount in reversed(top_spans[:-1]):
        parent = jnp.repeat(stored(descend), 2, axis=0).astype(jnp.float32)
        descend = top_far[offset:offset + amount] + jnp.einsum('nab,nbr->nar', top_trans[offset:offset + amount], parent)
    parent = jnp.repeat(stored(descend), 2, axis=0).astype(jnp.float32)
    second_down = group_far[:, 2] + jnp.einsum('gab,gbr->gar', group_trans[:, 2], parent)
    first_down = group_far[:, :2] + jnp.einsum('ghab,gbr->ghar', group_trans[:, :2], stored(second_down).astype(jnp.float32))
    parent = jnp.repeat(stored(first_down.reshape(2 * GROUPS, RANK, RHS)), 2, axis=0).astype(jnp.float32)
    descend = (local_far[:, LOCCL - 1] + jnp.einsum('dab,dbr->dar', transfer[:, LOCCL - 1], parent))[:, None]
    for offset, amount in reversed(level_spans[:-1]):
        parent = jnp.repeat(stored(descend), 2, axis=1).astype(jnp.float32)
        descend = local_far[:, offset:offset + amount] + jnp.einsum('dnab,dnbr->dnar', transfer[:, offset:offset + amount], parent)
    leaf_down = stored(descend).astype(jnp.float32).reshape(NLEAVES, RANK, RHS)
    far_part = jnp.einsum('lkr,klp->rlp', leaf_down, basis_rows)

    point_rows = points.transpose(1, 0, 2)

    def near_block(pieces):
        picked = point_rows[pieces[1]]
        return jnp.einsum('tkqp,tkrp->rtq', blocks(pieces[0], LEAF, LEAF).astype(jnp.float32), picked)

    near_part = lax.map(near_block, (near_blocks.reshape(devices, LEAF_DEV, NEAR, LEAF * LEAF), near_list.reshape(devices, LEAF_DEV, NEAR)))
    near_part = near_part.transpose(1, 0, 2, 3).reshape(RHS, NLEAVES, LEAF)
    return (far_part + near_part).reshape(RHS, NPTS)
```

```python
import functools

import jax
import jax.numpy as jnp
from jax import lax
from jax.experimental import pallas as pl
from jax.experimental.pallas import tpu as pltpu
from jax.sharding import PartitionSpec as P

BF = jnp.bfloat16
F32 = jnp.float32
MESH = pl.DeviceIdType.MESH
TOP_OFF = (0, 32, 48, 56, 60, 62)
S_Q, S_X, S_Z, S_D, S_U, S_XH, S_TAB, S_GT, N_SEM = 0, 8, 12, 20, 28, 32, 34, 38, 40


def nt(a, b):
    return lax.dot_general(a, b, (((1,), (1,)), ((), ())), preferred_element_type=F32)


def nn(a, b):
    return jnp.dot(a, b, preferred_element_type=F32)


def half_swap(v):
    return pltpu.roll(v, 64, 1)


def iota(shape, dim):
    return lax.broadcasted_iota(jnp.int32, shape, dim)


def kernel(
    near_list_hbm, local_partner_hbm, local_count_hbm, group_partner_hbm, group_count_hbm, top_partner_hbm,
    top_count_hbm, x_hbm, basis_hbm, near_hbm, ltrans_hbm, lcouple_hbm, gtrans_hbm, gcouple_hbm, ttrans_hbm, tcouple_hbm,
    out,
    xs, bs, nb, lt, lc, gt_in, gc, tt, tc,
    ef, es, gf, ge, tf, et, sf, ts, bd, tab, bdt, xbd, pp, rl,
    qb, hr, p1, p2, p3, p4, ub, gu, gt, gs, zb, far, nearp, vht,
    near_list, local_partner, local_count, group_partner, group_count, top_partner, top_count,
    lsem, ssem, rsem,
):
    leaf = lax.axis_index("leaf")
    sub = lax.axis_index("sub")
    col, ylo = lax.div(leaf, 2), lax.rem(leaf, 2)
    z, x = lax.div(col, 4), lax.rem(col, 4)
    member = ylo * 4 + sub
    b = leaf * 4 + sub
    half = lax.div(sub, 2)

    relay = (ylo == 0) & (sub < 2)
    late = (ylo == 0) & (sub >= 2)

    def column_peer(m):
        return (col * 2 + lax.div(m, 4), lax.rem(m, 4))

    def ring_peer(step):
        n = lax.rem(b + step, 256)
        return (lax.div(n, 4), lax.rem(n, 4))

    col_peers = [column_peer(lax.rem(member + d, 8)) for d in range(8)]
    relays = [(col * 2, 0), (col * 2, 1)]
    x_peers = [((z * 4 + lax.rem(x + d, 4)) * 2 + ylo, sub) for d in range(4)]
    z_peers = [((lax.rem(z + d, 8) * 4 + x) * 2 + ylo, sub) for d in range(8)]
    sub_peers = [(leaf, lax.rem(sub + d, 4)) for d in range(4)]
    after, before = ring_peer(1), ring_peer(255)
    g_after = (lax.rem(leaf + 1, 64), sub)
    g_before = (lax.rem(leaf + 63, 64), sub)

    local = []

    def fetch(src, dst):
        cp = pltpu.make_async_copy(src, dst, lsem.at[len(local)])
        cp.start()
        local.append(cp)
        return cp

    w_x = [fetch(x_hbm.at[:, pl.ds(128 * m, 128)], xs.at[4 + m]) for m in range(8)]
    w_b = [fetch(basis_hbm, bs)]
    w_lt = [fetch(ltrans_hbm, lt)]
    w_gt = [fetch(gtrans_hbm, gt_in)]
    w_tt = [fetch(ttrans_hbm, tt)]
    w_tc = [fetch(tcouple_hbm, tc)]
    w_top = [fetch(top_partner_hbm, top_partner), fetch(top_count_hbm, top_count)]
    w_nb = [fetch(near_hbm, nb), fetch(near_list_hbm, near_list)]
    w_lc = [fetch(lcouple_hbm, lc), fetch(local_partner_hbm, local_partner), fetch(local_count_hbm, local_count)]
    w_gc = [fetch(gcouple_hbm, gc), fetch(group_partner_hbm, group_partner), fetch(group_count_hbm, group_count)]

    def ready(copies):
        for cp in copies:
            cp.wait()

    barrier = pltpu.get_barrier_semaphore()
    def greet(peers):
        for peer in peers:
            pl.semaphore_signal(barrier, inc=1, device_id=peer, device_id_type=MESH)

    greet(sub_peers[1:] + [after, before, g_after, g_before])

    @pl.when(relay)
    def _():
        greet(col_peers[1:] + x_peers[1:] + z_peers[1:])

    @pl.when(jnp.logical_not(relay))
    def _():
        greet(relays)

    def copy(src, dst, sent, got, peer):
        return pltpu.make_async_remote_copy(
            src_ref=src, dst_ref=dst, send_sem=ssem.at[sent], recv_sem=rsem.at[got],
            device_id=peer, device_id_type=MESH,
        )

    def send(src, dst, place, peer):
        cp = copy(src, dst, place, place, peer)
        cp.start()
        return cp

    lane = iota((1, 128), 1)
    left = lane < 64
    m_left = jnp.where(left, 1.0, 0.0).astype(BF)
    m_right = jnp.where(left, 0.0, 1.0).astype(BF)
    row, column = iota((128, 128), 0), iota((128, 128), 1)
    from_row = lax.div(row, 64) * 64 + 2 * lax.rem(row, 32) + lax.div(lax.rem(row, 64), 32)
    pp[...] = jnp.where(column == from_row, 1.0, 0.0).astype(BF)
    eye = jnp.where(iota((64, 64), 0) == iota((64, 64), 1), 1.0, 0.0).astype(BF)

    def unpack(load, n, dst, masked):
        if masked:
            cluster = iota((n, 128), 0)
            side = lax.rem(lax.div(cluster, 2), 2)
            if n == 31:
                side = jnp.where(cluster == 30, 0, side)
            lanes = iota((n, 128), 1)
            keep_l = (side == 0) & (lanes < 64)
            keep_r = (side == 1) & (lanes >= 64)
        for j in range(32):
            v = load(j).astype(F32)
            r = half_swap(v)
            if masked:
                zero = jnp.zeros_like(v)
                even = jnp.where(keep_l, v, jnp.where(keep_r, r, zero))
                odd = jnp.where(keep_l, r, jnp.where(keep_r, v, zero))
            else:
                even = jnp.where(left, v, r)
                odd = jnp.where(left, r, v)
            dst[pl.ds(2 * j, n, stride=64), :] = even
            dst[pl.ds(2 * j + 1, n, stride=64), :] = odd

    ready(w_x)
    ready(w_b)
    for m in range(8):
        two = bs[:, 128 * m : 128 * m + 128]
        both = jnp.concatenate([two * m_left, two * m_right], axis=0)
        bd[m] = both
        tab[16 + m] = nt(xs[4 + m], both).astype(BF)
    ready(w_lt)
    ready(w_gt)

    def upward():
        unpack(lambda j: lt[:, 128 * j : 128 * j + 128], 31, ef, True)
        es[...] = ef[...].astype(BF)
        unpack(lambda j: gt_in[:, 128 * j : 128 * j + 128], 3, gf, False)
        ge[...] = gf[...].astype(BF).reshape(3, 64, 128)
        e_root = es[30 * 64 : 31 * 64, :]
        pair_down = nn(ge[half][:, :64], ge[2]).astype(BF)
        h_root = nn(e_root[:, :64], pair_down).astype(BF)
        hr[...] = h_root
        for lo, hi, n in ((16, 24, 4), (24, 28, 2), (28, 30, 1)):
            for i in range(n):
                kids = jnp.concatenate([tab[lo + 2 * i], tab[lo + 2 * i + 1]], axis=1)
                first = 2 * (lo - 16) + 4 * i
                tab[hi + i] = nn(kids, es[first * 64 : first * 64 + 256, :]).astype(BF)
        c_root = nn(tab[30], es[28 * 64 : 30 * 64, :]).astype(BF)
        tab[31] = c_root
        q = nn(c_root[:, :64], h_root)
        qb[...] = q.reshape(2, 32, 128)
        ub[...] = nn(c_root[:, :64], e_root).astype(BF)

    def seen(l, first):
        mine = TOP_OFF[l] + lax.div(col, 2**l)
        total = jnp.zeros((64, 128), F32)
        for k in range(3):
            partner = jnp.where(k < top_count[mine], top_partner[k, mine], -1)
            target = jnp.where(left, first, first + 1)
            total = total + jnp.where(target == partner, gs[3 * l + k], 0.0)
        return total

    def prepare_top():
        unpack(lambda j: tt[:, 128 * j : 128 * j + 128], 62, tf, True)
        et[...] = tf[...].astype(BF)
        level_row, cluster_column = iota((8, 63), 0), iota((8, 63), 1)
        ancestor = level_row * 0 - 1
        for l in range(6):
            ancestor = jnp.where(level_row == l, TOP_OFF[l] + lax.div(col, 2**l), ancestor)
        pick = jnp.where(cluster_column == ancestor, 1.0, 0.0).astype(BF)
        for k in range(3):
            rows = nn(pick, tc[k])
            unpack(lambda j: rows[:, 128 * j : 128 * j + 128], 8, sf.at[pl.ds(512 * k, 512)], False)
        ts[...] = sf[...].astype(BF)
        path = None
        for l in range(6):
            for k in range(3):
                at = (8 * k + l) * 64
                gs[3 * l + k] = sf[at : at + 64, :] if l == 0 else nn(path[:, :64], ts[at : at + 64, :])
            if l < 5:
                place = pl.multiple_of((TOP_OFF[l] + lax.div(col, 2**l)) * 64, 64)
                step = et[pl.ds(place, 64), :]
                step = step + half_swap(step)
                path = step if l == 0 else nn(path[:, :64], step).astype(BF)
        level = [seen(5, 62).astype(BF)]
        for l in range(4, -1, -1):
            offset = TOP_OFF[l]
            lower_level = []
            for i, parents in enumerate(level):
                first = offset + 4 * i
                if l == 4:
                    w = et[first * 64 : (first + 2) * 64, :]
                    lower_level.append((nt(parents[:, :64], w[:, :64]) + seen(l, first)).astype(BF))
                else:
                    both = nt(parents, et[first * 64 : (first + 4) * 64, :])
                    lower_level.append((both[:, :128] + seen(l, first)).astype(BF))
                    lower_level.append((both[:, 128:] + seen(l, first + 2)).astype(BF))
            level = lower_level
        for i in range(16):
            zb[i] = level[i]

    ready(w_tt)
    ready(w_tc)
    ready(w_top)

    @pl.when(jnp.logical_not(late))
    def _():
        upward()

    @pl.when(relay)
    def _():
        prepare_top()

    pl.semaphore_wait(barrier, jnp.where(relay, 24, 9))
    leaves_own, upper_own = tab.at[pl.ds(16, 8)], tab.at[pl.ds(24, 8)]
    c_xh = [
        send(xs.at[pl.ds(8, 4)], xs.at[pl.ds(0, 4)], S_XH, after),
        send(xs.at[pl.ds(4, 4)], xs.at[pl.ds(12, 4)], S_XH + 1, before),
    ]
    c_leaves = [
        send(leaves_own, tab.at[pl.ds(0, 8)], S_TAB, after),
        send(leaves_own, tab.at[pl.ds(32, 8)], S_TAB + 1, before),
    ]

    @pl.when(late)
    def _():
        upward()

    c_q = [copy(qb.at[c], p1.at[member], S_Q + c, S_Q + member, relays[c]) for c in range(2)]
    for c in range(2):

        @pl.when(member != c)
        def _(c=c):
            c_q[c].start()

    c_u = [send(ub, gu.at[sub], S_U + d, sub_peers[d]) for d in range(1, 4)]
    c_upper = [
        send(upper_own, tab.at[pl.ds(8, 8)], S_TAB + 2, after),
        send(upper_own, tab.at[pl.ds(40, 8)], S_TAB + 3, before),
    ]
    gu[sub] = ub[...]

    def widen(src, dst, lo, n):
        def step(i, carry):
            for h in range(8):
                at = lo + 8 * i + h
                v = src[at]
                r = half_swap(v)
                dst[2 * at] = jnp.concatenate([v * m_left, r * m_right], axis=0)
                dst[2 * at + 1] = jnp.concatenate([r * m_left, v * m_right], axis=0)
            return carry

        lax.fori_loop(0, n, step, 0)

    def spread(load, n, ref):
        for j in range(32):
            ref[pl.ds(j, n, stride=32), :] = load(j).astype(F32)
        even, odd = [], []
        for k in range(0, n, 2):
            one, two = ref[32 * k : 32 * k + 32, :], ref[32 * k + 32 : 32 * k + 64, :]
            even.append(jnp.where(left, one, half_swap(two)))
            odd.append(jnp.where(left, half_swap(one), two))
        rows = [jnp.concatenate(even, axis=1), jnp.concatenate(odd, axis=1)]
        return jnp.concatenate(rows, axis=0).astype(BF)

    def coupled(table, ids, w):
        pairs = [table[ids[k], 0:64, :] + table[ids[k + 1], 64:128, :] for k in range(0, len(ids), 2)]
        return nt(jnp.concatenate(pairs, axis=1), w)

    def in_order(one, two):
        return nn(jnp.concatenate([one, two], axis=1).astype(BF), pp[...])

    ready(w_nb)
    widen(xs, xbd, 4, 1)
    for cp in c_xh:
        cp.wait_recv()
    for at in (0, 12):
        for h in range(4):
            v = xs[at + h]
            r = half_swap(v)
            xbd[2 * (at + h)] = jnp.concatenate([v * m_left, r * m_right], axis=0)
            xbd[2 * (at + h) + 1] = jnp.concatenate([r * m_left, v * m_right], axis=0)

    def near_step(i, carry):
        weights = []
        for h in range(8):
            t = 8 * i + h
            weights.append(spread(lambda j: nb[t, :, 128 * j : 128 * j + 128], 8, rl.at[h]))
        parts = []
        for h in range(8):
            ids = [jnp.clip(near_list[k, 8 * i + h] - (b * 16 - 8), 0, 31) for k in range(8)]
            parts.append(coupled(xbd, ids, weights[h]))
        for h in range(4):
            nearp[4 * i + h] = in_order(parts[2 * h], parts[2 * h + 1])
        return carry

    lax.fori_loop(0, 2, near_step, 0)

    c_z = [copy(p2.at[z], p2.at[z], S_Z + d, S_Z + d, z_peers[d]) for d in range(1, 8)]

    @pl.when(relay)
    def _():
        p1[member] = qb[member]
        for m in range(8):

            @pl.when(member != m)
            def _(m=m):
                copy(qb.at[0], p1.at[m], S_Q, S_Q + m, relays[0]).wait_recv()

        total = p1[0]
        for m in range(1, 8):
            total = total + p1[m]
        p2[z] = jnp.where(left, total[:16], total[16:]).astype(BF)
        for cp in c_z:
            cp.start()

    ready(w_lc)

    def far_step(i, carry):
        weights = []
        for h in range(8):
            c = jnp.minimum(8 * i + h, 30)
            weights.append(spread(lambda j: lc[c, :, 128 * j : 128 * j + 128], 8, rl.at[h]))
        parts = []
        for h in range(8):
            c = jnp.minimum(8 * i + h, 30)
            count = jnp.where(8 * i + h < 31, local_count[c], 0)
            ids = []
            for k in range(8):
                e = jnp.clip(local_partner[k, c] - (b - 1) * 31, 0, 92)
                e = e + jnp.where(e >= 31, 1, 0) + jnp.where(e >= 62, 1, 0)
                ids.append(jnp.where(k < count, e, 63))
            parts.append(coupled(bdt, ids, weights[h]))
        for h in range(4):
            far[4 * i + h] = in_order(parts[2 * h], parts[2 * h + 1])
        return carry

    widen(tab, bdt, 16, 2)
    for cp in c_leaves:
        cp.wait_recv()
    widen(tab, bdt, 0, 1)
    widen(tab, bdt, 32, 1)
    lax.fori_loop(0, 2, far_step, 0)

    c_x = [copy(p2, p3.at[x], S_X + d, S_X + d, x_peers[d]) for d in range(1, 4)]

    @pl.when(relay)
    def _():
        for cp in c_z:
            cp.wait_recv()
        for cp in c_x:
            cp.start()
        p3[x] = p2[...]

    for cp in c_u:
        cp.wait_recv()
    g0 = (gu[0].astype(F32) + gu[1].astype(F32)).astype(BF)
    g1 = (gu[2].astype(F32) + gu[3].astype(F32)).astype(BF)
    g2 = (nn(g0[:, :64], ge[0]) + nn(g1[:, :64], ge[1])).astype(BF)
    gt[3] = g0 + half_swap(g0)
    gt[4] = g1 + half_swap(g1)
    gt[5] = g2
    gt[9] = jnp.zeros((64, 128), BF)
    c_gt = [
        send(gt.at[pl.ds(3, 3)], gt.at[pl.ds(0, 3)], S_GT, g_after),
        send(gt.at[pl.ds(3, 3)], gt.at[pl.ds(6, 3)], S_GT + 1, g_before),
    ]

    for cp in c_upper:
        cp.wait_recv()
    widen(tab, bdt, 8, 1)
    widen(tab, bdt, 40, 1)
    lax.fori_loop(2, 4, far_step, 0)

    c_d = [copy(p4.at[sub], p4.at[sub], S_D + 1 + d, S_D + sub, col_peers[d]) for d in range(1, 8)]

    @pl.when(relay)
    def _():
        for cp in c_x:
            cp.wait_recv()
        have = []
        for i in range(16):
            one, two = p3[2 * (i % 2), i // 2], p3[2 * (i % 2) + 1, i // 2]
            up = one * m_left + half_swap(two) * m_right
            down = half_swap(one) * m_left + two * m_right
            have.append(jnp.concatenate([up, down], axis=0))
        weigh = jnp.concatenate([zb[i] for i in range(16)], axis=1)
        d = nt(jnp.concatenate(have, axis=1), weigh)
        p4[sub] = jnp.concatenate([d, d], axis=1).astype(BF)
        for cp in c_d:
            cp.start()

    ready(w_gc)
    for cp in c_gt:
        cp.wait_recv()
    found = []
    for c in range(3):
        w = spread(lambda j: gc[c, :, 128 * j : 128 * j + 128], 4, rl.at[c])
        entries = []
        for k in range(4):
            e = jnp.clip(group_partner[c, k] - (leaf - 1) * 3, 0, 8)
            entries.append(gt[jnp.where(k < group_count[c], e, 9)])
        pairs = [entries[k] * m_left + entries[k + 1] * m_right for k in (0, 2)]
        found.append(nt(jnp.concatenate(pairs, axis=1), w))
    f01 = in_order(found[0], found[1])
    f2 = in_order(found[2], found[2])
    f_half = jnp.where(half == 0, f01, half_swap(f01))[:, :64]
    d_half = f_half + nt(f2[:, :64].astype(BF), ge[half][:, :64])

    e_root = es[30 * 64 : 31 * 64, :]
    d_root = far[15][:, :64] + nt(d_half.astype(BF), e_root[:, :64])
    state = jnp.concatenate([d_root, nt(eye, hr[...][:, :64])], axis=0).astype(BF)
    nothing = jnp.zeros((64, 128), F32)

    def with_far(v, i):
        return (v + jnp.concatenate([far[i], nothing], axis=0)).astype(BF)

    states = [with_far(nt(state, es[28 * 64 : 30 * 64, :64]), 14)]
    for first, pair in ((24, 12), (16, 8), (0, 0)):
        lower_level = []
        for i, parents in enumerate(states):
            at = (first + 4 * i) * 64
            both = nt(parents, es[at : at + 256, :])
            lower_level.append(with_far(both[:, :128], pair + 2 * i))
            lower_level.append(with_far(both[:, 128:], pair + 2 * i + 1))
        states = lower_level
    for m in range(8):
        r = nn(states[m], bd[m])
        nearp[m] = nearp[m] + r[:64]
        vht[m] = r[64:].astype(BF)

    for c in range(2):

        @pl.when(member != c)
        def _(c=c):
            copy(p4.at[c], p4.at[c], S_D, S_D + c, relays[c]).wait_recv()

    d_col = p4[...].reshape(64, 128)[:, :64]
    for m in range(8):
        out[:, 128 * m : 128 * m + 128] = nearp[m] + nn(d_col, vht[m])

    for cp in c_u + c_xh + c_leaves + c_upper + c_gt:
        cp.wait_send()
    for c in range(2):

        @pl.when(member != c)
        def _(c=c):
            c_q[c].wait_send()

    @pl.when(relay)
    def _():
        for cp in c_z + c_x + c_d:
            cp.wait_send()


def body(
    right_sides, leaf_basis, near_blocks, near_list, local_transfer, local_couple, local_partner, local_count,
    group_transfer, group_couple, group_partner, group_count, top_transfer, top_couple, top_partner, top_count,
):
    hbm = pl.BlockSpec(memory_space=pltpu.HBM)
    vm = pltpu.VMEM
    return pl.pallas_call(
        kernel,
        out_shape=jax.ShapeDtypeStruct((64, 1024), F32),
        in_specs=[hbm] * 16,
        out_specs=pl.BlockSpec(memory_space=pltpu.VMEM),
        scratch_shapes=[
            vm((16, 64, 128), BF),
            vm((64, 1024), BF),
            vm((16, 8, 4096), BF),
            vm((31, 4096), BF),
            vm((31, 8, 4096), BF),
            vm((3, 4096), BF),
            vm((3, 4, 4096), BF),
            vm((62, 4096), BF),
            vm((3, 63, 4096), BF),
            vm((31 * 64, 128), F32),
            vm((31 * 64, 128), BF),
            vm((3 * 64, 128), F32),
            vm((3, 64, 128), BF),
            vm((62 * 64, 128), F32),
            vm((62 * 64, 128), BF),
            vm((24 * 64, 128), F32),
            vm((24 * 64, 128), BF),
            vm((8, 128, 128), BF),
            vm((48, 64, 128), BF),
            vm((96, 128, 128), BF),
            vm((32, 128, 128), BF),
            vm((128, 128), BF),
            vm((8, 256, 128), F32),
            vm((2, 32, 128), F32),
            vm((64, 128), BF),
            vm((8, 32, 128), F32),
            vm((8, 16, 128), BF),
            vm((4, 8, 16, 128), BF),
            vm((2, 32, 128), BF),
            vm((64, 128), BF),
            vm((4, 64, 128), BF),
            vm((10, 64, 128), BF),
            vm((18, 64, 128), F32),
            vm((16, 64, 128), BF),
            vm((16, 64, 128), F32),
            vm((8, 64, 128), F32),
            vm((8, 64, 128), BF),
            pltpu.SMEM((8, 16), jnp.int32),
            pltpu.SMEM((8, 31), jnp.int32),
            pltpu.SMEM((31,), jnp.int32),
            pltpu.SMEM((3, 4), jnp.int32),
            pltpu.SMEM((3,), jnp.int32),
            pltpu.SMEM((3, 63), jnp.int32),
            pltpu.SMEM((63,), jnp.int32),
            pltpu.SemaphoreType.DMA((24,)),
            pltpu.SemaphoreType.DMA((N_SEM,)),
            pltpu.SemaphoreType.DMA((N_SEM,)),
        ],
        compiler_params=pltpu.CompilerParams(
            collective_id=0, has_side_effects=True, vmem_limit_bytes=60 * 1024 * 1024
        ),
        name="h2",
    )(
        near_list.T, local_partner.T, local_count, group_partner, group_count, top_partner.T, top_count,
        right_sides, leaf_basis, near_blocks, local_transfer, local_couple, group_transfer, group_couple,
        top_transfer, jnp.transpose(top_couple, (1, 0, 2)),
    )


def solution(mesh):
    both = ("leaf", "sub")
    placed = (
        P(None, both), P(None, both), P(both, None, None), P(both, None), P(both, None), P(both, None, None),
        P(both, None), P(both), P("leaf", None), P("leaf", None, None), P("leaf", None), P("leaf"),
        P(), P(), P(), P(),
    )
    return jax.shard_map(body, mesh=mesh, in_specs=placed, out_specs=P(None, both), check_vma=False)
```

```python
import functools

import jax
import jax.numpy as jnp
from jax import lax
from jax.experimental import pallas as pl
from jax.experimental.pallas import tpu as pltpu
from jax.sharding import PartitionSpec as P

BF = jnp.bfloat16
F32 = jnp.float32
MESH = pl.DeviceIdType.MESH
TOP_OFF = (0, 32, 48, 56, 60, 62)
S_Q, S_C, S_D, S_U, S_XH, S_TAB, S_GT, N_SEM = 0, 8, 12, 20, 24, 26, 30, 32


def nt(a, b):
    return lax.dot_general(a, b, (((1,), (1,)), ((), ())), preferred_element_type=F32)


def nn(a, b):
    return jnp.dot(a, b, preferred_element_type=F32)


def half_swap(v):
    return pltpu.roll(v, 64, 1)


def iota(shape, dim):
    return lax.broadcasted_iota(jnp.int32, shape, dim)


def kernel(
    near_list_hbm, local_partner_hbm, local_count_hbm, group_partner_hbm, group_count_hbm, top_partner_hbm,
    top_count_hbm, x_hbm, basis_hbm, near_hbm, ltrans_hbm, lcouple_hbm, gtrans_hbm, gcouple_hbm, ttrans_hbm, tcouple_hbm,
    out,
    xs, bs, nb, lt, lc, gt_in, gc, tt, tc,
    ef, es, gf, ge, tf, et, sf, ts, bd, tab, bdt, xbd, pp, rl,
    qb, hr, p1, p3, p4, ub, gu, gt, gs, zb, far, nearp, vht,
    near_list, local_partner, local_count, group_partner, group_count, top_partner, top_count,
    lsem, ssem, rsem, csem,
):
    leaf = lax.axis_index("leaf")
    sub = lax.axis_index("sub")
    col, ylo = lax.div(leaf, 2), lax.rem(leaf, 2)
    z, x = lax.div(col, 4), lax.rem(col, 4)
    member = ylo * 4 + sub
    b = leaf * 4 + sub
    half = lax.div(sub, 2)

    source = member == z

    def column_peer(m):
        return (col * 2 + lax.div(m, 4), lax.rem(m, 4))

    def ring_peer(step):
        n = lax.rem(b + step, 256)
        return (lax.div(n, 4), lax.rem(n, 4))

    col_peers = [column_peer(lax.rem(member + d, 8)) for d in range(8)]
    plane_peers = [(lax.rem(col + d, 32) * 2 + ylo, sub) for d in range(32)]
    plane_sources = [((member * 4 + i) * 2 + ylo, sub) for i in range(4)]
    sub_peers = [(leaf, lax.rem(sub + d, 4)) for d in range(4)]
    after, before = ring_peer(1), ring_peer(255)
    g_after = (lax.rem(leaf + 1, 64), sub)
    g_before = (lax.rem(leaf + 63, 64), sub)

    local = []

    def fetch(src, dst):
        cp = pltpu.make_async_copy(src, dst, lsem.at[len(local)])
        cp.start()
        local.append(cp)
        return cp

    w_x = [fetch(x_hbm.at[:, pl.ds(128 * m, 128)], xs.at[4 + m]) for m in range(8)]
    w_b = [fetch(basis_hbm, bs)]
    w_lt = [fetch(ltrans_hbm, lt)]
    w_gt = [fetch(gtrans_hbm, gt_in)]
    w_tt = [fetch(ttrans_hbm, tt)]
    w_tc = [fetch(tcouple_hbm, tc)]
    w_top = [fetch(top_partner_hbm, top_partner), fetch(top_count_hbm, top_count)]
    w_nb = [fetch(near_hbm, nb), fetch(near_list_hbm, near_list)]
    w_lc = [fetch(lcouple_hbm, lc), fetch(local_partner_hbm, local_partner), fetch(local_count_hbm, local_count)]
    w_gc = [fetch(gcouple_hbm, gc), fetch(group_partner_hbm, group_partner), fetch(group_count_hbm, group_count)]

    def ready(copies):
        for cp in copies:
            cp.wait()

    barrier = pltpu.get_barrier_semaphore()
    def greet(peers):
        for peer in peers:
            pl.semaphore_signal(barrier, inc=1, device_id=peer, device_id_type=MESH)

    greet(col_peers[1:] + [after, before, g_after, g_before])

    @pl.when(source)
    def _():
        greet(plane_peers[1:])

    @pl.when(jnp.logical_not(source))
    def _():
        greet(plane_sources)

    def copy(src, dst, sent, got, peer):
        return pltpu.make_async_remote_copy(
            src_ref=src, dst_ref=dst, send_sem=ssem.at[sent], recv_sem=rsem.at[got],
            device_id=peer, device_id_type=MESH,
        )

    def send(src, dst, place, peer):
        cp = copy(src, dst, place, place, peer)
        cp.start()
        return cp

    lane = iota((1, 128), 1)
    left = lane < 64
    m_left = jnp.where(left, 1.0, 0.0).astype(BF)
    m_right = jnp.where(left, 0.0, 1.0).astype(BF)
    row, column = iota((128, 128), 0), iota((128, 128), 1)
    from_row = lax.div(row, 64) * 64 + 2 * lax.rem(row, 32) + lax.div(lax.rem(row, 64), 32)
    pp[...] = jnp.where(column == from_row, 1.0, 0.0).astype(BF)
    eye = jnp.where(iota((64, 64), 0) == iota((64, 64), 1), 1.0, 0.0).astype(BF)

    def unpack(load, n, dst, masked):
        if masked:
            cluster = iota((n, 128), 0)
            side = lax.rem(lax.div(cluster, 2), 2)
            if n == 31:
                side = jnp.where(cluster == 30, 0, side)
            lanes = iota((n, 128), 1)
            keep_l = (side == 0) & (lanes < 64)
            keep_r = (side == 1) & (lanes >= 64)
        for j in range(32):
            v = load(j).astype(F32)
            r = half_swap(v)
            if masked:
                zero = jnp.zeros_like(v)
                even = jnp.where(keep_l, v, jnp.where(keep_r, r, zero))
                odd = jnp.where(keep_l, r, jnp.where(keep_r, v, zero))
            else:
                even = jnp.where(left, v, r)
                odd = jnp.where(left, r, v)
            dst[pl.ds(2 * j, n, stride=64), :] = even
            dst[pl.ds(2 * j + 1, n, stride=64), :] = odd

    ready(w_x)
    ready(w_b)
    for m in range(8):
        two = bs[:, 128 * m : 128 * m + 128]
        both = jnp.concatenate([two * m_left, two * m_right], axis=0)
        bd[m] = both
        tab[16 + m] = nt(xs[4 + m], both).astype(BF)
    ready(w_lt)
    ready(w_gt)

    def upward():
        unpack(lambda j: lt[:, 128 * j : 128 * j + 128], 31, ef, True)
        es[...] = ef[...].astype(BF)
        unpack(lambda j: gt_in[:, 128 * j : 128 * j + 128], 3, gf, False)
        ge[...] = gf[...].astype(BF).reshape(3, 64, 128)
        e_root = es[30 * 64 : 31 * 64, :]
        pair_down = nn(ge[half][:, :64], ge[2]).astype(BF)
        h_root = nn(e_root[:, :64], pair_down).astype(BF)
        hr[...] = h_root
        for lo, hi, n in ((16, 24, 4), (24, 28, 2), (28, 30, 1)):
            for i in range(n):
                kids = jnp.concatenate([tab[lo + 2 * i], tab[lo + 2 * i + 1]], axis=1)
                first = 2 * (lo - 16) + 4 * i
                tab[hi + i] = nn(kids, es[first * 64 : first * 64 + 256, :]).astype(BF)
        c_root = nn(tab[30], es[28 * 64 : 30 * 64, :]).astype(BF)
        tab[31] = c_root
        q = nn(c_root[:, :64], h_root)
        qb[...] = jnp.where(left, q[:32], q[32:]).astype(BF)
        ub[...] = nn(c_root[:, :64], e_root).astype(BF)

    def seen(l, first):
        mine = TOP_OFF[l] + lax.div(col, 2**l)
        total = jnp.zeros((64, 128), F32)
        for k in range(3):
            partner = jnp.where(k < top_count[mine], top_partner[k, mine], -1)
            target = jnp.where(left, first, first + 1)
            total = total + jnp.where(target == partner, gs[3 * l + k], 0.0)
        return total

    def prepare_top():
        wanted = [60 + lax.div(member, 4), 56 + lax.div(member, 2), 48 + member]
        wanted += [32 + 2 * member + i for i in range(2)] + [4 * member + i for i in range(4)]
        wanted += [TOP_OFF[l] + lax.div(col, 2**l) for l in range(5)]

        def pick(rows, n, clusters):
            at = iota((rows, n), 0)
            cluster = at * 0 - 1
            for i, c in enumerate(clusters):
                cluster = jnp.where(at == i, c, cluster)
            return jnp.where(iota((rows, n), 1) == cluster, 1.0, 0.0).astype(BF)

        rows = nn(pick(16, 62, wanted), tt[...])
        unpack(lambda j: rows[:, 128 * j : 128 * j + 128], 16, tf, False)
        et[...] = tf[...].astype(BF)
        ancestors = pick(8, 63, [TOP_OFF[l] + lax.div(col, 2**l) for l in range(6)])
        for k in range(3):
            rows = nn(ancestors, tc[k])
            unpack(lambda j: rows[:, 128 * j : 128 * j + 128], 8, sf.at[pl.ds(512 * k, 512)], False)
        ts[...] = sf[...].astype(BF)
        path = None
        for l in range(6):
            for k in range(3):
                at = (8 * k + l) * 64
                gs[3 * l + k] = sf[at : at + 64, :] if l == 0 else nn(path[:, :64], ts[at : at + 64, :])
            if l < 5:
                step = et[(9 + l) * 64 : (10 + l) * 64, :]
                path = step if l == 0 else nn(path[:, :64], step).astype(BF)
        v = seen(5, 62)
        for i, l in enumerate((4, 3, 2)):
            v = nt(v[:, :64].astype(BF), et[64 * i : 64 * i + 64, :64]) + seen(l, wanted[i])[:, :64]
        v = nt(v.astype(BF), et[3 * 64 : 5 * 64, :64]) + seen(1, wanted[3])
        w = jnp.concatenate([et[5 * 64 : 7 * 64, :] * m_left, et[7 * 64 : 9 * 64, :] * m_right], axis=0)
        v = nt(v.astype(BF), w)
        v = v + jnp.concatenate([seen(0, wanted[5]), seen(0, wanted[7])], axis=1)
        zb[...] = v.astype(BF)

    upward()
    pl.semaphore_wait(barrier, jnp.where(source, 42, 15))

    c_q = copy(qb, p1.at[member], S_Q, S_Q + member, column_peer(z))

    @pl.when(jnp.logical_not(source))
    def _():
        c_q.start()

    c_u = [send(ub, gu.at[sub], S_U + d, sub_peers[d]) for d in range(1, 4)]
    gu[sub] = ub[...]
    c_xh = [
        send(xs.at[pl.ds(8, 4)], xs.at[pl.ds(0, 4)], S_XH, after),
        send(xs.at[pl.ds(4, 4)], xs.at[pl.ds(12, 4)], S_XH + 1, before),
    ]
    leaves_own, upper_own = tab.at[pl.ds(16, 8)], tab.at[pl.ds(24, 8)]
    c_leaves = [
        send(leaves_own, tab.at[pl.ds(0, 8)], S_TAB, after),
        send(leaves_own, tab.at[pl.ds(32, 8)], S_TAB + 1, before),
    ]
    c_upper = [
        send(upper_own, tab.at[pl.ds(8, 8)], S_TAB + 2, after),
        send(upper_own, tab.at[pl.ds(40, 8)], S_TAB + 3, before),
    ]

    ready(w_tt)
    ready(w_tc)
    ready(w_top)
    prepare_top()

    c_c = [
        pltpu.make_async_remote_copy(
            src_ref=p3.at[x], dst_ref=p3.at[x], send_sem=csem.at[d], recv_sem=rsem.at[S_C + x],
            device_id=plane_peers[d], device_id_type=MESH,
        )
        for d in range(1, 32)
    ]

    @pl.when(source)
    def _():
        p1[member] = qb[...]
        for m in range(8):

            @pl.when(member != m)
            def _(m=m):
                copy(qb, p1.at[m], S_Q, S_Q + m, col_peers[1]).wait_recv()

        total = p1[0].astype(F32)
        for m in range(1, 8):
            total = total + p1[m].astype(F32)
        p3[x] = total.astype(BF)
        for cp in c_c:
            cp.start()

    def widen(src, dst, lo, n):
        def step(i, carry):
            for h in range(8):
                at = lo + 8 * i + h
                v = src[at]
                r = half_swap(v)
                dst[2 * at] = jnp.concatenate([v * m_left, r * m_right], axis=0)
                dst[2 * at + 1] = jnp.concatenate([r * m_left, v * m_right], axis=0)
            return carry

        lax.fori_loop(0, n, step, 0)

    def spread(load, n, ref):
        for j in range(32):
            ref[pl.ds(j, n, stride=32), :] = load(j).astype(F32)
        even, odd = [], []
        for k in range(0, n, 2):
            one, two = ref[32 * k : 32 * k + 32, :], ref[32 * k + 32 : 32 * k + 64, :]
            even.append(jnp.where(left, one, half_swap(two)))
            odd.append(jnp.where(left, half_swap(one), two))
        rows = [jnp.concatenate(even, axis=1), jnp.concatenate(odd, axis=1)]
        return jnp.concatenate(rows, axis=0).astype(BF)

    def coupled(table, ids, w):
        pairs = [table[ids[k], 0:64, :] + table[ids[k + 1], 64:128, :] for k in range(0, len(ids), 2)]
        return nt(jnp.concatenate(pairs, axis=1), w)

    def in_order(one, two):
        return nn(jnp.concatenate([one, two], axis=1).astype(BF), pp[...])

    ready(w_nb)
    widen(xs, xbd, 4, 1)
    for cp in c_xh:
        cp.wait_recv()
    for at in (0, 12):
        for h in range(4):
            v = xs[at + h]
            r = half_swap(v)
            xbd[2 * (at + h)] = jnp.concatenate([v * m_left, r * m_right], axis=0)
            xbd[2 * (at + h) + 1] = jnp.concatenate([r * m_left, v * m_right], axis=0)

    def near_step(i, carry):
        weights = []
        for h in range(8):
            t = 8 * i + h
            weights.append(spread(lambda j: nb[t, :, 128 * j : 128 * j + 128], 8, rl.at[h]))
        parts = []
        for h in range(8):
            ids = [jnp.clip(near_list[k, 8 * i + h] - (b * 16 - 8), 0, 31) for k in range(8)]
            parts.append(coupled(xbd, ids, weights[h]))
        for h in range(4):
            nearp[4 * i + h] = in_order(parts[2 * h], parts[2 * h + 1])
        return carry

    lax.fori_loop(0, 2, near_step, 0)

    c_d = [copy(p4.at[member], p4.at[member], S_D + d, S_D + d, col_peers[d]) for d in range(1, 8)]
    for i in range(4):

        @pl.when(jnp.logical_not(source & (x == i)))
        def _(i=i):
            copy(p3.at[i], p3.at[i], S_C, S_C + i, col_peers[1]).wait_recv()

    have = []
    for i in (0, 2):
        up = p3[i] * m_left + half_swap(p3[i + 1]) * m_right
        down = half_swap(p3[i]) * m_left + p3[i + 1] * m_right
        have.append(jnp.concatenate([up, down], axis=0))
    d = nt(jnp.concatenate(have, axis=1), zb[...])
    p4[member] = jnp.concatenate([d[:32], d[32:]], axis=1).astype(BF)
    for cp in c_d:
        cp.start()

    ready(w_lc)

    def far_step(i, carry):
        weights = []
        for h in range(8):
            c = jnp.minimum(8 * i + h, 30)
            weights.append(spread(lambda j: lc[c, :, 128 * j : 128 * j + 128], 8, rl.at[h]))
        parts = []
        for h in range(8):
            c = jnp.minimum(8 * i + h, 30)
            count = jnp.where(8 * i + h < 31, local_count[c], 0)
            ids = []
            for k in range(8):
                e = jnp.clip(local_partner[k, c] - (b - 1) * 31, 0, 92)
                e = e + jnp.where(e >= 31, 1, 0) + jnp.where(e >= 62, 1, 0)
                ids.append(jnp.where(k < count, e, 63))
            parts.append(coupled(bdt, ids, weights[h]))
        for h in range(4):
            far[4 * i + h] = in_order(parts[2 * h], parts[2 * h + 1])
        return carry

    widen(tab, bdt, 16, 2)
    for cp in c_leaves:
        cp.wait_recv()
    widen(tab, bdt, 0, 1)
    widen(tab, bdt, 32, 1)
    lax.fori_loop(0, 2, far_step, 0)

    for cp in c_u:
        cp.wait_recv()
    g0 = (gu[0].astype(F32) + gu[1].astype(F32)).astype(BF)
    g1 = (gu[2].astype(F32) + gu[3].astype(F32)).astype(BF)
    g2 = (nn(g0[:, :64], ge[0]) + nn(g1[:, :64], ge[1])).astype(BF)
    gt[3] = g0 + half_swap(g0)
    gt[4] = g1 + half_swap(g1)
    gt[5] = g2
    gt[9] = jnp.zeros((64, 128), BF)
    c_gt = [
        send(gt.at[pl.ds(3, 3)], gt.at[pl.ds(0, 3)], S_GT, g_after),
        send(gt.at[pl.ds(3, 3)], gt.at[pl.ds(6, 3)], S_GT + 1, g_before),
    ]

    for cp in c_upper:
        cp.wait_recv()
    widen(tab, bdt, 8, 1)
    widen(tab, bdt, 40, 1)
    lax.fori_loop(2, 4, far_step, 0)

    ready(w_gc)
    for cp in c_gt:
        cp.wait_recv()
    found = []
    for c in range(3):
        w = spread(lambda j: gc[c, :, 128 * j : 128 * j + 128], 4, rl.at[c])
        entries = []
        for k in range(4):
            e = jnp.clip(group_partner[c, k] - (leaf - 1) * 3, 0, 8)
            entries.append(gt[jnp.where(k < group_count[c], e, 9)])
        pairs = [entries[k] * m_left + entries[k + 1] * m_right for k in (0, 2)]
        found.append(nt(jnp.concatenate(pairs, axis=1), w))
    f01 = in_order(found[0], found[1])
    f2 = in_order(found[2], found[2])
    f_half = jnp.where(half == 0, f01, half_swap(f01))[:, :64]
    d_half = f_half + nt(f2[:, :64].astype(BF), ge[half][:, :64])

    e_root = es[30 * 64 : 31 * 64, :]
    d_root = far[15][:, :64] + nt(d_half.astype(BF), e_root[:, :64])
    state = jnp.concatenate([d_root, nt(eye, hr[...][:, :64])], axis=0).astype(BF)
    nothing = jnp.zeros((64, 128), F32)

    def with_far(v, i):
        return (v + jnp.concatenate([far[i], nothing], axis=0)).astype(BF)

    states = [with_far(nt(state, es[28 * 64 : 30 * 64, :64]), 14)]
    for first, pair in ((24, 12), (16, 8), (0, 0)):
        lower_level = []
        for i, parents in enumerate(states):
            at = (first + 4 * i) * 64
            both = nt(parents, es[at : at + 256, :])
            lower_level.append(with_far(both[:, :128], pair + 2 * i))
            lower_level.append(with_far(both[:, 128:], pair + 2 * i + 1))
        states = lower_level
    for m in range(8):
        r = nn(states[m], bd[m])
        nearp[m] = nearp[m] + r[:64]
        vht[m] = r[64:].astype(BF)

    for cp in c_d:
        cp.wait_recv()
    total = p4[0].astype(F32)
    for m in range(1, 8):
        total = total + p4[m].astype(F32)
    d_col = jnp.concatenate([total[:, :64], total[:, 64:]], axis=0).astype(BF)
    for m in range(8):
        out[:, 128 * m : 128 * m + 128] = nearp[m] + nn(d_col, vht[m])

    for cp in c_u + c_xh + c_leaves + c_upper + c_gt + c_d:
        cp.wait_send()

    @pl.when(source)
    def _():
        for cp in c_c:
            cp.wait_send()

    @pl.when(jnp.logical_not(source))
    def _():
        c_q.wait_send()


def body(
    right_sides, leaf_basis, near_blocks, near_list, local_transfer, local_couple, local_partner, local_count,
    group_transfer, group_couple, group_partner, group_count, top_transfer, top_couple, top_partner, top_count,
):
    hbm = pl.BlockSpec(memory_space=pltpu.HBM)
    vm = pltpu.VMEM
    return pl.pallas_call(
        kernel,
        out_shape=jax.ShapeDtypeStruct((64, 1024), F32),
        in_specs=[hbm] * 16,
        out_specs=pl.BlockSpec(memory_space=pltpu.VMEM),
        scratch_shapes=[
            vm((16, 64, 128), BF),
            vm((64, 1024), BF),
            vm((16, 8, 4096), BF),
            vm((31, 4096), BF),
            vm((31, 8, 4096), BF),
            vm((3, 4096), BF),
            vm((3, 4, 4096), BF),
            vm((62, 4096), BF),
            vm((3, 63, 4096), BF),
            vm((31 * 64, 128), F32),
            vm((31 * 64, 128), BF),
            vm((3 * 64, 128), F32),
            vm((3, 64, 128), BF),
            vm((16 * 64, 128), F32),
            vm((16 * 64, 128), BF),
            vm((24 * 64, 128), F32),
            vm((24 * 64, 128), BF),
            vm((8, 128, 128), BF),
            vm((48, 64, 128), BF),
            vm((96, 128, 128), BF),
            vm((32, 128, 128), BF),
            vm((128, 128), BF),
            vm((8, 256, 128), F32),
            vm((32, 128), BF),
            vm((64, 128), BF),
            vm((8, 32, 128), BF),
            vm((4, 32, 128), BF),
            vm((8, 32, 128), BF),
            vm((64, 128), BF),
            vm((4, 64, 128), BF),
            vm((10, 64, 128), BF),
            vm((18, 64, 128), F32),
            vm((64, 256), BF),
            vm((16, 64, 128), F32),
            vm((8, 64, 128), F32),
            vm((8, 64, 128), BF),
            pltpu.SMEM((8, 16), jnp.int32),
            pltpu.SMEM((8, 31), jnp.int32),
            pltpu.SMEM((31,), jnp.int32),
            pltpu.SMEM((3, 4), jnp.int32),
            pltpu.SMEM((3,), jnp.int32),
            pltpu.SMEM((3, 63), jnp.int32),
            pltpu.SMEM((63,), jnp.int32),
            pltpu.SemaphoreType.DMA((24,)),
            pltpu.SemaphoreType.DMA((N_SEM,)),
            pltpu.SemaphoreType.DMA((N_SEM,)),
            pltpu.SemaphoreType.DMA((32,)),
        ],
        compiler_params=pltpu.CompilerParams(
            collective_id=0, has_side_effects=True, vmem_limit_bytes=60 * 1024 * 1024
        ),
        name="h2",
    )(
        near_list.T, local_partner.T, local_count, group_partner, group_count, top_partner.T, top_count,
        right_sides, leaf_basis, near_blocks, local_transfer, local_couple, group_transfer, group_couple,
        top_transfer, jnp.transpose(top_couple, (1, 0, 2)),
    )


def solution(mesh):
    both = ("leaf", "sub")
    placed = (
        P(None, both), P(None, both), P(both, None, None), P(both, None), P(both, None), P(both, None, None),
        P(both, None), P(both), P("leaf", None), P("leaf", None, None), P("leaf", None), P("leaf"),
        P(), P(), P(), P(),
    )
    return jax.shard_map(body, mesh=mesh, in_specs=placed, out_specs=P(None, both), check_vma=False)
```

```python
import functools

import jax
import jax.numpy as jnp
from jax import lax
from jax.experimental import pallas as pl
from jax.experimental.pallas import tpu as pltpu
from jax.sharding import PartitionSpec as P

BF = jnp.bfloat16
F32 = jnp.float32
MESH = pl.DeviceIdType.MESH
TOP_OFF = (0, 32, 48, 56, 60, 62)
S_Q, S_C, S_D, S_U, S_GT, S_B, S_F, N_SEM = 0, 8, 12, 20, 24, 26, 38, 41
HALO, LEAVES, UPPER = (0, 2, 8, 4, 0, 12, 16), (1, 4, 16, 16, 0, 32, 48), (2, 4, 24, 24, 8, 40, 52)


def nt(a, b):
    return lax.dot_general(a, b, (((1,), (1,)), ((), ())), preferred_element_type=F32)


def nn(a, b):
    return jnp.dot(a, b, preferred_element_type=F32)


def half_swap(v):
    return pltpu.roll(v, 64, 1)


def iota(shape, dim):
    return lax.broadcasted_iota(jnp.int32, shape, dim)


def kernel(
    near_list_hbm, local_partner_hbm, local_count_hbm, group_partner_hbm, group_count_hbm, top_partner_hbm,
    top_count_hbm, x_hbm, basis_hbm, near_hbm, ltrans_hbm, lcouple_hbm, gtrans_hbm, gcouple_hbm, ttrans_hbm, tcouple_hbm,
    out,
    xs, bs, nb, lt, lc, gt_in, gc, tt, tc,
    ef, es, gf, ge, tf, et, sf, ts, bd, tab, bdt, xbd, pp, rl,
    qb, hr, p1, p3, p4, ub, gu, gt, gs, zb, far, nearp, vht,
    near_list, local_partner, local_count, group_partner, group_count, top_partner, top_count,
    lsem, ssem, rsem, csem,
):
    leaf = lax.axis_index("leaf")
    sub = lax.axis_index("sub")
    col, ylo = lax.div(leaf, 2), lax.rem(leaf, 2)
    z, x = lax.div(col, 4), lax.rem(col, 4)
    member = ylo * 4 + sub
    b = leaf * 4 + sub
    half = lax.div(sub, 2)

    source = member == z
    odd = lax.rem(member, 2)
    other = 4 - 4 * ylo
    far_after, far_before = lax.rem(member, 4) == 1, lax.rem(member, 4) == 2

    def column_peer(m):
        return (col * 2 + lax.div(m, 4), lax.rem(m, 4))

    def ring_peer(step):
        n = lax.rem(b + step, 256)
        return (lax.div(n, 4), lax.rem(n, 4))

    col_peers = [column_peer(lax.rem(member + d, 8)) for d in range(8)]
    plane_peers = [(lax.rem(col + d, 32) * 2 + ylo, sub) for d in range(32)]
    plane_sources = [((member * 4 + i) * 2 + ylo, sub) for i in range(4)]
    sub_peers = [(leaf, lax.rem(sub + d, 4)) for d in range(4)]
    after, before = ring_peer(1), ring_peer(255)
    g_after = (lax.rem(leaf + 1, 64), sub)
    g_before = (lax.rem(leaf + 63, 64), sub)

    local = []

    def fetch(src, dst):
        cp = pltpu.make_async_copy(src, dst, lsem.at[len(local)])
        cp.start()
        local.append(cp)
        return cp

    w_x = [fetch(x_hbm.at[:, pl.ds(128 * m, 128)], xs.at[4 + m]) for m in range(8)]
    w_b = [fetch(basis_hbm, bs)]
    w_lt = [fetch(ltrans_hbm, lt)]
    w_gt = [fetch(gtrans_hbm, gt_in)]
    w_tt = [fetch(ttrans_hbm, tt)]
    w_tc = [fetch(tcouple_hbm, tc)]
    w_top = [fetch(top_partner_hbm, top_partner), fetch(top_count_hbm, top_count)]
    w_nb = [fetch(near_hbm, nb), fetch(near_list_hbm, near_list)]
    w_lc = [fetch(lcouple_hbm, lc), fetch(local_partner_hbm, local_partner), fetch(local_count_hbm, local_count)]
    w_gc = [fetch(gcouple_hbm, gc), fetch(group_partner_hbm, group_partner), fetch(group_count_hbm, group_count)]

    def ready(copies):
        for cp in copies:
            cp.wait()

    barrier = pltpu.get_barrier_semaphore()
    def greet(peers):
        for peer in peers:
            pl.semaphore_signal(barrier, inc=1, device_id=peer, device_id_type=MESH)

    greet(col_peers[1:] + [after, before, g_after, g_before])

    @pl.when(source)
    def _():
        greet(plane_peers[1:])

    @pl.when(jnp.logical_not(source))
    def _():
        greet(plane_sources)

    def copy(src, dst, sent, got, peer):
        return pltpu.make_async_remote_copy(
            src_ref=src, dst_ref=dst, send_sem=ssem.at[sent], recv_sem=rsem.at[got],
            device_id=peer, device_id_type=MESH,
        )

    def send(src, dst, place, peer):
        cp = copy(src, dst, place, place, peer)
        cp.start()
        return cp

    lane = iota((1, 128), 1)
    left = lane < 64
    m_left = jnp.where(left, 1.0, 0.0).astype(BF)
    m_right = jnp.where(left, 0.0, 1.0).astype(BF)
    row, column = iota((128, 128), 0), iota((128, 128), 1)
    from_row = lax.div(row, 64) * 64 + 2 * lax.rem(row, 32) + lax.div(lax.rem(row, 64), 32)
    pp[...] = jnp.where(column == from_row, 1.0, 0.0).astype(BF)
    eye = jnp.where(iota((64, 64), 0) == iota((64, 64), 1), 1.0, 0.0).astype(BF)

    def unpack(load, n, dst, masked):
        if masked:
            cluster = iota((n, 128), 0)
            side = lax.rem(lax.div(cluster, 2), 2)
            if n == 31:
                side = jnp.where(cluster == 30, 0, side)
            lanes = iota((n, 128), 1)
            keep_l = (side == 0) & (lanes < 64)
            keep_r = (side == 1) & (lanes >= 64)
        for j in range(32):
            v = load(j).astype(F32)
            r = half_swap(v)
            if masked:
                zero = jnp.zeros_like(v)
                even = jnp.where(keep_l, v, jnp.where(keep_r, r, zero))
                odd = jnp.where(keep_l, r, jnp.where(keep_r, v, zero))
            else:
                even = jnp.where(left, v, r)
                odd = jnp.where(left, r, v)
            dst[pl.ds(2 * j, n, stride=64), :] = even
            dst[pl.ds(2 * j + 1, n, stride=64), :] = odd

    ready(w_x)
    ready(w_b)
    for m in range(8):
        two = bs[:, 128 * m : 128 * m + 128]
        both = jnp.concatenate([two * m_left, two * m_right], axis=0)
        bd[m] = both
        tab[16 + m] = nt(xs[4 + m], both).astype(BF)
    ready(w_lt)
    ready(w_gt)

    def upward():
        unpack(lambda j: lt[:, 128 * j : 128 * j + 128], 31, ef, True)
        es[...] = ef[...].astype(BF)
        unpack(lambda j: gt_in[:, 128 * j : 128 * j + 128], 3, gf, False)
        ge[...] = gf[...].astype(BF).reshape(3, 64, 128)
        e_root = es[30 * 64 : 31 * 64, :]
        pair_down = nn(ge[half][:, :64], ge[2]).astype(BF)
        h_root = nn(e_root[:, :64], pair_down).astype(BF)
        hr[...] = h_root
        for lo, hi, n in ((16, 24, 4), (24, 28, 2), (28, 30, 1)):
            for i in range(n):
                kids = jnp.concatenate([tab[lo + 2 * i], tab[lo + 2 * i + 1]], axis=1)
                first = 2 * (lo - 16) + 4 * i
                tab[hi + i] = nn(kids, es[first * 64 : first * 64 + 256, :]).astype(BF)
        c_root = nn(tab[30], es[28 * 64 : 30 * 64, :]).astype(BF)
        tab[31] = c_root
        q = nn(c_root[:, :64], h_root)
        qb[...] = jnp.where(left, q[:32], q[32:]).astype(BF)
        ub[...] = nn(c_root[:, :64], e_root).astype(BF)

    def seen(l, first):
        mine = TOP_OFF[l] + lax.div(col, 2**l)
        total = jnp.zeros((64, 128), F32)
        for k in range(3):
            partner = jnp.where(k < top_count[mine], top_partner[k, mine], -1)
            target = jnp.where(left, first, first + 1)
            total = total + jnp.where(target == partner, gs[3 * l + k], 0.0)
        return total

    def prepare_top():
        wanted = [60 + lax.div(member, 4), 56 + lax.div(member, 2), 48 + member]
        wanted += [32 + 2 * member + i for i in range(2)] + [4 * member + i for i in range(4)]
        wanted += [TOP_OFF[l] + lax.div(col, 2**l) for l in range(5)]

        def pick(rows, n, clusters):
            at = iota((rows, n), 0)
            cluster = at * 0 - 1
            for i, c in enumerate(clusters):
                cluster = jnp.where(at == i, c, cluster)
            return jnp.where(iota((rows, n), 1) == cluster, 1.0, 0.0).astype(BF)

        rows = nn(pick(16, 62, wanted), tt[...])
        unpack(lambda j: rows[:, 128 * j : 128 * j + 128], 16, tf, False)
        et[...] = tf[...].astype(BF)
        ancestors = pick(8, 63, [TOP_OFF[l] + lax.div(col, 2**l) for l in range(6)])
        for k in range(3):
            rows = nn(ancestors, tc[k])
            unpack(lambda j: rows[:, 128 * j : 128 * j + 128], 8, sf.at[pl.ds(512 * k, 512)], False)
        ts[...] = sf[...].astype(BF)
        path = None
        for l in range(6):
            for k in range(3):
                at = (8 * k + l) * 64
                gs[3 * l + k] = sf[at : at + 64, :] if l == 0 else nn(path[:, :64], ts[at : at + 64, :])
            if l < 5:
                step = et[(9 + l) * 64 : (10 + l) * 64, :]
                path = step if l == 0 else nn(path[:, :64], step).astype(BF)
        v = seen(5, 62)
        for i, l in enumerate((4, 3, 2)):
            v = nt(v[:, :64].astype(BF), et[64 * i : 64 * i + 64, :64]) + seen(l, wanted[i])[:, :64]
        v = nt(v.astype(BF), et[3 * 64 : 5 * 64, :64]) + seen(1, wanted[3])
        w = jnp.concatenate([et[5 * 64 : 7 * 64, :] * m_left, et[7 * 64 : 9 * 64, :] * m_right], axis=0)
        v = nt(v.astype(BF), w)
        v = v + jnp.concatenate([seen(0, wanted[5]), seen(0, wanted[7])], axis=1)
        zb[...] = v.astype(BF)

    def peer_or(far, place, near):
        peer = column_peer(place)
        return tuple(jnp.where(far, a, c) for a, c in zip(peer, near))

    def exchange(ref, kind):
        k, n, to_after, to_before, from_before, from_after, kept = kind
        copies = []
        for h in range(2):
            cp = copy(
                ref.at[pl.ds(to_after + h * n, n)],
                ref.at[pl.ds(jnp.where(far_after, kept, from_before + h * n), n)],
                S_B + 4 * k + h,
                jnp.where(far_after, S_F + k, S_B + 4 * k + h),
                peer_or(far_after, other + 2 * h, after),
            )
            cp.start()
            copies.append(cp)
            cp = copy(
                ref.at[pl.ds(to_before + h * n, n)],
                ref.at[pl.ds(jnp.where(far_before, kept, from_after + h * n), n)],
                S_B + 4 * k + 2 + h,
                jnp.where(far_before, S_F + k, S_B + 4 * k + 2 + h),
                peer_or(far_before, other + 2 * h + 1, before),
            )
            cp.start()
            copies.append(cp)
        return copies

    def forward(ref, kind):
        k, n, _, _, from_before, from_after, kept = kind
        mine = ref.at[pl.ds(kept, n)]
        copy(mine, mine, S_F + k, S_F + k, col_peers[1]).wait_recv()
        cp = copy(
            mine,
            ref.at[pl.ds(jnp.where(odd == 1, from_after, from_before) + half * n, n)],
            S_F + k,
            S_B + 4 * k + 2 * odd + half,
            column_peer(other + 2 - odd),
        )
        cp.start()
        return cp

    def arrived(ref, kind):
        k, n, _, _, from_before, from_after, _ = kind
        for side, first in enumerate((from_before, from_after)):
            for h in range(2):
                part = ref.at[pl.ds(first + h * n, n)]
                copy(part, part, S_F, S_B + 4 * k + 2 * side + h, col_peers[1]).wait_recv()

    pl.semaphore_wait(barrier, jnp.where(source, 42, 15))
    c_bulk = exchange(xs, HALO) + exchange(tab, LEAVES)
    upward()

    c_q = copy(qb, p1.at[member], S_Q, S_Q + member, column_peer(z))

    @pl.when(jnp.logical_not(source))
    def _():
        c_q.start()

    c_u = [send(ub, gu.at[sub], S_U + d, sub_peers[d]) for d in range(1, 4)]
    gu[sub] = ub[...]
    c_upper = exchange(tab, UPPER)
    c_forward = [forward(xs, HALO), forward(tab, LEAVES)]

    ready(w_tt)
    ready(w_tc)
    ready(w_top)
    prepare_top()

    c_c = [
        pltpu.make_async_remote_copy(
            src_ref=p3.at[x], dst_ref=p3.at[x], send_sem=csem.at[d], recv_sem=rsem.at[S_C + x],
            device_id=plane_peers[d], device_id_type=MESH,
        )
        for d in range(1, 32)
    ]

    @pl.when(source)
    def _():
        p1[member] = qb[...]
        for m in range(8):

            @pl.when(member != m)
            def _(m=m):
                copy(qb, p1.at[m], S_Q, S_Q + m, col_peers[1]).wait_recv()

        total = p1[0].astype(F32)
        for m in range(1, 8):
            total = total + p1[m].astype(F32)
        p3[x] = total.astype(BF)
        for cp in c_c:
            cp.start()

    c_forward.append(forward(tab, UPPER))

    def widen(src, dst, lo, n):
        def step(i, carry):
            for h in range(8):
                at = lo + 8 * i + h
                v = src[at]
                r = half_swap(v)
                dst[2 * at] = jnp.concatenate([v * m_left, r * m_right], axis=0)
                dst[2 * at + 1] = jnp.concatenate([r * m_left, v * m_right], axis=0)
            return carry

        lax.fori_loop(0, n, step, 0)

    def spread(load, n, ref):
        for j in range(32):
            ref[pl.ds(j, n, stride=32), :] = load(j).astype(F32)
        even, odd = [], []
        for k in range(0, n, 2):
            one, two = ref[32 * k : 32 * k + 32, :], ref[32 * k + 32 : 32 * k + 64, :]
            even.append(jnp.where(left, one, half_swap(two)))
            odd.append(jnp.where(left, half_swap(one), two))
        rows = [jnp.concatenate(even, axis=1), jnp.concatenate(odd, axis=1)]
        return jnp.concatenate(rows, axis=0).astype(BF)

    def coupled(table, ids, w):
        pairs = [table[ids[k], 0:64, :] + table[ids[k + 1], 64:128, :] for k in range(0, len(ids), 2)]
        return nt(jnp.concatenate(pairs, axis=1), w)

    def in_order(one, two):
        return nn(jnp.concatenate([one, two], axis=1).astype(BF), pp[...])

    ready(w_nb)
    widen(xs, xbd, 4, 1)
    arrived(xs, HALO)
    for at in (0, 12):
        for h in range(4):
            v = xs[at + h]
            r = half_swap(v)
            xbd[2 * (at + h)] = jnp.concatenate([v * m_left, r * m_right], axis=0)
            xbd[2 * (at + h) + 1] = jnp.concatenate([r * m_left, v * m_right], axis=0)

    def near_step(i, carry):
        weights = []
        for h in range(8):
            t = 8 * i + h
            weights.append(spread(lambda j: nb[t, :, 128 * j : 128 * j + 128], 8, rl.at[h]))
        parts = []
        for h in range(8):
            ids = [jnp.clip(near_list[k, 8 * i + h] - (b * 16 - 8), 0, 31) for k in range(8)]
            parts.append(coupled(xbd, ids, weights[h]))
        for h in range(4):
            nearp[4 * i + h] = in_order(parts[2 * h], parts[2 * h + 1])
        return carry

    lax.fori_loop(0, 2, near_step, 0)

    c_d = [copy(p4.at[member], p4.at[member], S_D + d, S_D + d, col_peers[d]) for d in range(1, 8)]
    for i in range(4):

        @pl.when(jnp.logical_not(source & (x == i)))
        def _(i=i):
            copy(p3.at[i], p3.at[i], S_C, S_C + i, col_peers[1]).wait_recv()

    have = []
    for i in (0, 2):
        up = p3[i] * m_left + half_swap(p3[i + 1]) * m_right
        down = half_swap(p3[i]) * m_left + p3[i + 1] * m_right
        have.append(jnp.concatenate([up, down], axis=0))
    d = nt(jnp.concatenate(have, axis=1), zb[...])
    p4[member] = jnp.concatenate([d[:32], d[32:]], axis=1).astype(BF)
    for cp in c_d:
        cp.start()

    ready(w_lc)

    def far_step(i, carry):
        weights = []
        for h in range(8):
            c = jnp.minimum(8 * i + h, 30)
            weights.append(spread(lambda j: lc[c, :, 128 * j : 128 * j + 128], 8, rl.at[h]))
        parts = []
        for h in range(8):
            c = jnp.minimum(8 * i + h, 30)
            count = jnp.where(8 * i + h < 31, local_count[c], 0)
            ids = []
            for k in range(8):
                e = jnp.clip(local_partner[k, c] - (b - 1) * 31, 0, 92)
                e = e + jnp.where(e >= 31, 1, 0) + jnp.where(e >= 62, 1, 0)
                ids.append(jnp.where(k < count, e, 63))
            parts.append(coupled(bdt, ids, weights[h]))
        for h in range(4):
            far[4 * i + h] = in_order(parts[2 * h], parts[2 * h + 1])
        return carry

    widen(tab, bdt, 16, 2)
    arrived(tab, LEAVES)
    widen(tab, bdt, 0, 1)
    widen(tab, bdt, 32, 1)
    lax.fori_loop(0, 2, far_step, 0)

    for cp in c_u:
        cp.wait_recv()
    g0 = (gu[0].astype(F32) + gu[1].astype(F32)).astype(BF)
    g1 = (gu[2].astype(F32) + gu[3].astype(F32)).astype(BF)
    g2 = (nn(g0[:, :64], ge[0]) + nn(g1[:, :64], ge[1])).astype(BF)
    gt[3] = g0 + half_swap(g0)
    gt[4] = g1 + half_swap(g1)
    gt[5] = g2
    gt[9] = jnp.zeros((64, 128), BF)
    c_gt = [
        send(gt.at[pl.ds(3, 3)], gt.at[pl.ds(0, 3)], S_GT, g_after),
        send(gt.at[pl.ds(3, 3)], gt.at[pl.ds(6, 3)], S_GT + 1, g_before),
    ]

    arrived(tab, UPPER)
    widen(tab, bdt, 8, 1)
    widen(tab, bdt, 40, 1)
    lax.fori_loop(2, 4, far_step, 0)

    ready(w_gc)
    for cp in c_gt:
        cp.wait_recv()
    found = []
    for c in range(3):
        w = spread(lambda j: gc[c, :, 128 * j : 128 * j + 128], 4, rl.at[c])
        entries = []
        for k in range(4):
            e = jnp.clip(group_partner[c, k] - (leaf - 1) * 3, 0, 8)
            entries.append(gt[jnp.where(k < group_count[c], e, 9)])
        pairs = [entries[k] * m_left + entries[k + 1] * m_right for k in (0, 2)]
        found.append(nt(jnp.concatenate(pairs, axis=1), w))
    f01 = in_order(found[0], found[1])
    f2 = in_order(found[2], found[2])
    f_half = jnp.where(half == 0, f01, half_swap(f01))[:, :64]
    d_half = f_half + nt(f2[:, :64].astype(BF), ge[half][:, :64])

    e_root = es[30 * 64 : 31 * 64, :]
    d_root = far[15][:, :64] + nt(d_half.astype(BF), e_root[:, :64])
    state = jnp.concatenate([d_root, nt(eye, hr[...][:, :64])], axis=0).astype(BF)
    nothing = jnp.zeros((64, 128), F32)

    def with_far(v, i):
        return (v + jnp.concatenate([far[i], nothing], axis=0)).astype(BF)

    states = [with_far(nt(state, es[28 * 64 : 30 * 64, :64]), 14)]
    for first, pair in ((24, 12), (16, 8), (0, 0)):
        lower_level = []
        for i, parents in enumerate(states):
            at = (first + 4 * i) * 64
            both = nt(parents, es[at : at + 256, :])
            lower_level.append(with_far(both[:, :128], pair + 2 * i))
            lower_level.append(with_far(both[:, 128:], pair + 2 * i + 1))
        states = lower_level
    for m in range(8):
        r = nn(states[m], bd[m])
        nearp[m] = nearp[m] + r[:64]
        vht[m] = r[64:].astype(BF)

    for cp in c_d:
        cp.wait_recv()
    total = p4[0].astype(F32)
    for m in range(1, 8):
        total = total + p4[m].astype(F32)
    d_col = jnp.concatenate([total[:, :64], total[:, 64:]], axis=0).astype(BF)
    for m in range(8):
        out[:, 128 * m : 128 * m + 128] = nearp[m] + nn(d_col, vht[m])

    for cp in c_bulk + c_upper + c_forward + c_u + c_gt + c_d:
        cp.wait_send()

    @pl.when(source)
    def _():
        for cp in c_c:
            cp.wait_send()

    @pl.when(jnp.logical_not(source))
    def _():
        c_q.wait_send()


def body(
    right_sides, leaf_basis, near_blocks, near_list, local_transfer, local_couple, local_partner, local_count,
    group_transfer, group_couple, group_partner, group_count, top_transfer, top_couple, top_partner, top_count,
):
    hbm = pl.BlockSpec(memory_space=pltpu.HBM)
    vm = pltpu.VMEM
    return pl.pallas_call(
        kernel,
        out_shape=jax.ShapeDtypeStruct((64, 1024), F32),
        in_specs=[hbm] * 16,
        out_specs=pl.BlockSpec(memory_space=pltpu.VMEM),
        scratch_shapes=[
            vm((18, 64, 128), BF),
            vm((64, 1024), BF),
            vm((16, 8, 4096), BF),
            vm((31, 4096), BF),
            vm((31, 8, 4096), BF),
            vm((3, 4096), BF),
            vm((3, 4, 4096), BF),
            vm((62, 4096), BF),
            vm((3, 63, 4096), BF),
            vm((31 * 64, 128), F32),
            vm((31 * 64, 128), BF),
            vm((3 * 64, 128), F32),
            vm((3, 64, 128), BF),
            vm((16 * 64, 128), F32),
            vm((16 * 64, 128), BF),
            vm((24 * 64, 128), F32),
            vm((24 * 64, 128), BF),
            vm((8, 128, 128), BF),
            vm((56, 64, 128), BF),
            vm((96, 128, 128), BF),
            vm((32, 128, 128), BF),
            vm((128, 128), BF),
            vm((8, 256, 128), F32),
            vm((32, 128), BF),
            vm((64, 128), BF),
            vm((8, 32, 128), BF),
            vm((4, 32, 128), BF),
            vm((8, 32, 128), BF),
            vm((64, 128), BF),
            vm((4, 64, 128), BF),
            vm((10, 64, 128), BF),
            vm((18, 64, 128), F32),
            vm((64, 256), BF),
            vm((16, 64, 128), F32),
            vm((8, 64, 128), F32),
            vm((8, 64, 128), BF),
            pltpu.SMEM((8, 16), jnp.int32),
            pltpu.SMEM((8, 31), jnp.int32),
            pltpu.SMEM((31,), jnp.int32),
            pltpu.SMEM((3, 4), jnp.int32),
            pltpu.SMEM((3,), jnp.int32),
            pltpu.SMEM((3, 63), jnp.int32),
            pltpu.SMEM((63,), jnp.int32),
            pltpu.SemaphoreType.DMA((24,)),
            pltpu.SemaphoreType.DMA((N_SEM,)),
            pltpu.SemaphoreType.DMA((N_SEM,)),
            pltpu.SemaphoreType.DMA((32,)),
        ],
        compiler_params=pltpu.CompilerParams(
            collective_id=0, has_side_effects=True, vmem_limit_bytes=60 * 1024 * 1024
        ),
        name="h2",
    )(
        near_list.T, local_partner.T, local_count, group_partner, group_count, top_partner.T, top_count,
        right_sides, leaf_basis, near_blocks, local_transfer, local_couple, group_transfer, group_couple,
        top_transfer, jnp.transpose(top_couple, (1, 0, 2)),
    )


def solution(mesh):
    both = ("leaf", "sub")
    placed = (
        P(None, both), P(None, both), P(both, None, None), P(both, None), P(both, None), P(both, None, None),
        P(both, None), P(both), P("leaf", None), P("leaf", None, None), P("leaf", None), P("leaf"),
        P(), P(), P(), P(),
    )
    return jax.shard_map(body, mesh=mesh, in_specs=placed, out_specs=P(None, both), check_vma=False)
```

```python
import functools

import jax
import jax.numpy as jnp
from jax import lax
from jax.experimental import pallas as pl
from jax.experimental.pallas import tpu as pltpu
from jax.sharding import PartitionSpec as P

BF = jnp.bfloat16
F32 = jnp.float32
MESH = pl.DeviceIdType.MESH
TOP_OFF = (0, 32, 48, 56, 60, 62)
S_Q, S_C, S_D, S_U, S_XH, S_TAB, S_GT, N_SEM = 0, 8, 12, 20, 24, 26, 30, 32


def nt(a, b):
    return lax.dot_general(a, b, (((1,), (1,)), ((), ())), preferred_element_type=F32)


def nn(a, b):
    return jnp.dot(a, b, preferred_element_type=F32)


def half_swap(v):
    return pltpu.roll(v, 64, 1)


def iota(shape, dim):
    return lax.broadcasted_iota(jnp.int32, shape, dim)


def kernel(
    near_list_hbm, local_partner_hbm, local_count_hbm, group_partner_hbm, group_count_hbm, top_partner_hbm,
    top_count_hbm, x_hbm, basis_hbm, near_hbm, ltrans_hbm, lcouple_hbm, gtrans_hbm, gcouple_hbm, ttrans_hbm, tcouple_hbm,
    out,
    xs, bs, nb, lt, lc, gt_in, gc, tt, tc,
    es, ge, et, ts, bd, tab, bdt, xbd, pp,
    qb, hr, p1, p3, p4, ub, gu, gt, gs, zb, far, nearp, vht,
    near_list, local_partner, local_count, group_partner, group_count, top_partner, top_count,
    lsem, ssem, rsem, csem,
):
    leaf = lax.axis_index("leaf")
    sub = lax.axis_index("sub")
    col, ylo = lax.div(leaf, 2), lax.rem(leaf, 2)
    z, x = lax.div(col, 4), lax.rem(col, 4)
    member = ylo * 4 + sub
    b = leaf * 4 + sub
    half = lax.div(sub, 2)

    source = member == z

    def column_peer(m):
        return (col * 2 + lax.div(m, 4), lax.rem(m, 4))

    def ring_peer(step):
        n = lax.rem(b + step, 256)
        return (lax.div(n, 4), lax.rem(n, 4))

    col_peers = [column_peer(lax.rem(member + d, 8)) for d in range(8)]
    plane_peers = [(lax.rem(col + d, 32) * 2 + ylo, sub) for d in range(32)]
    plane_sources = [((member * 4 + i) * 2 + ylo, sub) for i in range(4)]
    sub_peers = [(leaf, lax.rem(sub + d, 4)) for d in range(4)]
    after, before = ring_peer(1), ring_peer(255)
    g_after = (lax.rem(leaf + 1, 64), sub)
    g_before = (lax.rem(leaf + 63, 64), sub)

    local = []

    def fetch(src, dst):
        cp = pltpu.make_async_copy(src, dst, lsem.at[len(local)])
        cp.start()
        local.append(cp)
        return cp

    w_x = [fetch(x_hbm.at[:, pl.ds(128 * m, 128)], xs.at[4 + m]) for m in range(8)]
    w_b = [fetch(basis_hbm, bs)]
    w_lt = [fetch(ltrans_hbm, lt)]
    w_gt = [fetch(gtrans_hbm, gt_in)]
    w_tt = [fetch(ttrans_hbm, tt)]
    w_tc = [fetch(tcouple_hbm, tc)]
    w_top = [fetch(top_partner_hbm, top_partner), fetch(top_count_hbm, top_count)]
    w_nb = [fetch(near_hbm, nb), fetch(near_list_hbm, near_list)]
    w_lc = [fetch(lcouple_hbm, lc), fetch(local_partner_hbm, local_partner), fetch(local_count_hbm, local_count)]
    w_gc = [fetch(gcouple_hbm, gc), fetch(group_partner_hbm, group_partner), fetch(group_count_hbm, group_count)]

    def ready(copies):
        for cp in copies:
            cp.wait()

    barrier = pltpu.get_barrier_semaphore()
    def greet(peers):
        for peer in peers:
            pl.semaphore_signal(barrier, inc=1, device_id=peer, device_id_type=MESH)

    greet(col_peers[1:] + [after, before, g_after, g_before])

    @pl.when(source)
    def _():
        greet(plane_peers[1:])

    @pl.when(jnp.logical_not(source))
    def _():
        greet(plane_sources)

    def copy(src, dst, sent, got, peer):
        return pltpu.make_async_remote_copy(
            src_ref=src, dst_ref=dst, send_sem=ssem.at[sent], recv_sem=rsem.at[got],
            device_id=peer, device_id_type=MESH,
        )

    def send(src, dst, place, peer):
        cp = copy(src, dst, place, place, peer)
        cp.start()
        return cp

    lane = iota((1, 128), 1)
    left = lane < 64
    m_left = jnp.where(left, 1.0, 0.0).astype(BF)
    m_right = jnp.where(left, 0.0, 1.0).astype(BF)
    row, column = iota((128, 128), 0), iota((128, 128), 1)
    from_row = lax.div(row, 64) * 64 + 2 * lax.rem(row, 32) + lax.div(lax.rem(row, 64), 32)
    pp[...] = jnp.where(column == from_row, 1.0, 0.0).astype(BF)
    eye = jnp.where(iota((64, 64), 0) == iota((64, 64), 1), 1.0, 0.0).astype(BF)

    def unpack(load):
        parts = []
        for lo in (0, 16):
            tiles = []
            for j in range(lo, lo + 16):
                v = load(j)
                tiles += [v, half_swap(v)]
            parts.append(jnp.swapaxes(jnp.stack(tiles), 0, 1))
        return lambda c: jnp.concatenate([part[c] for part in parts], axis=0).astype(BF)

    def filled(v):
        v = v.astype(F32)
        if v.shape[0] == 8:
            return v
        return jnp.concatenate([v, jnp.zeros((8 - v.shape[0], 128), F32)], axis=0)

    def on_left(v):
        return v * m_left

    def on_right(v):
        return half_swap(v * m_left)

    def on_both(v):
        return on_left(v) + on_right(v)

    ready(w_x)
    ready(w_b)
    for m in range(8):
        two = bs[:, 128 * m : 128 * m + 128]
        both = jnp.concatenate([two * m_left, two * m_right], axis=0)
        bd[m] = both
        tab[16 + m] = nt(xs[4 + m], both).astype(BF)
    ready(w_lt)
    ready(w_gt)

    def upward():
        for lo in range(0, 31, 8):
            hi = min(lo + 8, 31)
            matrix = unpack(lambda j: filled(lt[lo:hi, 128 * j : 128 * j + 128]))
            for c in range(lo, hi):
                right = c < 30 and (c // 2) % 2 == 1
                v = matrix(c - lo)
                es[64 * c : 64 * c + 64, :] = on_right(v) if right else on_left(v)
        matrix = unpack(lambda j: filled(gt_in[:, 128 * j : 128 * j + 128]))
        for c in range(3):
            ge[c] = on_both(matrix(c))
        e_root = es[30 * 64 : 31 * 64, :]
        pair_down = nn(ge[half][:, :64], ge[2]).astype(BF)
        h_root = nn(e_root[:, :64], pair_down).astype(BF)
        hr[...] = h_root
        for lo, hi, n in ((16, 24, 4), (24, 28, 2), (28, 30, 1)):
            for i in range(n):
                kids = jnp.concatenate([tab[lo + 2 * i], tab[lo + 2 * i + 1]], axis=1)
                first = 2 * (lo - 16) + 4 * i
                tab[hi + i] = nn(kids, es[first * 64 : first * 64 + 256, :]).astype(BF)
        c_root = nn(tab[30], es[28 * 64 : 30 * 64, :]).astype(BF)
        tab[31] = c_root
        q = nn(c_root[:, :64], h_root)
        qb[...] = jnp.where(left, q[:32], q[32:]).astype(BF)
        ub[...] = nn(c_root[:, :64], e_root).astype(BF)

    def seen(l, first):
        mine = TOP_OFF[l] + lax.div(col, 2**l)
        total = jnp.zeros((64, 128), F32)
        for k in range(3):
            partner = jnp.where(k < top_count[mine], top_partner[k, mine], -1)
            target = jnp.where(left, first, first + 1)
            total = total + jnp.where(target == partner, gs[3 * l + k], 0.0)
        return total

    def prepare_top():
        wanted = [60 + lax.div(member, 4), 56 + lax.div(member, 2), 48 + member]
        wanted += [32 + 2 * member + i for i in range(2)] + [4 * member + i for i in range(4)]
        wanted += [TOP_OFF[l] + lax.div(col, 2**l) for l in range(5)]

        def pick(rows, n, clusters):
            at = iota((rows, n), 0)
            cluster = at * 0 - 1
            for i, c in enumerate(clusters):
                cluster = jnp.where(at == i, c, cluster)
            return jnp.where(iota((rows, n), 1) == cluster, 1.0, 0.0).astype(BF)

        rows = nn(pick(16, 62, wanted), tt[...])
        for lo in (0, 8):
            matrix = unpack(lambda j: rows[lo : lo + 8, 128 * j : 128 * j + 128])
            for c in range(lo, min(lo + 8, 14)):
                v = matrix(c - lo)
                et[64 * c : 64 * c + 64, :] = on_right(v) if c in (7, 8) else on_left(v) if c < 9 else on_both(v)
        ancestors = pick(8, 63, [TOP_OFF[l] + lax.div(col, 2**l) for l in range(6)])
        for k in range(3):
            rows = nn(ancestors, tc[k])
            matrix = unpack(lambda j: rows[:, 128 * j : 128 * j + 128])
            for l in range(6):
                ts[3 * l + k] = on_both(matrix(l))
        path = None
        for l in range(6):
            for k in range(3):
                s = ts[3 * l + k]
                gs[3 * l + k] = s.astype(F32) if l == 0 else nn(path[:, :64], s)
            if l < 5:
                step = et[(9 + l) * 64 : (10 + l) * 64, :]
                path = step if l == 0 else nn(path[:, :64], step).astype(BF)
        v = seen(5, 62)
        for i, l in enumerate((4, 3, 2)):
            v = nt(v[:, :64].astype(BF), et[64 * i : 64 * i + 64, :64]) + seen(l, wanted[i])[:, :64]
        v = nt(v.astype(BF), et[3 * 64 : 5 * 64, :64]) + seen(1, wanted[3])
        v = nt(v.astype(BF), et[5 * 64 : 9 * 64, :])
        v = v + jnp.concatenate([seen(0, wanted[5]), seen(0, wanted[7])], axis=1)
        zb[...] = v.astype(BF)

    upward()
    pl.semaphore_wait(barrier, jnp.where(source, 42, 15))

    c_q = copy(qb, p1.at[member], S_Q, S_Q + member, column_peer(z))

    @pl.when(jnp.logical_not(source))
    def _():
        c_q.start()

    c_u = [send(ub, gu.at[sub], S_U + d, sub_peers[d]) for d in range(1, 4)]
    gu[sub] = ub[...]
    c_xh = [
        send(xs.at[pl.ds(8, 4)], xs.at[pl.ds(0, 4)], S_XH, after),
        send(xs.at[pl.ds(4, 4)], xs.at[pl.ds(12, 4)], S_XH + 1, before),
    ]
    leaves_own, upper_own = tab.at[pl.ds(16, 8)], tab.at[pl.ds(24, 8)]
    c_leaves = [
        send(leaves_own, tab.at[pl.ds(0, 8)], S_TAB, after),
        send(leaves_own, tab.at[pl.ds(32, 8)], S_TAB + 1, before),
    ]
    c_upper = [
        send(upper_own, tab.at[pl.ds(8, 8)], S_TAB + 2, after),
        send(upper_own, tab.at[pl.ds(40, 8)], S_TAB + 3, before),
    ]

    ready(w_tt)
    ready(w_tc)
    ready(w_top)
    prepare_top()

    c_c = [
        pltpu.make_async_remote_copy(
            src_ref=p3.at[x], dst_ref=p3.at[x], send_sem=csem.at[d], recv_sem=rsem.at[S_C + x],
            device_id=plane_peers[d], device_id_type=MESH,
        )
        for d in range(1, 32)
    ]

    @pl.when(source)
    def _():
        p1[member] = qb[...]
        for m in range(8):

            @pl.when(member != m)
            def _(m=m):
                copy(qb, p1.at[m], S_Q, S_Q + m, col_peers[1]).wait_recv()

        total = p1[0].astype(F32)
        for m in range(1, 8):
            total = total + p1[m].astype(F32)
        p3[x] = total.astype(BF)
        for cp in c_c:
            cp.start()

    def widen(src, dst, lo, n):
        def step(i, carry):
            for h in range(8):
                at = lo + 8 * i + h
                v = src[at]
                r = half_swap(v)
                dst[2 * at] = jnp.concatenate([v * m_left, r * m_right], axis=0)
                dst[2 * at + 1] = jnp.concatenate([r * m_left, v * m_right], axis=0)
            return carry

        lax.fori_loop(0, n, step, 0)

    def spread(load, n):
        tiles = jnp.swapaxes(jnp.stack([load(j).astype(F32) for j in range(32)]), 0, 1)
        even, odd = [], []
        for k in range(0, n, 2):
            one, two = tiles[k], tiles[k + 1]
            even.append(jnp.where(left, one, half_swap(two)))
            odd.append(jnp.where(left, half_swap(one), two))
        rows = [jnp.concatenate(even, axis=1), jnp.concatenate(odd, axis=1)]
        return jnp.concatenate(rows, axis=0).astype(BF)

    def coupled(table, ids, w):
        pairs = [table[ids[k], 0:64, :] + table[ids[k + 1], 64:128, :] for k in range(0, len(ids), 2)]
        return nt(jnp.concatenate(pairs, axis=1), w)

    def in_order(one, two):
        return nn(jnp.concatenate([one, two], axis=1).astype(BF), pp[...])

    ready(w_nb)
    widen(xs, xbd, 4, 1)
    for cp in c_xh:
        cp.wait_recv()
    for at in (0, 12):
        for h in range(4):
            v = xs[at + h]
            r = half_swap(v)
            xbd[2 * (at + h)] = jnp.concatenate([v * m_left, r * m_right], axis=0)
            xbd[2 * (at + h) + 1] = jnp.concatenate([r * m_left, v * m_right], axis=0)

    def near_step(i, carry):
        weights = []
        for h in range(8):
            t = 8 * i + h
            weights.append(spread(lambda j: nb[t, :, 128 * j : 128 * j + 128], 8))
        parts = []
        for h in range(8):
            ids = [jnp.clip(near_list[k, 8 * i + h] - (b * 16 - 8), 0, 31) for k in range(8)]
            parts.append(coupled(xbd, ids, weights[h]))
        for h in range(4):
            nearp[4 * i + h] = in_order(parts[2 * h], parts[2 * h + 1])
        return carry

    lax.fori_loop(0, 2, near_step, 0)

    c_d = [copy(p4.at[member], p4.at[member], S_D + d, S_D + d, col_peers[d]) for d in range(1, 8)]
    for i in range(4):

        @pl.when(jnp.logical_not(source & (x == i)))
        def _(i=i):
            copy(p3.at[i], p3.at[i], S_C, S_C + i, col_peers[1]).wait_recv()

    have = []
    for i in (0, 2):
        up = p3[i] * m_left + half_swap(p3[i + 1]) * m_right
        down = half_swap(p3[i]) * m_left + p3[i + 1] * m_right
        have.append(jnp.concatenate([up, down], axis=0))
    d = nt(jnp.concatenate(have, axis=1), zb[...])
    p4[member] = jnp.concatenate([d[:32], d[32:]], axis=1).astype(BF)
    for cp in c_d:
        cp.start()

    ready(w_lc)

    def far_step(i, carry):
        weights = []
        for h in range(8):
            c = jnp.minimum(8 * i + h, 30)
            weights.append(spread(lambda j: lc[c, :, 128 * j : 128 * j + 128], 8))
        parts = []
        for h in range(8):
            c = jnp.minimum(8 * i + h, 30)
            count = jnp.where(8 * i + h < 31, local_count[c], 0)
            ids = []
            for k in range(8):
                e = jnp.clip(local_partner[k, c] - (b - 1) * 31, 0, 92)
                e = e + jnp.where(e >= 31, 1, 0) + jnp.where(e >= 62, 1, 0)
                ids.append(jnp.where(k < count, e, 63))
            parts.append(coupled(bdt, ids, weights[h]))
        for h in range(4):
            far[4 * i + h] = in_order(parts[2 * h], parts[2 * h + 1])
        return carry

    widen(tab, bdt, 16, 2)
    for cp in c_leaves:
        cp.wait_recv()
    widen(tab, bdt, 0, 1)
    widen(tab, bdt, 32, 1)
    lax.fori_loop(0, 2, far_step, 0)

    for cp in c_u:
        cp.wait_recv()
    g0 = (gu[0].astype(F32) + gu[1].astype(F32)).astype(BF)
    g1 = (gu[2].astype(F32) + gu[3].astype(F32)).astype(BF)
    g2 = (nn(g0[:, :64], ge[0]) + nn(g1[:, :64], ge[1])).astype(BF)
    gt[3] = g0 + half_swap(g0)
    gt[4] = g1 + half_swap(g1)
    gt[5] = g2
    gt[9] = jnp.zeros((64, 128), BF)
    c_gt = [
        send(gt.at[pl.ds(3, 3)], gt.at[pl.ds(0, 3)], S_GT, g_after),
        send(gt.at[pl.ds(3, 3)], gt.at[pl.ds(6, 3)], S_GT + 1, g_before),
    ]

    for cp in c_upper:
        cp.wait_recv()
    widen(tab, bdt, 8, 1)
    widen(tab, bdt, 40, 1)
    lax.fori_loop(2, 4, far_step, 0)

    ready(w_gc)
    for cp in c_gt:
        cp.wait_recv()
    found = []
    for c in range(3):
        w = spread(lambda j: gc[c, :, 128 * j : 128 * j + 128], 4)
        entries = []
        for k in range(4):
            e = jnp.clip(group_partner[c, k] - (leaf - 1) * 3, 0, 8)
            entries.append(gt[jnp.where(k < group_count[c], e, 9)])
        pairs = [entries[k] * m_left + entries[k + 1] * m_right for k in (0, 2)]
        found.append(nt(jnp.concatenate(pairs, axis=1), w))
    f01 = in_order(found[0], found[1])
    f2 = in_order(found[2], found[2])
    f_half = jnp.where(half == 0, f01, half_swap(f01))[:, :64]
    d_half = f_half + nt(f2[:, :64].astype(BF), ge[half][:, :64])

    e_root = es[30 * 64 : 31 * 64, :]
    d_root = far[15][:, :64] + nt(d_half.astype(BF), e_root[:, :64])
    state = jnp.concatenate([d_root, nt(eye, hr[...][:, :64])], axis=0).astype(BF)
    nothing = jnp.zeros((64, 128), F32)

    def with_far(v, i):
        return (v + jnp.concatenate([far[i], nothing], axis=0)).astype(BF)

    states = [with_far(nt(state, es[28 * 64 : 30 * 64, :64]), 14)]
    for first, pair in ((24, 12), (16, 8), (0, 0)):
        lower_level = []
        for i, parents in enumerate(states):
            at = (first + 4 * i) * 64
            both = nt(parents, es[at : at + 256, :])
            lower_level.append(with_far(both[:, :128], pair + 2 * i))
            lower_level.append(with_far(both[:, 128:], pair + 2 * i + 1))
        states = lower_level
    for m in range(8):
        r = nn(states[m], bd[m])
        nearp[m] = nearp[m] + r[:64]
        vht[m] = r[64:].astype(BF)

    for cp in c_d:
        cp.wait_recv()
    total = p4[0].astype(F32)
    for m in range(1, 8):
        total = total + p4[m].astype(F32)
    d_col = jnp.concatenate([total[:, :64], total[:, 64:]], axis=0).astype(BF)
    for m in range(8):
        out[:, 128 * m : 128 * m + 128] = nearp[m] + nn(d_col, vht[m])

    for cp in c_u + c_xh + c_leaves + c_upper + c_gt + c_d:
        cp.wait_send()

    @pl.when(source)
    def _():
        for cp in c_c:
            cp.wait_send()

    @pl.when(jnp.logical_not(source))
    def _():
        c_q.wait_send()


def body(
    right_sides, leaf_basis, near_blocks, near_list, local_transfer, local_couple, local_partner, local_count,
    group_transfer, group_couple, group_partner, group_count, top_transfer, top_couple, top_partner, top_count,
):
    hbm = pl.BlockSpec(memory_space=pltpu.HBM)
    vm = pltpu.VMEM
    return pl.pallas_call(
        kernel,
        out_shape=jax.ShapeDtypeStruct((64, 1024), F32),
        in_specs=[hbm] * 16,
        out_specs=pl.BlockSpec(memory_space=pltpu.VMEM),
        scratch_shapes=[
            vm((16, 64, 128), BF),
            vm((64, 1024), BF),
            vm((16, 8, 4096), BF),
            vm((31, 4096), BF),
            vm((31, 8, 4096), BF),
            vm((3, 4096), BF),
            vm((3, 4, 4096), BF),
            vm((62, 4096), BF),
            vm((3, 63, 4096), BF),
            vm((31 * 64, 128), BF),
            vm((3, 64, 128), BF),
            vm((16 * 64, 128), BF),
            vm((18, 64, 128), BF),
            vm((8, 128, 128), BF),
            vm((48, 64, 128), BF),
            vm((96, 128, 128), BF),
            vm((32, 128, 128), BF),
            vm((128, 128), BF),
            vm((32, 128), BF),
            vm((64, 128), BF),
            vm((8, 32, 128), BF),
            vm((4, 32, 128), BF),
            vm((8, 32, 128), BF),
            vm((64, 128), BF),
            vm((4, 64, 128), BF),
            vm((10, 64, 128), BF),
            vm((18, 64, 128), F32),
            vm((64, 256), BF),
            vm((16, 64, 128), F32),
            vm((8, 64, 128), F32),
            vm((8, 64, 128), BF),
            pltpu.SMEM((8, 16), jnp.int32),
            pltpu.SMEM((8, 31), jnp.int32),
            pltpu.SMEM((31,), jnp.int32),
            pltpu.SMEM((3, 4), jnp.int32),
            pltpu.SMEM((3,), jnp.int32),
            pltpu.SMEM((3, 63), jnp.int32),
            pltpu.SMEM((63,), jnp.int32),
            pltpu.SemaphoreType.DMA((24,)),
            pltpu.SemaphoreType.DMA((N_SEM,)),
            pltpu.SemaphoreType.DMA((N_SEM,)),
            pltpu.SemaphoreType.DMA((32,)),
        ],
        compiler_params=pltpu.CompilerParams(
            collective_id=0, has_side_effects=True, vmem_limit_bytes=60 * 1024 * 1024
        ),
        name="h2",
    )(
        near_list.T, local_partner.T, local_count, group_partner, group_count, top_partner.T, top_count,
        right_sides, leaf_basis, near_blocks, local_transfer, local_couple, group_transfer, group_couple,
        top_transfer, jnp.transpose(top_couple, (1, 0, 2)),
    )


def solution(mesh):
    both = ("leaf", "sub")
    placed = (
        P(None, both), P(None, both), P(both, None, None), P(both, None), P(both, None), P(both, None, None),
        P(both, None), P(both), P("leaf", None), P("leaf", None, None), P("leaf", None), P("leaf"),
        P(), P(), P(), P(),
    )
    return jax.shard_map(body, mesh=mesh, in_specs=placed, out_specs=P(None, both), check_vma=False)
```

```python
import functools

import jax
import jax.numpy as jnp
from jax import lax
from jax.experimental import pallas as pl
from jax.experimental.pallas import tpu as pltpu
from jax.sharding import PartitionSpec as P

BF = jnp.bfloat16
F32 = jnp.float32
MESH = pl.DeviceIdType.MESH
TOP_OFF = (0, 32, 48, 56, 60, 62)
S_Q, S_C, S_D, S_U, S_XH, S_TAB, S_GT, N_SEM = 0, 8, 12, 20, 24, 26, 30, 32


def nt(a, b):
    return lax.dot_general(a, b, (((1,), (1,)), ((), ())), preferred_element_type=F32)


def nn(a, b):
    return jnp.dot(a, b, preferred_element_type=F32)


def half_swap(v):
    return pltpu.roll(v, 64, 1)


def iota(shape, dim):
    return lax.broadcasted_iota(jnp.int32, shape, dim)


def kernel(
    near_list_hbm, local_partner_hbm, local_count_hbm, group_partner_hbm, group_count_hbm, top_partner_hbm,
    top_count_hbm, x_hbm, basis_hbm, near_hbm, ltrans_hbm, lcouple_hbm, gtrans_hbm, gcouple_hbm, ttrans_hbm, tcouple_hbm,
    out,
    xs, bs, nb, lt, lc, gt_in, gc, tt, tc,
    es, ge, et, ts, bd, tab, bdt, xbd, pp,
    qb, hr, p1, p3, p4, ub, gu, gt, gs, zb, far, nearp, vht,
    near_list, local_partner, local_count, group_partner, group_count, top_partner, top_count,
    lsem, ssem, rsem, csem,
):
    leaf = lax.axis_index("leaf")
    sub = lax.axis_index("sub")
    col, ylo = lax.div(leaf, 2), lax.rem(leaf, 2)
    z, x = lax.div(col, 4), lax.rem(col, 4)
    member = ylo * 4 + sub
    b = leaf * 4 + sub
    half = lax.div(sub, 2)

    source = member == z

    def column_peer(m):
        return (col * 2 + lax.div(m, 4), lax.rem(m, 4))

    def ring_peer(step):
        n = lax.rem(b + step, 256)
        return (lax.div(n, 4), lax.rem(n, 4))

    col_peers = [column_peer(lax.rem(member + d, 8)) for d in range(8)]
    plane_peers = [(lax.rem(col + d, 32) * 2 + ylo, sub) for d in range(32)]
    plane_sources = [((member * 4 + i) * 2 + ylo, sub) for i in range(4)]
    sub_peers = [(leaf, lax.rem(sub + d, 4)) for d in range(4)]
    after, before = ring_peer(1), ring_peer(255)
    g_after = (lax.rem(leaf + 1, 64), sub)
    g_before = (lax.rem(leaf + 63, 64), sub)

    local = []

    def fetch(src, dst):
        cp = pltpu.make_async_copy(src, dst, lsem.at[len(local)])
        cp.start()
        local.append(cp)
        return cp

    w_x = [fetch(x_hbm.at[:, pl.ds(128 * m, 128)], xs.at[4 + m]) for m in range(8)]
    w_b = [fetch(basis_hbm, bs)]
    w_lt = [fetch(ltrans_hbm, lt)]
    w_gt = [fetch(gtrans_hbm, gt_in)]
    w_tt = [fetch(ttrans_hbm, tt)]
    w_tc = [fetch(tcouple_hbm, tc)]
    w_top = [fetch(top_partner_hbm, top_partner), fetch(top_count_hbm, top_count)]
    w_nb = [fetch(near_hbm, nb), fetch(near_list_hbm, near_list)]
    w_lc = [fetch(lcouple_hbm, lc), fetch(local_partner_hbm, local_partner), fetch(local_count_hbm, local_count)]
    w_gc = [fetch(gcouple_hbm, gc), fetch(group_partner_hbm, group_partner), fetch(group_count_hbm, group_count)]

    def ready(copies):
        for cp in copies:
            cp.wait()

    barrier = pltpu.get_barrier_semaphore()
    def greet(peers):
        for peer in peers:
            pl.semaphore_signal(barrier, inc=1, device_id=peer, device_id_type=MESH)

    greet(col_peers[1:] + [after, before, g_after, g_before])

    @pl.when(source)
    def _():
        greet(plane_peers[1:])

    @pl.when(jnp.logical_not(source))
    def _():
        greet(plane_sources)

    def copy(src, dst, sent, got, peer):
        return pltpu.make_async_remote_copy(
            src_ref=src, dst_ref=dst, send_sem=ssem.at[sent], recv_sem=rsem.at[got],
            device_id=peer, device_id_type=MESH,
        )

    def send(src, dst, place, peer):
        cp = copy(src, dst, place, place, peer)
        cp.start()
        return cp

    lane = iota((1, 128), 1)
    left = lane < 64
    m_left = jnp.where(left, 1.0, 0.0).astype(BF)
    m_right = jnp.where(left, 0.0, 1.0).astype(BF)
    row, column = iota((128, 128), 0), iota((128, 128), 1)
    from_row = lax.div(row, 64) * 64 + 2 * lax.rem(row, 32) + lax.div(lax.rem(row, 64), 32)
    pp[...] = jnp.where(column == from_row, 1.0, 0.0).astype(BF)
    eye = jnp.where(iota((64, 64), 0) == iota((64, 64), 1), 1.0, 0.0).astype(BF)

    def unpack(load):
        parts = []
        for lo in (0, 16):
            tiles = []
            for j in range(lo, lo + 16):
                v = load(j)
                tiles += [v, half_swap(v)]
            parts.append(jnp.swapaxes(jnp.stack(tiles), 0, 1))
        return lambda c: jnp.concatenate([part[c] for part in parts], axis=0).astype(BF)

    def filled(v):
        v = v.astype(F32)
        if v.shape[0] == 8:
            return v
        return jnp.concatenate([v, jnp.zeros((8 - v.shape[0], 128), F32)], axis=0)

    def on_left(v):
        return v * m_left

    def on_right(v):
        return half_swap(v * m_left)

    def on_both(v):
        return on_left(v) + on_right(v)

    ready(w_x)
    ready(w_b)
    for m in range(8):
        two = bs[:, 128 * m : 128 * m + 128]
        both = jnp.concatenate([two * m_left, two * m_right], axis=0)
        bd[m] = both
        tab[16 + m] = nt(xs[4 + m], both).astype(BF)
    ready(w_lt)
    ready(w_gt)

    def upward():
        for lo in range(0, 31, 8):
            hi = min(lo + 8, 31)
            matrix = unpack(lambda j: filled(lt[lo:hi, 128 * j : 128 * j + 128]))
            for c in range(lo, hi):
                right = c < 30 and (c // 2) % 2 == 1
                v = matrix(c - lo)
                es[64 * c : 64 * c + 64, :] = on_right(v) if right else on_left(v)
        matrix = unpack(lambda j: filled(gt_in[:, 128 * j : 128 * j + 128]))
        for c in range(3):
            ge[c] = on_both(matrix(c))
        e_root = es[30 * 64 : 31 * 64, :]
        pair_down = nn(ge[half][:, :64], ge[2]).astype(BF)
        h_root = nn(e_root[:, :64], pair_down).astype(BF)
        hr[...] = h_root
        for lo, hi, n in ((16, 24, 4), (24, 28, 2), (28, 30, 1)):
            for i in range(n):
                kids = jnp.concatenate([tab[lo + 2 * i], tab[lo + 2 * i + 1]], axis=1)
                first = 2 * (lo - 16) + 4 * i
                tab[hi + i] = nn(kids, es[first * 64 : first * 64 + 256, :]).astype(BF)
        c_root = nn(tab[30], es[28 * 64 : 30 * 64, :]).astype(BF)
        tab[31] = c_root
        q = nn(c_root[:, :64], h_root)
        qb[...] = jnp.where(left, q[:32], q[32:]).astype(BF)
        ub[...] = nn(c_root[:, :64], e_root).astype(BF)

    def seen(l, first):
        mine = TOP_OFF[l] + lax.div(col, 2**l)
        total = jnp.zeros((64, 128), F32)
        for k in range(3):
            partner = jnp.where(k < top_count[mine], top_partner[k, mine], -1)
            target = jnp.where(left, first, first + 1)
            total = total + jnp.where(target == partner, gs[3 * l + k], 0.0)
        return total

    def prepare_top():
        wanted = [60 + lax.div(member, 4), 56 + lax.div(member, 2), 48 + member]
        wanted += [32 + 2 * member + i for i in range(2)] + [4 * member + i for i in range(4)]
        wanted += [TOP_OFF[l] + lax.div(col, 2**l) for l in range(5)]

        def pick(rows, n, clusters):
            at = iota((rows, n), 0)
            cluster = at * 0 - 1
            for i, c in enumerate(clusters):
                cluster = jnp.where(at == i, c, cluster)
            return jnp.where(iota((rows, n), 1) == cluster, 1.0, 0.0).astype(BF)

        rows = nn(pick(16, 62, wanted), tt[...])
        for lo in (0, 8):
            matrix = unpack(lambda j: rows[lo : lo + 8, 128 * j : 128 * j + 128])
            for c in range(lo, min(lo + 8, 14)):
                v = matrix(c - lo)
                et[64 * c : 64 * c + 64, :] = on_right(v) if c in (7, 8) else on_left(v) if c < 9 else on_both(v)
        ancestors = pick(8, 63, [TOP_OFF[l] + lax.div(col, 2**l) for l in range(6)])
        for k in range(3):
            rows = nn(ancestors, tc[k])
            matrix = unpack(lambda j: rows[:, 128 * j : 128 * j + 128])
            for l in range(6):
                ts[3 * l + k] = on_both(matrix(l))
        path = None
        for l in range(6):
            for k in range(3):
                s = ts[3 * l + k]
                gs[3 * l + k] = s.astype(F32) if l == 0 else nn(path[:, :64], s)
            if l < 5:
                step = et[(9 + l) * 64 : (10 + l) * 64, :]
                path = step if l == 0 else nn(path[:, :64], step).astype(BF)
        v = seen(5, 62)
        for i, l in enumerate((4, 3, 2)):
            v = nt(v[:, :64].astype(BF), et[64 * i : 64 * i + 64, :64]) + seen(l, wanted[i])[:, :64]
        v = nt(v.astype(BF), et[3 * 64 : 5 * 64, :64]) + seen(1, wanted[3])
        v = nt(v.astype(BF), et[5 * 64 : 9 * 64, :])
        v = v + jnp.concatenate([seen(0, wanted[5]), seen(0, wanted[7])], axis=1)
        zb[...] = v.astype(BF)

    pl.semaphore_wait(barrier, jnp.where(source, 42, 15))
    c_xh = [
        send(xs.at[pl.ds(8, 4)], xs.at[pl.ds(0, 4)], S_XH, after),
        send(xs.at[pl.ds(4, 4)], xs.at[pl.ds(12, 4)], S_XH + 1, before),
    ]
    upward()

    c_q = copy(qb, p1.at[member], S_Q, S_Q + member, column_peer(z))
    leaves_own, upper_own = tab.at[pl.ds(16, 8)], tab.at[pl.ds(24, 8)]
    c_leaves = [
        copy(leaves_own, tab.at[pl.ds(0, 8)], S_TAB, S_TAB, after),
        copy(leaves_own, tab.at[pl.ds(32, 8)], S_TAB + 1, S_TAB + 1, before),
    ]

    @pl.when(jnp.logical_not(source))
    def _():
        c_q.start()

    c_u = [send(ub, gu.at[sub], S_U + d, sub_peers[d]) for d in range(1, 4)]
    gu[sub] = ub[...]

    @pl.when(jnp.logical_not(source))
    def _():
        for cp in c_leaves:
            cp.start()

    ready(w_tt)
    ready(w_tc)
    ready(w_top)
    prepare_top()

    c_c = [
        pltpu.make_async_remote_copy(
            src_ref=p3.at[x], dst_ref=p3.at[x], send_sem=csem.at[d], recv_sem=rsem.at[S_C + x],
            device_id=plane_peers[d], device_id_type=MESH,
        )
        for d in range(1, 32)
    ]

    @pl.when(source)
    def _():
        p1[member] = qb[...]
        for m in range(8):

            @pl.when(member != m)
            def _(m=m):
                copy(qb, p1.at[m], S_Q, S_Q + m, col_peers[1]).wait_recv()

        total = p1[0].astype(F32)
        for m in range(1, 8):
            total = total + p1[m].astype(F32)
        p3[x] = total.astype(BF)
        for cp in c_c + c_leaves:
            cp.start()

    def widen(src, dst, lo, n):
        def step(i, carry):
            for h in range(8):
                at = lo + 8 * i + h
                v = src[at]
                r = half_swap(v)
                dst[2 * at] = jnp.concatenate([v * m_left, r * m_right], axis=0)
                dst[2 * at + 1] = jnp.concatenate([r * m_left, v * m_right], axis=0)
            return carry

        lax.fori_loop(0, n, step, 0)

    def spread(load, n):
        tiles = jnp.swapaxes(jnp.stack([load(j).astype(F32) for j in range(32)]), 0, 1)
        even, odd = [], []
        for k in range(0, n, 2):
            one, two = tiles[k], tiles[k + 1]
            even.append(jnp.where(left, one, half_swap(two)))
            odd.append(jnp.where(left, half_swap(one), two))
        rows = [jnp.concatenate(even, axis=1), jnp.concatenate(odd, axis=1)]
        return jnp.concatenate(rows, axis=0).astype(BF)

    def coupled(table, ids, w):
        pairs = [table[ids[k], 0:64, :] + table[ids[k + 1], 64:128, :] for k in range(0, len(ids), 2)]
        return nt(jnp.concatenate(pairs, axis=1), w)

    def in_order(one, two):
        return nn(jnp.concatenate([one, two], axis=1).astype(BF), pp[...])

    ready(w_nb)
    widen(xs, xbd, 4, 1)
    for cp in c_xh:
        cp.wait_recv()
    for at in (0, 12):
        for h in range(4):
            v = xs[at + h]
            r = half_swap(v)
            xbd[2 * (at + h)] = jnp.concatenate([v * m_left, r * m_right], axis=0)
            xbd[2 * (at + h) + 1] = jnp.concatenate([r * m_left, v * m_right], axis=0)

    def near_step(i, carry):
        weights = []
        for h in range(8):
            t = 8 * i + h
            weights.append(spread(lambda j: nb[t, :, 128 * j : 128 * j + 128], 8))
        parts = []
        for h in range(8):
            ids = [jnp.clip(near_list[k, 8 * i + h] - (b * 16 - 8), 0, 31) for k in range(8)]
            parts.append(coupled(xbd, ids, weights[h]))
        for h in range(4):
            nearp[4 * i + h] = in_order(parts[2 * h], parts[2 * h + 1])
        return carry

    lax.fori_loop(0, 2, near_step, 0)

    c_d = [copy(p4.at[member], p4.at[member], S_D + d, S_D + d, col_peers[d]) for d in range(1, 8)]
    for i in range(4):

        @pl.when(jnp.logical_not(source & (x == i)))
        def _(i=i):
            copy(p3.at[i], p3.at[i], S_C, S_C + i, col_peers[1]).wait_recv()

    have = []
    for i in (0, 2):
        up = p3[i] * m_left + half_swap(p3[i + 1]) * m_right
        down = half_swap(p3[i]) * m_left + p3[i + 1] * m_right
        have.append(jnp.concatenate([up, down], axis=0))
    d = nt(jnp.concatenate(have, axis=1), zb[...])
    p4[member] = jnp.concatenate([d[:32], d[32:]], axis=1).astype(BF)
    for cp in c_d:
        cp.start()

    for cp in c_u:
        cp.wait_recv()
    g0 = (gu[0].astype(F32) + gu[1].astype(F32)).astype(BF)
    g1 = (gu[2].astype(F32) + gu[3].astype(F32)).astype(BF)
    g2 = (nn(g0[:, :64], ge[0]) + nn(g1[:, :64], ge[1])).astype(BF)
    gt[3] = g0 + half_swap(g0)
    gt[4] = g1 + half_swap(g1)
    gt[5] = g2
    gt[9] = jnp.zeros((64, 128), BF)
    c_gt = [
        send(gt.at[pl.ds(3, 3)], gt.at[pl.ds(0, 3)], S_GT, g_after),
        send(gt.at[pl.ds(3, 3)], gt.at[pl.ds(6, 3)], S_GT + 1, g_before),
    ]

    c_upper = [
        send(upper_own, tab.at[pl.ds(8, 8)], S_TAB + 2, after),
        send(upper_own, tab.at[pl.ds(40, 8)], S_TAB + 3, before),
    ]

    ready(w_lc)

    def far_step(i, carry):
        weights = []
        for h in range(8):
            c = jnp.minimum(8 * i + h, 30)
            weights.append(spread(lambda j: lc[c, :, 128 * j : 128 * j + 128], 8))
        parts = []
        for h in range(8):
            c = jnp.minimum(8 * i + h, 30)
            count = jnp.where(8 * i + h < 31, local_count[c], 0)
            ids = []
            for k in range(8):
                e = jnp.clip(local_partner[k, c] - (b - 1) * 31, 0, 92)
                e = e + jnp.where(e >= 31, 1, 0) + jnp.where(e >= 62, 1, 0)
                ids.append(jnp.where(k < count, e, 63))
            parts.append(coupled(bdt, ids, weights[h]))
        for h in range(4):
            far[4 * i + h] = in_order(parts[2 * h], parts[2 * h + 1])
        return carry

    widen(tab, bdt, 16, 2)
    for cp in c_leaves:
        cp.wait_recv()
    widen(tab, bdt, 0, 1)
    widen(tab, bdt, 32, 1)
    lax.fori_loop(0, 2, far_step, 0)

    for cp in c_upper:
        cp.wait_recv()
    widen(tab, bdt, 8, 1)
    widen(tab, bdt, 40, 1)
    lax.fori_loop(2, 4, far_step, 0)

    ready(w_gc)
    for cp in c_gt:
        cp.wait_recv()
    found = []
    for c in range(3):
        w = spread(lambda j: gc[c, :, 128 * j : 128 * j + 128], 4)
        entries = []
        for k in range(4):
            e = jnp.clip(group_partner[c, k] - (leaf - 1) * 3, 0, 8)
            entries.append(gt[jnp.where(k < group_count[c], e, 9)])
        pairs = [entries[k] * m_left + entries[k + 1] * m_right for k in (0, 2)]
        found.append(nt(jnp.concatenate(pairs, axis=1), w))
    f01 = in_order(found[0], found[1])
    f2 = in_order(found[2], found[2])
    f_half = jnp.where(half == 0, f01, half_swap(f01))[:, :64]
    d_half = f_half + nt(f2[:, :64].astype(BF), ge[half][:, :64])

    e_root = es[30 * 64 : 31 * 64, :]
    d_root = far[15][:, :64] + nt(d_half.astype(BF), e_root[:, :64])
    state = jnp.concatenate([d_root, nt(eye, hr[...][:, :64])], axis=0).astype(BF)
    nothing = jnp.zeros((64, 128), F32)

    def with_far(v, i):
        return (v + jnp.concatenate([far[i], nothing], axis=0)).astype(BF)

    states = [with_far(nt(state, es[28 * 64 : 30 * 64, :64]), 14)]
    for first, pair in ((24, 12), (16, 8), (0, 0)):
        lower_level = []
        for i, parents in enumerate(states):
            at = (first + 4 * i) * 64
            both = nt(parents, es[at : at + 256, :])
            lower_level.append(with_far(both[:, :128], pair + 2 * i))
            lower_level.append(with_far(both[:, 128:], pair + 2 * i + 1))
        states = lower_level
    for m in range(8):
        r = nn(states[m], bd[m])
        nearp[m] = nearp[m] + r[:64]
        vht[m] = r[64:].astype(BF)

    for cp in c_d:
        cp.wait_recv()
    total = p4[0].astype(F32)
    for m in range(1, 8):
        total = total + p4[m].astype(F32)
    d_col = jnp.concatenate([total[:, :64], total[:, 64:]], axis=0).astype(BF)
    for m in range(8):
        out[:, 128 * m : 128 * m + 128] = nearp[m] + nn(d_col, vht[m])

    for cp in c_u + c_xh + c_leaves + c_upper + c_gt + c_d:
        cp.wait_send()

    @pl.when(source)
    def _():
        for cp in c_c:
            cp.wait_send()

    @pl.when(jnp.logical_not(source))
    def _():
        c_q.wait_send()


def body(
    right_sides, leaf_basis, near_blocks, near_list, local_transfer, local_couple, local_partner, local_count,
    group_transfer, group_couple, group_partner, group_count, top_transfer, top_couple, top_partner, top_count,
):
    hbm = pl.BlockSpec(memory_space=pltpu.HBM)
    vm = pltpu.VMEM
    return pl.pallas_call(
        kernel,
        out_shape=jax.ShapeDtypeStruct((64, 1024), F32),
        in_specs=[hbm] * 16,
        out_specs=pl.BlockSpec(memory_space=pltpu.VMEM),
        scratch_shapes=[
            vm((16, 64, 128), BF),
            vm((64, 1024), BF),
            vm((16, 8, 4096), BF),
            vm((31, 4096), BF),
            vm((31, 8, 4096), BF),
            vm((3, 4096), BF),
            vm((3, 4, 4096), BF),
            vm((62, 4096), BF),
            vm((3, 63, 4096), BF),
            vm((31 * 64, 128), BF),
            vm((3, 64, 128), BF),
            vm((16 * 64, 128), BF),
            vm((18, 64, 128), BF),
            vm((8, 128, 128), BF),
            vm((48, 64, 128), BF),
            vm((96, 128, 128), BF),
            vm((32, 128, 128), BF),
            vm((128, 128), BF),
            vm((32, 128), BF),
            vm((64, 128), BF),
            vm((8, 32, 128), BF),
            vm((4, 32, 128), BF),
            vm((8, 32, 128), BF),
            vm((64, 128), BF),
            vm((4, 64, 128), BF),
            vm((10, 64, 128), BF),
            vm((18, 64, 128), F32),
            vm((64, 256), BF),
            vm((16, 64, 128), F32),
            vm((8, 64, 128), F32),
            vm((8, 64, 128), BF),
            pltpu.SMEM((8, 16), jnp.int32),
            pltpu.SMEM((8, 31), jnp.int32),
            pltpu.SMEM((31,), jnp.int32),
            pltpu.SMEM((3, 4), jnp.int32),
            pltpu.SMEM((3,), jnp.int32),
            pltpu.SMEM((3, 63), jnp.int32),
            pltpu.SMEM((63,), jnp.int32),
            pltpu.SemaphoreType.DMA((24,)),
            pltpu.SemaphoreType.DMA((N_SEM,)),
            pltpu.SemaphoreType.DMA((N_SEM,)),
            pltpu.SemaphoreType.DMA((32,)),
        ],
        compiler_params=pltpu.CompilerParams(
            collective_id=0, has_side_effects=True, vmem_limit_bytes=60 * 1024 * 1024
        ),
        name="h2",
    )(
        near_list.T, local_partner.T, local_count, group_partner, group_count, top_partner.T, top_count,
        right_sides, leaf_basis, near_blocks, local_transfer, local_couple, group_transfer, group_couple,
        top_transfer, jnp.transpose(top_couple, (1, 0, 2)),
    )


def solution(mesh):
    both = ("leaf", "sub")
    placed = (
        P(None, both), P(None, both), P(both, None, None), P(both, None), P(both, None), P(both, None, None),
        P(both, None), P(both), P("leaf", None), P("leaf", None, None), P("leaf", None), P("leaf"),
        P(), P(), P(), P(),
    )
    return jax.shard_map(body, mesh=mesh, in_specs=placed, out_specs=P(None, both), check_vma=False)
```

```python
import functools

import jax
import jax.numpy as jnp
from jax import lax
from jax.experimental import pallas as pl
from jax.experimental.pallas import tpu as pltpu
from jax.sharding import PartitionSpec as P

BF = jnp.bfloat16
F32 = jnp.float32
MESH = pl.DeviceIdType.MESH
TOP_OFF = (0, 32, 48, 56, 60, 62)
S_Q, S_C, S_D, S_U, S_XH, S_TAB, S_GT, N_SEM = 0, 8, 12, 20, 24, 26, 30, 32


def nt(a, b):
    return lax.dot_general(a, b, (((1,), (1,)), ((), ())), preferred_element_type=F32)


def nn(a, b):
    return jnp.dot(a, b, preferred_element_type=F32)


def half_swap(v):
    return pltpu.roll(v, 64, 1)


def iota(shape, dim):
    return lax.broadcasted_iota(jnp.int32, shape, dim)


def kernel(
    near_list_hbm, local_partner_hbm, local_count_hbm, group_partner_hbm, group_count_hbm, top_partner_hbm,
    top_count_hbm, x_hbm, basis_hbm, near_hbm, ltrans_hbm, lcouple_hbm, gtrans_hbm, gcouple_hbm, ttrans_hbm, tcouple_hbm,
    out,
    xs, bs, nb, lt, lc, gt_in, gc, tt, tc,
    es, ge, et, ts, bd, tab, bdt, xbd, pp,
    qb, hr, p1, p3, p4, ub, gu, gt, gs, zb, far, nearp, vht,
    near_list, local_partner, local_count, group_partner, group_count, top_partner, top_count,
    lsem, ssem, rsem, csem,
):
    leaf = lax.axis_index("leaf")
    sub = lax.axis_index("sub")
    col, ylo = lax.div(leaf, 2), lax.rem(leaf, 2)
    z, x = lax.div(col, 4), lax.rem(col, 4)
    member = ylo * 4 + sub
    b = leaf * 4 + sub
    half = lax.div(sub, 2)

    source = member == z

    def column_peer(m):
        return (col * 2 + lax.div(m, 4), lax.rem(m, 4))

    def ring_peer(step):
        n = lax.rem(b + step, 256)
        return (lax.div(n, 4), lax.rem(n, 4))

    col_peers = [column_peer(lax.rem(member + d, 8)) for d in range(8)]
    plane_peers = [(lax.rem(col + d, 32) * 2 + ylo, sub) for d in range(32)]
    plane_sources = [((member * 4 + i) * 2 + ylo, sub) for i in range(4)]
    sub_peers = [(leaf, lax.rem(sub + d, 4)) for d in range(4)]
    after, before = ring_peer(1), ring_peer(255)
    g_after = (lax.rem(leaf + 1, 64), sub)
    g_before = (lax.rem(leaf + 63, 64), sub)

    local = []

    def fetch(src, dst):
        cp = pltpu.make_async_copy(src, dst, lsem.at[len(local)])
        cp.start()
        local.append(cp)
        return cp

    w_x = [fetch(x_hbm.at[:, pl.ds(128 * m, 128)], xs.at[4 + m]) for m in range(8)]
    w_b = [fetch(basis_hbm, bs)]
    w_lt = [fetch(ltrans_hbm, lt)]
    w_gt = [fetch(gtrans_hbm, gt_in)]
    w_tt = [fetch(ttrans_hbm, tt)]
    w_tc = [fetch(tcouple_hbm, tc)]
    w_top = [fetch(top_partner_hbm, top_partner), fetch(top_count_hbm, top_count)]
    w_nb = [fetch(near_hbm, nb), fetch(near_list_hbm, near_list)]
    w_lc = [fetch(lcouple_hbm, lc), fetch(local_partner_hbm, local_partner), fetch(local_count_hbm, local_count)]
    w_gc = [fetch(gcouple_hbm, gc), fetch(group_partner_hbm, group_partner), fetch(group_count_hbm, group_count)]

    def ready(copies):
        for cp in copies:
            cp.wait()

    barrier = pltpu.get_barrier_semaphore()
    def greet(peers):
        for peer in peers:
            pl.semaphore_signal(barrier, inc=1, device_id=peer, device_id_type=MESH)

    greet(col_peers[1:] + [after, before, g_after, g_before])

    @pl.when(source)
    def _():
        greet(plane_peers[1:])

    @pl.when(jnp.logical_not(source))
    def _():
        greet(plane_sources)

    def copy(src, dst, sent, got, peer):
        return pltpu.make_async_remote_copy(
            src_ref=src, dst_ref=dst, send_sem=ssem.at[sent], recv_sem=rsem.at[got],
            device_id=peer, device_id_type=MESH,
        )

    def send(src, dst, place, peer):
        cp = copy(src, dst, place, place, peer)
        cp.start()
        return cp

    lane = iota((1, 128), 1)
    left = lane < 64
    m_left = jnp.where(left, 1.0, 0.0).astype(BF)
    m_right = jnp.where(left, 0.0, 1.0).astype(BF)
    row, column = iota((128, 128), 0), iota((128, 128), 1)
    from_row = lax.div(row, 64) * 64 + 2 * lax.rem(row, 32) + lax.div(lax.rem(row, 64), 32)
    pp[...] = jnp.where(column == from_row, 1.0, 0.0).astype(BF)
    eye = jnp.where(iota((64, 64), 0) == iota((64, 64), 1), 1.0, 0.0).astype(BF)

    def unpack(load):
        parts = []
        for lo in (0, 16):
            tiles = []
            for j in range(lo, lo + 16):
                v = load(j)
                tiles += [v, half_swap(v)]
            parts.append(jnp.swapaxes(jnp.stack(tiles), 0, 1))
        return lambda c: jnp.concatenate([part[c] for part in parts], axis=0).astype(BF)

    def filled(v):
        v = v.astype(F32)
        if v.shape[0] == 8:
            return v
        return jnp.concatenate([v, jnp.zeros((8 - v.shape[0], 128), F32)], axis=0)

    def on_left(v):
        return v * m_left

    def on_right(v):
        return half_swap(v * m_left)

    def on_both(v):
        return on_left(v) + on_right(v)

    ready(w_x)
    ready(w_b)
    for m in range(8):
        two = bs[:, 128 * m : 128 * m + 128]
        both = jnp.concatenate([two * m_left, two * m_right], axis=0)
        bd[m] = both
        tab[16 + m] = nt(xs[4 + m], both).astype(BF)
    ready(w_lt)
    ready(w_gt)

    def upward():
        for lo in range(0, 31, 8):
            hi = min(lo + 8, 31)
            matrix = unpack(lambda j: filled(lt[lo:hi, 128 * j : 128 * j + 128]))
            for c in range(lo, hi):
                right = c < 30 and (c // 2) % 2 == 1
                v = matrix(c - lo)
                es[64 * c : 64 * c + 64, :] = on_right(v) if right else on_left(v)
        matrix = unpack(lambda j: filled(gt_in[:, 128 * j : 128 * j + 128]))
        for c in range(3):
            ge[c] = on_both(matrix(c))
        e_root = es[30 * 64 : 31 * 64, :]
        pair_down = nn(ge[half][:, :64], ge[2]).astype(BF)
        h_root = nn(e_root[:, :64], pair_down).astype(BF)
        hr[...] = h_root
        for lo, hi, n in ((16, 24, 4), (24, 28, 2), (28, 30, 1)):
            for i in range(n):
                kids = jnp.concatenate([tab[lo + 2 * i], tab[lo + 2 * i + 1]], axis=1)
                first = 2 * (lo - 16) + 4 * i
                tab[hi + i] = nn(kids, es[first * 64 : first * 64 + 256, :]).astype(BF)
        c_root = nn(tab[30], es[28 * 64 : 30 * 64, :]).astype(BF)
        tab[31] = c_root
        q = nn(c_root[:, :64], h_root)
        qb[...] = jnp.where(left, q[:32], q[32:]).astype(BF)
        ub[...] = nn(c_root[:, :64], e_root).astype(BF)

    def seen(l, first):
        mine = TOP_OFF[l] + lax.div(col, 2**l)
        total = jnp.zeros((64, 128), F32)
        for k in range(3):
            partner = jnp.where(k < top_count[mine], top_partner[k, mine], -1)
            target = jnp.where(left, first, first + 1)
            total = total + jnp.where(target == partner, gs[3 * l + k], 0.0)
        return total

    def prepare_top():
        wanted = [60 + lax.div(member, 4), 56 + lax.div(member, 2), 48 + member]
        wanted += [32 + 2 * member + i for i in range(2)] + [4 * member + i for i in range(4)]
        wanted += [TOP_OFF[l] + lax.div(col, 2**l) for l in range(5)]

        def pick(rows, n, clusters):
            at = iota((rows, n), 0)
            cluster = at * 0 - 1
            for i, c in enumerate(clusters):
                cluster = jnp.where(at == i, c, cluster)
            return jnp.where(iota((rows, n), 1) == cluster, 1.0, 0.0).astype(BF)

        rows = nn(pick(16, 62, wanted), tt[...])
        for lo in (0, 8):
            matrix = unpack(lambda j: rows[lo : lo + 8, 128 * j : 128 * j + 128])
            for c in range(lo, min(lo + 8, 14)):
                v = matrix(c - lo)
                et[64 * c : 64 * c + 64, :] = on_right(v) if c in (7, 8) else on_left(v) if c < 9 else on_both(v)
        ancestors = pick(8, 63, [TOP_OFF[l] + lax.div(col, 2**l) for l in range(6)])
        for k in range(3):
            rows = nn(ancestors, tc[k])
            matrix = unpack(lambda j: rows[:, 128 * j : 128 * j + 128])
            for l in range(6):
                ts[3 * l + k] = on_both(matrix(l))
        path = None
        for l in range(6):
            for k in range(3):
                s = ts[3 * l + k]
                gs[3 * l + k] = s.astype(F32) if l == 0 else nn(path[:, :64], s)
            if l < 5:
                step = et[(9 + l) * 64 : (10 + l) * 64, :]
                path = step if l == 0 else nn(path[:, :64], step).astype(BF)
        v = seen(5, 62)
        for i, l in enumerate((4, 3, 2)):
            v = nt(v[:, :64].astype(BF), et[64 * i : 64 * i + 64, :64]) + seen(l, wanted[i])[:, :64]
        v = nt(v.astype(BF), et[3 * 64 : 5 * 64, :64]) + seen(1, wanted[3])
        v = nt(v.astype(BF), et[5 * 64 : 9 * 64, :])
        v = v + jnp.concatenate([seen(0, wanted[5]), seen(0, wanted[7])], axis=1)
        zb[...] = v.astype(BF)

    pl.semaphore_wait(barrier, jnp.where(source, 42, 15))
    c_xh = [
        send(xs.at[pl.ds(8, 4)], xs.at[pl.ds(0, 4)], S_XH, after),
        send(xs.at[pl.ds(4, 4)], xs.at[pl.ds(12, 4)], S_XH + 1, before),
    ]
    leaves_own, upper_own = tab.at[pl.ds(16, 8)], tab.at[pl.ds(24, 8)]
    c_leaves = [
        send(leaves_own, tab.at[pl.ds(0, 8)], S_TAB, after),
        send(leaves_own, tab.at[pl.ds(32, 8)], S_TAB + 1, before),
    ]
    upward()

    c_q = copy(qb, p1.at[member], S_Q, S_Q + member, column_peer(z))
    c_upper = [
        copy(upper_own, tab.at[pl.ds(8, 8)], S_TAB + 2, S_TAB + 2, after),
        copy(upper_own, tab.at[pl.ds(40, 8)], S_TAB + 3, S_TAB + 3, before),
    ]

    @pl.when(jnp.logical_not(source))
    def _():
        c_q.start()

    c_u = [send(ub, gu.at[sub], S_U + d, sub_peers[d]) for d in range(1, 4)]
    gu[sub] = ub[...]

    @pl.when(jnp.logical_not(source))
    def _():
        for cp in c_upper:
            cp.start()

    ready(w_tt)
    ready(w_tc)
    ready(w_top)
    prepare_top()

    c_c = [
        pltpu.make_async_remote_copy(
            src_ref=p3.at[x], dst_ref=p3.at[x], send_sem=csem.at[d], recv_sem=rsem.at[S_C + x],
            device_id=plane_peers[d], device_id_type=MESH,
        )
        for d in range(1, 32)
    ]

    @pl.when(source)
    def _():
        p1[member] = qb[...]
        for m in range(8):

            @pl.when(member != m)
            def _(m=m):
                copy(qb, p1.at[m], S_Q, S_Q + m, col_peers[1]).wait_recv()

        total = p1[0].astype(F32)
        for m in range(1, 8):
            total = total + p1[m].astype(F32)
        p3[x] = total.astype(BF)
        for cp in c_c + c_upper:
            cp.start()

    def widen(src, dst, lo, n):
        def step(i, carry):
            for h in range(8):
                at = lo + 8 * i + h
                v = src[at]
                r = half_swap(v)
                dst[2 * at] = jnp.concatenate([v * m_left, r * m_right], axis=0)
                dst[2 * at + 1] = jnp.concatenate([r * m_left, v * m_right], axis=0)
            return carry

        lax.fori_loop(0, n, step, 0)

    def spread(load, n):
        tiles = jnp.swapaxes(jnp.stack([load(j).astype(F32) for j in range(32)]), 0, 1)
        even, odd = [], []
        for k in range(0, n, 2):
            one, two = tiles[k], tiles[k + 1]
            even.append(jnp.where(left, one, half_swap(two)))
            odd.append(jnp.where(left, half_swap(one), two))
        rows = [jnp.concatenate(even, axis=1), jnp.concatenate(odd, axis=1)]
        return jnp.concatenate(rows, axis=0).astype(BF)

    def coupled(table, ids, w):
        pairs = [table[ids[k], 0:64, :] + table[ids[k + 1], 64:128, :] for k in range(0, len(ids), 2)]
        return nt(jnp.concatenate(pairs, axis=1), w)

    def in_order(one, two):
        return nn(jnp.concatenate([one, two], axis=1).astype(BF), pp[...])

    ready(w_nb)
    widen(xs, xbd, 4, 1)
    for cp in c_xh:
        cp.wait_recv()
    for at in (0, 12):
        for h in range(4):
            v = xs[at + h]
            r = half_swap(v)
            xbd[2 * (at + h)] = jnp.concatenate([v * m_left, r * m_right], axis=0)
            xbd[2 * (at + h) + 1] = jnp.concatenate([r * m_left, v * m_right], axis=0)

    def near_step(i, carry):
        weights = []
        for h in range(8):
            t = 8 * i + h
            weights.append(spread(lambda j: nb[t, :, 128 * j : 128 * j + 128], 8))
        parts = []
        for h in range(8):
            ids = [jnp.clip(near_list[k, 8 * i + h] - (b * 16 - 8), 0, 31) for k in range(8)]
            parts.append(coupled(xbd, ids, weights[h]))
        for h in range(4):
            nearp[4 * i + h] = in_order(parts[2 * h], parts[2 * h + 1])
        return carry

    lax.fori_loop(0, 2, near_step, 0)

    c_d = [copy(p4.at[member], p4.at[member], S_D + d, S_D + d, col_peers[d]) for d in range(1, 8)]
    for i in range(4):

        @pl.when(jnp.logical_not(source & (x == i)))
        def _(i=i):
            copy(p3.at[i], p3.at[i], S_C, S_C + i, col_peers[1]).wait_recv()

    have = []
    for i in (0, 2):
        up = p3[i] * m_left + half_swap(p3[i + 1]) * m_right
        down = half_swap(p3[i]) * m_left + p3[i + 1] * m_right
        have.append(jnp.concatenate([up, down], axis=0))
    d = nt(jnp.concatenate(have, axis=1), zb[...])
    p4[member] = jnp.concatenate([d[:32], d[32:]], axis=1).astype(BF)
    for cp in c_d:
        cp.start()

    for cp in c_u:
        cp.wait_recv()
    g0 = (gu[0].astype(F32) + gu[1].astype(F32)).astype(BF)
    g1 = (gu[2].astype(F32) + gu[3].astype(F32)).astype(BF)
    g2 = (nn(g0[:, :64], ge[0]) + nn(g1[:, :64], ge[1])).astype(BF)
    gt[3] = g0 + half_swap(g0)
    gt[4] = g1 + half_swap(g1)
    gt[5] = g2
    gt[9] = jnp.zeros((64, 128), BF)
    c_gt = [
        send(gt.at[pl.ds(3, 3)], gt.at[pl.ds(0, 3)], S_GT, g_after),
        send(gt.at[pl.ds(3, 3)], gt.at[pl.ds(6, 3)], S_GT + 1, g_before),
    ]

    ready(w_lc)

    def far_step(i, carry):
        weights = []
        for h in range(8):
            c = jnp.minimum(8 * i + h, 30)
            weights.append(spread(lambda j: lc[c, :, 128 * j : 128 * j + 128], 8))
        parts = []
        for h in range(8):
            c = jnp.minimum(8 * i + h, 30)
            count = jnp.where(8 * i + h < 31, local_count[c], 0)
            ids = []
            for k in range(8):
                e = jnp.clip(local_partner[k, c] - (b - 1) * 31, 0, 92)
                e = e + jnp.where(e >= 31, 1, 0) + jnp.where(e >= 62, 1, 0)
                ids.append(jnp.where(k < count, e, 63))
            parts.append(coupled(bdt, ids, weights[h]))
        for h in range(4):
            far[4 * i + h] = in_order(parts[2 * h], parts[2 * h + 1])
        return carry

    widen(tab, bdt, 16, 2)
    for cp in c_leaves:
        cp.wait_recv()
    widen(tab, bdt, 0, 1)
    widen(tab, bdt, 32, 1)
    lax.fori_loop(0, 2, far_step, 0)

    ready(w_gc)
    for cp in c_gt:
        cp.wait_recv()
    found = []
    for c in range(3):
        w = spread(lambda j: gc[c, :, 128 * j : 128 * j + 128], 4)
        entries = []
        for k in range(4):
            e = jnp.clip(group_partner[c, k] - (leaf - 1) * 3, 0, 8)
            entries.append(gt[jnp.where(k < group_count[c], e, 9)])
        pairs = [entries[k] * m_left + entries[k + 1] * m_right for k in (0, 2)]
        found.append(nt(jnp.concatenate(pairs, axis=1), w))
    f01 = in_order(found[0], found[1])
    f2 = in_order(found[2], found[2])
    f_half = jnp.where(half == 0, f01, half_swap(f01))[:, :64]
    d_half = f_half + nt(f2[:, :64].astype(BF), ge[half][:, :64])

    for cp in c_upper:
        cp.wait_recv()
    widen(tab, bdt, 8, 1)
    widen(tab, bdt, 40, 1)
    lax.fori_loop(2, 4, far_step, 0)

    e_root = es[30 * 64 : 31 * 64, :]
    d_root = far[15][:, :64] + nt(d_half.astype(BF), e_root[:, :64])
    state = jnp.concatenate([d_root, nt(eye, hr[...][:, :64])], axis=0).astype(BF)
    nothing = jnp.zeros((64, 128), F32)

    def with_far(v, i):
        return (v + jnp.concatenate([far[i], nothing], axis=0)).astype(BF)

    states = [with_far(nt(state, es[28 * 64 : 30 * 64, :64]), 14)]
    for first, pair in ((24, 12), (16, 8), (0, 0)):
        lower_level = []
        for i, parents in enumerate(states):
            at = (first + 4 * i) * 64
            both = nt(parents, es[at : at + 256, :])
            lower_level.append(with_far(both[:, :128], pair + 2 * i))
            lower_level.append(with_far(both[:, 128:], pair + 2 * i + 1))
        states = lower_level
    for m in range(8):
        r = nn(states[m], bd[m])
        nearp[m] = nearp[m] + r[:64]
        vht[m] = r[64:].astype(BF)

    for cp in c_d:
        cp.wait_recv()
    total = p4[0].astype(F32)
    for m in range(1, 8):
        total = total + p4[m].astype(F32)
    d_col = jnp.concatenate([total[:, :64], total[:, 64:]], axis=0).astype(BF)
    for m in range(8):
        out[:, 128 * m : 128 * m + 128] = nearp[m] + nn(d_col, vht[m])

    for cp in c_u + c_xh + c_leaves + c_upper + c_gt + c_d:
        cp.wait_send()

    @pl.when(source)
    def _():
        for cp in c_c:
            cp.wait_send()

    @pl.when(jnp.logical_not(source))
    def _():
        c_q.wait_send()


def body(
    right_sides, leaf_basis, near_blocks, near_list, local_transfer, local_couple, local_partner, local_count,
    group_transfer, group_couple, group_partner, group_count, top_transfer, top_couple, top_partner, top_count,
):
    hbm = pl.BlockSpec(memory_space=pltpu.HBM)
    vm = pltpu.VMEM
    return pl.pallas_call(
        kernel,
        out_shape=jax.ShapeDtypeStruct((64, 1024), F32),
        in_specs=[hbm] * 16,
        out_specs=pl.BlockSpec(memory_space=pltpu.VMEM),
        scratch_shapes=[
            vm((16, 64, 128), BF),
            vm((64, 1024), BF),
            vm((16, 8, 4096), BF),
            vm((31, 4096), BF),
            vm((31, 8, 4096), BF),
            vm((3, 4096), BF),
            vm((3, 4, 4096), BF),
            vm((62, 4096), BF),
            vm((3, 63, 4096), BF),
            vm((31 * 64, 128), BF),
            vm((3, 64, 128), BF),
            vm((16 * 64, 128), BF),
            vm((18, 64, 128), BF),
            vm((8, 128, 128), BF),
            vm((48, 64, 128), BF),
            vm((96, 128, 128), BF),
            vm((32, 128, 128), BF),
            vm((128, 128), BF),
            vm((32, 128), BF),
            vm((64, 128), BF),
            vm((8, 32, 128), BF),
            vm((4, 32, 128), BF),
            vm((8, 32, 128), BF),
            vm((64, 128), BF),
            vm((4, 64, 128), BF),
            vm((10, 64, 128), BF),
            vm((18, 64, 128), F32),
            vm((64, 256), BF),
            vm((16, 64, 128), F32),
            vm((8, 64, 128), F32),
            vm((8, 64, 128), BF),
            pltpu.SMEM((8, 16), jnp.int32),
            pltpu.SMEM((8, 31), jnp.int32),
            pltpu.SMEM((31,), jnp.int32),
            pltpu.SMEM((3, 4), jnp.int32),
            pltpu.SMEM((3,), jnp.int32),
            pltpu.SMEM((3, 63), jnp.int32),
            pltpu.SMEM((63,), jnp.int32),
            pltpu.SemaphoreType.DMA((24,)),
            pltpu.SemaphoreType.DMA((N_SEM,)),
            pltpu.SemaphoreType.DMA((N_SEM,)),
            pltpu.SemaphoreType.DMA((32,)),
        ],
        compiler_params=pltpu.CompilerParams(
            collective_id=0, has_side_effects=True, vmem_limit_bytes=60 * 1024 * 1024
        ),
        name="h2",
    )(
        near_list.T, local_partner.T, local_count, group_partner, group_count, top_partner.T, top_count,
        right_sides, leaf_basis, near_blocks, local_transfer, local_couple, group_transfer, group_couple,
        top_transfer, jnp.transpose(top_couple, (1, 0, 2)),
    )


def solution(mesh):
    both = ("leaf", "sub")
    placed = (
        P(None, both), P(None, both), P(both, None, None), P(both, None), P(both, None), P(both, None, None),
        P(both, None), P(both), P("leaf", None), P("leaf", None, None), P("leaf", None), P("leaf"),
        P(), P(), P(), P(),
    )
    return jax.shard_map(body, mesh=mesh, in_specs=placed, out_specs=P(None, both), check_vma=False)
```

```python
import functools

import jax
import jax.numpy as jnp
from jax import lax
from jax.experimental import pallas as pl
from jax.experimental.pallas import tpu as pltpu
from jax.sharding import PartitionSpec as P

BF = jnp.bfloat16
F32 = jnp.float32
MESH = pl.DeviceIdType.MESH
TOP_OFF = (0, 32, 48, 56, 60, 62)
S_Q, S_C, S_D, S_U, S_XH, S_TAB, S_GT, N_SEM = 0, 8, 12, 20, 24, 26, 30, 32


def nt(a, b):
    return lax.dot_general(a, b, (((1,), (1,)), ((), ())), preferred_element_type=F32)


def nn(a, b):
    return jnp.dot(a, b, preferred_element_type=F32)


def half_swap(v):
    return pltpu.roll(v, 64, 1)


def iota(shape, dim):
    return lax.broadcasted_iota(jnp.int32, shape, dim)


def kernel(
    near_list_hbm, local_partner_hbm, local_count_hbm, group_partner_hbm, group_count_hbm, top_partner_hbm,
    top_count_hbm, x_hbm, basis_hbm, near_hbm, ltrans_hbm, lcouple_hbm, gtrans_hbm, gcouple_hbm, ttrans_hbm, tcouple_hbm,
    out,
    xs, bs, nb, lt, lc, gt_in, gc, tt, tc,
    es, ge, et, ts, wf, bd, tab, bdt, xbd, pp,
    qb, hr, p1, p3, p4, ub, gu, gt, gs, zb, far, nearp, vht,
    near_list, local_partner, local_count, group_partner, group_count, top_partner, top_count,
    lsem, ssem, rsem, csem,
):
    leaf = lax.axis_index("leaf")
    sub = lax.axis_index("sub")
    col, ylo = lax.div(leaf, 2), lax.rem(leaf, 2)
    z, x = lax.div(col, 4), lax.rem(col, 4)
    member = ylo * 4 + sub
    b = leaf * 4 + sub
    half = lax.div(sub, 2)

    source = member == z

    def column_peer(m):
        return (col * 2 + lax.div(m, 4), lax.rem(m, 4))

    def ring_peer(step):
        n = lax.rem(b + step, 256)
        return (lax.div(n, 4), lax.rem(n, 4))

    col_peers = [column_peer(lax.rem(member + d, 8)) for d in range(8)]
    plane_peers = [(lax.rem(col + d, 32) * 2 + ylo, sub) for d in range(32)]
    plane_sources = [((member * 4 + i) * 2 + ylo, sub) for i in range(4)]
    sub_peers = [(leaf, lax.rem(sub + d, 4)) for d in range(4)]
    after, before = ring_peer(1), ring_peer(255)
    g_after = (lax.rem(leaf + 1, 64), sub)
    g_before = (lax.rem(leaf + 63, 64), sub)

    local = []

    def fetch(src, dst):
        cp = pltpu.make_async_copy(src, dst, lsem.at[len(local)])
        cp.start()
        local.append(cp)
        return cp

    w_x = [fetch(x_hbm.at[:, pl.ds(128 * m, 128)], xs.at[4 + m]) for m in range(8)]
    w_b = [fetch(basis_hbm, bs)]
    w_lt = [fetch(ltrans_hbm, lt)]
    w_gt = [fetch(gtrans_hbm, gt_in)]
    w_tt = [fetch(ttrans_hbm, tt)]
    w_tc = [fetch(tcouple_hbm, tc)]
    w_top = [fetch(top_partner_hbm, top_partner), fetch(top_count_hbm, top_count)]
    w_nb = [fetch(near_hbm, nb), fetch(near_list_hbm, near_list)]
    w_lc = [fetch(lcouple_hbm, lc), fetch(local_partner_hbm, local_partner), fetch(local_count_hbm, local_count)]
    w_gc = [fetch(gcouple_hbm, gc), fetch(group_partner_hbm, group_partner), fetch(group_count_hbm, group_count)]

    def ready(copies):
        for cp in copies:
            cp.wait()

    barrier = pltpu.get_barrier_semaphore()
    def greet(peers):
        for peer in peers:
            pl.semaphore_signal(barrier, inc=1, device_id=peer, device_id_type=MESH)

    greet(col_peers[1:] + [after, before, g_after, g_before])

    @pl.when(source)
    def _():
        greet(plane_peers[1:])

    @pl.when(jnp.logical_not(source))
    def _():
        greet(plane_sources)

    def copy(src, dst, sent, got, peer):
        return pltpu.make_async_remote_copy(
            src_ref=src, dst_ref=dst, send_sem=ssem.at[sent], recv_sem=rsem.at[got],
            device_id=peer, device_id_type=MESH,
        )

    def send(src, dst, place, peer):
        cp = copy(src, dst, place, place, peer)
        cp.start()
        return cp

    lane = iota((1, 128), 1)
    left = lane < 64
    m_left = jnp.where(left, 1.0, 0.0).astype(BF)
    m_right = jnp.where(left, 0.0, 1.0).astype(BF)
    row, column = iota((128, 128), 0), iota((128, 128), 1)
    from_row = lax.div(row, 64) * 64 + 2 * lax.rem(row, 32) + lax.div(lax.rem(row, 64), 32)
    pp[...] = jnp.where(column == from_row, 1.0, 0.0).astype(BF)
    eye = jnp.where(iota((64, 64), 0) == iota((64, 64), 1), 1.0, 0.0).astype(BF)

    def unpack(load):
        parts = []
        for lo in (0, 16):
            tiles = []
            for j in range(lo, lo + 16):
                v = load(j)
                tiles += [v, half_swap(v)]
            parts.append(jnp.swapaxes(jnp.stack(tiles), 0, 1))
        return lambda c: jnp.concatenate([part[c] for part in parts], axis=0).astype(BF)

    def filled(v):
        v = v.astype(F32)
        if v.shape[0] == 8:
            return v
        return jnp.concatenate([v, jnp.zeros((8 - v.shape[0], 128), F32)], axis=0)

    def on_left(v):
        return v * m_left

    def on_right(v):
        return half_swap(v * m_left)

    def on_both(v):
        return on_left(v) + on_right(v)

    ready(w_x)
    ready(w_b)
    for m in range(8):
        two = bs[:, 128 * m : 128 * m + 128]
        both = jnp.concatenate([two * m_left, two * m_right], axis=0)
        bd[m] = both
        tab[16 + m] = nt(xs[4 + m], both).astype(BF)
    ready(w_lt)
    ready(w_gt)

    def upward():
        for lo in range(0, 31, 8):
            hi = min(lo + 8, 31)
            matrix = unpack(lambda j: filled(lt[lo:hi, 128 * j : 128 * j + 128]))
            for c in range(lo, hi):
                right = c < 30 and (c // 2) % 2 == 1
                v = matrix(c - lo)
                es[64 * c : 64 * c + 64, :] = on_right(v) if right else on_left(v)
        matrix = unpack(lambda j: filled(gt_in[:, 128 * j : 128 * j + 128]))
        for c in range(3):
            ge[c] = on_both(matrix(c))
        e_root = es[30 * 64 : 31 * 64, :]
        pair_down = nn(ge[half][:, :64], ge[2]).astype(BF)
        h_root = nn(e_root[:, :64], pair_down).astype(BF)
        hr[...] = h_root
        for lo, hi, n in ((16, 24, 4), (24, 28, 2), (28, 30, 1)):
            for i in range(n):
                kids = jnp.concatenate([tab[lo + 2 * i], tab[lo + 2 * i + 1]], axis=1)
                first = 2 * (lo - 16) + 4 * i
                tab[hi + i] = nn(kids, es[first * 64 : first * 64 + 256, :]).astype(BF)
        c_root = nn(tab[30], es[28 * 64 : 30 * 64, :]).astype(BF)
        tab[31] = c_root
        q = nn(c_root[:, :64], h_root)
        qb[...] = jnp.where(left, q[:32], q[32:]).astype(BF)
        ub[...] = nn(c_root[:, :64], e_root).astype(BF)

    def seen(l, first):
        mine = TOP_OFF[l] + lax.div(col, 2**l)
        total = jnp.zeros((64, 128), F32)
        for k in range(3):
            partner = jnp.where(k < top_count[mine], top_partner[k, mine], -1)
            target = jnp.where(left, first, first + 1)
            total = total + jnp.where(target == partner, gs[3 * l + k], 0.0)
        return total

    def prepare_top():
        wanted = [60 + lax.div(member, 4), 56 + lax.div(member, 2), 48 + member]
        wanted += [32 + 2 * member + i for i in range(2)] + [4 * member + i for i in range(4)]
        wanted += [TOP_OFF[l] + lax.div(col, 2**l) for l in range(5)]

        def pick(rows, n, clusters):
            at = iota((rows, n), 0)
            cluster = at * 0 - 1
            for i, c in enumerate(clusters):
                cluster = jnp.where(at == i, c, cluster)
            return jnp.where(iota((rows, n), 1) == cluster, 1.0, 0.0).astype(BF)

        rows = nn(pick(16, 62, wanted), tt[...])
        for lo in (0, 8):
            matrix = unpack(lambda j: rows[lo : lo + 8, 128 * j : 128 * j + 128])
            for c in range(lo, min(lo + 8, 14)):
                v = matrix(c - lo)
                et[64 * c : 64 * c + 64, :] = on_right(v) if c in (7, 8) else on_left(v) if c < 9 else on_both(v)
        ancestors = pick(8, 63, [TOP_OFF[l] + lax.div(col, 2**l) for l in range(6)])
        for k in range(3):
            rows = nn(ancestors, tc[k])
            matrix = unpack(lambda j: rows[:, 128 * j : 128 * j + 128])
            for l in range(6):
                ts[3 * l + k] = on_both(matrix(l))
        path = None
        for l in range(6):
            for k in range(3):
                s = ts[3 * l + k]
                gs[3 * l + k] = s.astype(F32) if l == 0 else nn(path[:, :64], s)
            if l < 5:
                step = et[(9 + l) * 64 : (10 + l) * 64, :]
                path = step if l == 0 else nn(path[:, :64], step).astype(BF)
        v = seen(5, 62)
        for i, l in enumerate((4, 3, 2)):
            v = nt(v[:, :64].astype(BF), et[64 * i : 64 * i + 64, :64]) + seen(l, wanted[i])[:, :64]
        v = nt(v.astype(BF), et[3 * 64 : 5 * 64, :64]) + seen(1, wanted[3])
        v = nt(v.astype(BF), et[5 * 64 : 9 * 64, :])
        v = v + jnp.concatenate([seen(0, wanted[5]), seen(0, wanted[7])], axis=1)
        zb[...] = v.astype(BF)

    upward()
    pl.semaphore_wait(barrier, jnp.where(source, 42, 15))

    c_q = copy(qb, p1.at[member], S_Q, S_Q + member, column_peer(z))

    @pl.when(jnp.logical_not(source))
    def _():
        c_q.start()

    c_u = [send(ub, gu.at[sub], S_U + d, sub_peers[d]) for d in range(1, 4)]
    gu[sub] = ub[...]
    c_xh = [
        send(xs.at[pl.ds(8, 4)], xs.at[pl.ds(0, 4)], S_XH, after),
        send(xs.at[pl.ds(4, 4)], xs.at[pl.ds(12, 4)], S_XH + 1, before),
    ]
    leaves_own, upper_own = tab.at[pl.ds(16, 8)], tab.at[pl.ds(24, 8)]
    c_leaves = [
        send(leaves_own, tab.at[pl.ds(0, 8)], S_TAB, after),
        send(leaves_own, tab.at[pl.ds(32, 8)], S_TAB + 1, before),
    ]
    c_upper = [
        send(upper_own, tab.at[pl.ds(8, 8)], S_TAB + 2, after),
        send(upper_own, tab.at[pl.ds(40, 8)], S_TAB + 3, before),
    ]

    ready(w_tt)
    ready(w_tc)
    ready(w_top)
    prepare_top()

    c_c = [
        pltpu.make_async_remote_copy(
            src_ref=p3.at[x], dst_ref=p3.at[x], send_sem=csem.at[d], recv_sem=rsem.at[S_C + x],
            device_id=plane_peers[d], device_id_type=MESH,
        )
        for d in range(1, 32)
    ]

    @pl.when(source)
    def _():
        p1[member] = qb[...]
        for m in range(8):

            @pl.when(member != m)
            def _(m=m):
                copy(qb, p1.at[m], S_Q, S_Q + m, col_peers[1]).wait_recv()

        total = p1[0].astype(F32)
        for m in range(1, 8):
            total = total + p1[m].astype(F32)
        p3[x] = total.astype(BF)
        for cp in c_c:
            cp.start()

    def widen(src, dst, lo, n):
        def step(i, carry):
            for h in range(8):
                at = lo + 8 * i + h
                v = src[at]
                r = half_swap(v)
                dst[2 * at] = jnp.concatenate([v * m_left, r * m_right], axis=0)
                dst[2 * at + 1] = jnp.concatenate([r * m_left, v * m_right], axis=0)
            return carry

        lax.fori_loop(0, n, step, 0)

    def spread(load, n):
        tiles = jnp.swapaxes(jnp.stack([load(j).astype(F32) for j in range(32)]), 0, 1)
        even, odd = [], []
        for k in range(0, n, 2):
            one, two = tiles[k], tiles[k + 1]
            even.append(jnp.where(left, one, half_swap(two)))
            odd.append(jnp.where(left, half_swap(one), two))
        rows = [jnp.concatenate(even, axis=1), jnp.concatenate(odd, axis=1)]
        return jnp.concatenate(rows, axis=0).astype(BF)

    def coupled(table, ids, w):
        pairs = [table[ids[k], 0:64, :] + table[ids[k + 1], 64:128, :] for k in range(0, len(ids), 2)]
        return nt(jnp.concatenate(pairs, axis=1), w)

    def in_order(one, two):
        return nn(jnp.concatenate([one, two], axis=1).astype(BF), pp[...])

    ready(w_nb)
    widen(xs, xbd, 4, 1)
    for cp in c_xh:
        cp.wait_recv()
    for at in (0, 12):
        for h in range(4):
            v = xs[at + h]
            r = half_swap(v)
            xbd[2 * (at + h)] = jnp.concatenate([v * m_left, r * m_right], axis=0)
            xbd[2 * (at + h) + 1] = jnp.concatenate([r * m_left, v * m_right], axis=0)

    def near_step(i, carry):
        weights = []
        for h in range(8):
            t = 8 * i + h
            weights.append(spread(lambda j: nb[t, :, 128 * j : 128 * j + 128], 8))
        parts = []
        for h in range(8):
            ids = [jnp.clip(near_list[k, 8 * i + h] - (b * 16 - 8), 0, 31) for k in range(8)]
            parts.append(coupled(xbd, ids, weights[h]))
        for h in range(4):
            nearp[4 * i + h] = in_order(parts[2 * h], parts[2 * h + 1])
        return carry

    lax.fori_loop(0, 2, near_step, 0)

    c_d = [copy(p4.at[member], p4.at[member], S_D + d, S_D + d, col_peers[d]) for d in range(1, 8)]
    for i in range(4):

        @pl.when(jnp.logical_not(source & (x == i)))
        def _(i=i):
            copy(p3.at[i], p3.at[i], S_C, S_C + i, col_peers[1]).wait_recv()

    have = []
    for i in (0, 2):
        up = p3[i] * m_left + half_swap(p3[i + 1]) * m_right
        down = half_swap(p3[i]) * m_left + p3[i + 1] * m_right
        have.append(jnp.concatenate([up, down], axis=0))
    d = nt(jnp.concatenate(have, axis=1), zb[...])
    p4[member] = jnp.concatenate([d[:32], d[32:]], axis=1).astype(BF)
    for cp in c_d:
        cp.start()

    for cp in c_u:
        cp.wait_recv()
    g0 = (gu[0].astype(F32) + gu[1].astype(F32)).astype(BF)
    g1 = (gu[2].astype(F32) + gu[3].astype(F32)).astype(BF)
    g2 = (nn(g0[:, :64], ge[0]) + nn(g1[:, :64], ge[1])).astype(BF)
    gt[3] = g0 + half_swap(g0)
    gt[4] = g1 + half_swap(g1)
    gt[5] = g2
    gt[9] = jnp.zeros((64, 128), BF)
    c_gt = [
        send(gt.at[pl.ds(3, 3)], gt.at[pl.ds(0, 3)], S_GT, g_after),
        send(gt.at[pl.ds(3, 3)], gt.at[pl.ds(6, 3)], S_GT + 1, g_before),
    ]

    ready(w_lc)

    def far_blocks(i, carry):
        for h in range(8):
            c = jnp.minimum(8 * i + h, 30)
            wf[8 * i + h] = spread(lambda j: lc[c, :, 128 * j : 128 * j + 128], 8)
        return carry

    lax.fori_loop(0, 4, far_blocks, 0)

    def far_step(i, carry):
        parts = []
        for h in range(8):
            c = jnp.minimum(8 * i + h, 30)
            count = jnp.where(8 * i + h < 31, local_count[c], 0)
            ids = []
            for k in range(8):
                e = jnp.clip(local_partner[k, c] - (b - 1) * 31, 0, 92)
                e = e + jnp.where(e >= 31, 1, 0) + jnp.where(e >= 62, 1, 0)
                ids.append(jnp.where(k < count, e, 63))
            parts.append(coupled(bdt, ids, wf[8 * i + h]))
        for h in range(4):
            far[4 * i + h] = in_order(parts[2 * h], parts[2 * h + 1])
        return carry

    widen(tab, bdt, 16, 2)
    for cp in c_leaves:
        cp.wait_recv()
    widen(tab, bdt, 0, 1)
    widen(tab, bdt, 32, 1)
    lax.fori_loop(0, 2, far_step, 0)

    ready(w_gc)
    for cp in c_gt:
        cp.wait_recv()
    found = []
    for c in range(3):
        w = spread(lambda j: gc[c, :, 128 * j : 128 * j + 128], 4)
        entries = []
        for k in range(4):
            e = jnp.clip(group_partner[c, k] - (leaf - 1) * 3, 0, 8)
            entries.append(gt[jnp.where(k < group_count[c], e, 9)])
        pairs = [entries[k] * m_left + entries[k + 1] * m_right for k in (0, 2)]
        found.append(nt(jnp.concatenate(pairs, axis=1), w))
    f01 = in_order(found[0], found[1])
    f2 = in_order(found[2], found[2])
    f_half = jnp.where(half == 0, f01, half_swap(f01))[:, :64]
    d_half = f_half + nt(f2[:, :64].astype(BF), ge[half][:, :64])

    for cp in c_upper:
        cp.wait_recv()
    widen(tab, bdt, 8, 1)
    widen(tab, bdt, 40, 1)
    lax.fori_loop(2, 4, far_step, 0)

    e_root = es[30 * 64 : 31 * 64, :]
    d_root = far[15][:, :64] + nt(d_half.astype(BF), e_root[:, :64])
    state = jnp.concatenate([d_root, nt(eye, hr[...][:, :64])], axis=0).astype(BF)
    nothing = jnp.zeros((64, 128), F32)

    def with_far(v, i):
        return (v + jnp.concatenate([far[i], nothing], axis=0)).astype(BF)

    states = [with_far(nt(state, es[28 * 64 : 30 * 64, :64]), 14)]
    for first, pair in ((24, 12), (16, 8), (0, 0)):
        lower_level = []
        for i, parents in enumerate(states):
            at = (first + 4 * i) * 64
            both = nt(parents, es[at : at + 256, :])
            lower_level.append(with_far(both[:, :128], pair + 2 * i))
            lower_level.append(with_far(both[:, 128:], pair + 2 * i + 1))
        states = lower_level
    for m in range(8):
        r = nn(states[m], bd[m])
        nearp[m] = nearp[m] + r[:64]
        vht[m] = r[64:].astype(BF)

    for cp in c_d:
        cp.wait_recv()
    total = p4[0].astype(F32)
    for m in range(1, 8):
        total = total + p4[m].astype(F32)
    d_col = jnp.concatenate([total[:, :64], total[:, 64:]], axis=0).astype(BF)
    for m in range(8):
        out[:, 128 * m : 128 * m + 128] = nearp[m] + nn(d_col, vht[m])

    for cp in c_u + c_xh + c_leaves + c_upper + c_gt + c_d:
        cp.wait_send()

    @pl.when(source)
    def _():
        for cp in c_c:
            cp.wait_send()

    @pl.when(jnp.logical_not(source))
    def _():
        c_q.wait_send()


def body(
    right_sides, leaf_basis, near_blocks, near_list, local_transfer, local_couple, local_partner, local_count,
    group_transfer, group_couple, group_partner, group_count, top_transfer, top_couple, top_partner, top_count,
):
    hbm = pl.BlockSpec(memory_space=pltpu.HBM)
    vm = pltpu.VMEM
    return pl.pallas_call(
        kernel,
        out_shape=jax.ShapeDtypeStruct((64, 1024), F32),
        in_specs=[hbm] * 16,
        out_specs=pl.BlockSpec(memory_space=pltpu.VMEM),
        scratch_shapes=[
            vm((16, 64, 128), BF),
            vm((64, 1024), BF),
            vm((16, 8, 4096), BF),
            vm((31, 4096), BF),
            vm((31, 8, 4096), BF),
            vm((3, 4096), BF),
            vm((3, 4, 4096), BF),
            vm((62, 4096), BF),
            vm((3, 63, 4096), BF),
            vm((31 * 64, 128), BF),
            vm((3, 64, 128), BF),
            vm((16 * 64, 128), BF),
            vm((18, 64, 128), BF),
            vm((32, 64, 512), BF),
            vm((8, 128, 128), BF),
            vm((48, 64, 128), BF),
            vm((96, 128, 128), BF),
            vm((32, 128, 128), BF),
            vm((128, 128), BF),
            vm((32, 128), BF),
            vm((64, 128), BF),
            vm((8, 32, 128), BF),
            vm((4, 32, 128), BF),
            vm((8, 32, 128), BF),
            vm((64, 128), BF),
            vm((4, 64, 128), BF),
            vm((10, 64, 128), BF),
            vm((18, 64, 128), F32),
            vm((64, 256), BF),
            vm((16, 64, 128), F32),
            vm((8, 64, 128), F32),
            vm((8, 64, 128), BF),
            pltpu.SMEM((8, 16), jnp.int32),
            pltpu.SMEM((8, 31), jnp.int32),
            pltpu.SMEM((31,), jnp.int32),
            pltpu.SMEM((3, 4), jnp.int32),
            pltpu.SMEM((3,), jnp.int32),
            pltpu.SMEM((3, 63), jnp.int32),
            pltpu.SMEM((63,), jnp.int32),
            pltpu.SemaphoreType.DMA((24,)),
            pltpu.SemaphoreType.DMA((N_SEM,)),
            pltpu.SemaphoreType.DMA((N_SEM,)),
            pltpu.SemaphoreType.DMA((32,)),
        ],
        compiler_params=pltpu.CompilerParams(
            collective_id=0, has_side_effects=True, vmem_limit_bytes=60 * 1024 * 1024
        ),
        name="h2",
    )(
        near_list.T, local_partner.T, local_count, group_partner, group_count, top_partner.T, top_count,
        right_sides, leaf_basis, near_blocks, local_transfer, local_couple, group_transfer, group_couple,
        top_transfer, jnp.transpose(top_couple, (1, 0, 2)),
    )


def solution(mesh):
    both = ("leaf", "sub")
    placed = (
        P(None, both), P(None, both), P(both, None, None), P(both, None), P(both, None), P(both, None, None),
        P(both, None), P(both), P("leaf", None), P("leaf", None, None), P("leaf", None), P("leaf"),
        P(), P(), P(), P(),
    )
    return jax.shard_map(body, mesh=mesh, in_specs=placed, out_specs=P(None, both), check_vma=False)
```

```python
import functools

import jax
import jax.numpy as jnp
from jax import lax
from jax.experimental import pallas as pl
from jax.experimental.pallas import tpu as pltpu
from jax.sharding import PartitionSpec as P

BF = jnp.bfloat16
F32 = jnp.float32
MESH = pl.DeviceIdType.MESH
TOP_OFF = (0, 32, 48, 56, 60, 62)
S_Q, S_C, S_D, S_U, S_XH, S_TAB, S_GT, N_SEM = 0, 8, 12, 20, 24, 26, 30, 32


def nt(a, b):
    return lax.dot_general(a, b, (((1,), (1,)), ((), ())), preferred_element_type=F32)


def nn(a, b):
    return jnp.dot(a, b, preferred_element_type=F32)


def half_swap(v):
    return pltpu.roll(v, 64, 1)


def iota(shape, dim):
    return lax.broadcasted_iota(jnp.int32, shape, dim)


def kernel(
    near_list_hbm, local_partner_hbm, local_count_hbm, group_partner_hbm, group_count_hbm, top_partner_hbm,
    top_count_hbm, x_hbm, basis_hbm, near_hbm, ltrans_hbm, lcouple_hbm, gtrans_hbm, gcouple_hbm, ttrans_hbm, tcouple_hbm,
    out,
    xs, bs, nb, lt, lc, gt_in, gc, tt, tc,
    es, ge, et, ts, wf, bd, tab, bdt, xbd, pp,
    qb, hr, p1, p3, p4, ub, gu, gt, gs, zb, far, nearp, vht,
    near_list, local_partner, local_count, group_partner, group_count, top_partner, top_count,
    lsem, ssem, rsem, csem,
):
    leaf = lax.axis_index("leaf")
    sub = lax.axis_index("sub")
    col, ylo = lax.div(leaf, 2), lax.rem(leaf, 2)
    z, x = lax.div(col, 4), lax.rem(col, 4)
    member = ylo * 4 + sub
    b = leaf * 4 + sub
    half = lax.div(sub, 2)

    source = member == z

    def column_peer(m):
        return (col * 2 + lax.div(m, 4), lax.rem(m, 4))

    def ring_peer(step):
        n = lax.rem(b + step, 256)
        return (lax.div(n, 4), lax.rem(n, 4))

    col_peers = [column_peer(lax.rem(member + d, 8)) for d in range(8)]
    plane_peers = [(lax.rem(col + d, 32) * 2 + ylo, sub) for d in range(32)]
    plane_sources = [((member * 4 + i) * 2 + ylo, sub) for i in range(4)]
    sub_peers = [(leaf, lax.rem(sub + d, 4)) for d in range(4)]
    after, before = ring_peer(1), ring_peer(255)
    g_after = (lax.rem(leaf + 1, 64), sub)
    g_before = (lax.rem(leaf + 63, 64), sub)

    local = []

    def fetch(src, dst):
        cp = pltpu.make_async_copy(src, dst, lsem.at[len(local)])
        cp.start()
        local.append(cp)
        return cp

    w_x = [fetch(x_hbm.at[:, pl.ds(128 * m, 128)], xs.at[4 + m]) for m in range(8)]
    w_b = [fetch(basis_hbm, bs)]
    w_lt = [fetch(ltrans_hbm, lt)]
    w_gt = [fetch(gtrans_hbm, gt_in)]
    w_tt = [fetch(ttrans_hbm, tt)]
    w_tc = [fetch(tcouple_hbm, tc)]
    w_top = [fetch(top_partner_hbm, top_partner), fetch(top_count_hbm, top_count)]
    w_nb = [fetch(near_hbm, nb), fetch(near_list_hbm, near_list)]
    w_lc = [fetch(lcouple_hbm, lc), fetch(local_partner_hbm, local_partner), fetch(local_count_hbm, local_count)]
    w_gc = [fetch(gcouple_hbm, gc), fetch(group_partner_hbm, group_partner), fetch(group_count_hbm, group_count)]

    def ready(copies):
        for cp in copies:
            cp.wait()

    barrier = pltpu.get_barrier_semaphore()
    def greet(peers):
        for peer in peers:
            pl.semaphore_signal(barrier, inc=1, device_id=peer, device_id_type=MESH)

    greet(col_peers[1:] + [after, before, g_after, g_before])

    @pl.when(source)
    def _():
        greet(plane_peers[1:])

    @pl.when(jnp.logical_not(source))
    def _():
        greet(plane_sources)

    def copy(src, dst, sent, got, peer):
        return pltpu.make_async_remote_copy(
            src_ref=src, dst_ref=dst, send_sem=ssem.at[sent], recv_sem=rsem.at[got],
            device_id=peer, device_id_type=MESH,
        )

    def send(src, dst, place, peer):
        cp = copy(src, dst, place, place, peer)
        cp.start()
        return cp

    lane = iota((1, 128), 1)
    left = lane < 64
    m_left = jnp.where(left, 1.0, 0.0).astype(BF)
    m_right = jnp.where(left, 0.0, 1.0).astype(BF)
    row, column = iota((128, 128), 0), iota((128, 128), 1)
    from_row = lax.div(row, 64) * 64 + 2 * lax.rem(row, 32) + lax.div(lax.rem(row, 64), 32)
    pp[...] = jnp.where(column == from_row, 1.0, 0.0).astype(BF)
    eye = jnp.where(iota((64, 64), 0) == iota((64, 64), 1), 1.0, 0.0).astype(BF)

    def unpack(load):
        parts = []
        for lo in (0, 16):
            tiles = []
            for j in range(lo, lo + 16):
                v = load(j)
                tiles += [v, half_swap(v)]
            parts.append(jnp.swapaxes(jnp.stack(tiles), 0, 1))
        return lambda c: jnp.concatenate([part[c] for part in parts], axis=0).astype(BF)

    def filled(v):
        v = v.astype(F32)
        if v.shape[0] == 8:
            return v
        return jnp.concatenate([v, jnp.zeros((8 - v.shape[0], 128), F32)], axis=0)

    def on_left(v):
        return v * m_left

    def on_right(v):
        return half_swap(v * m_left)

    def on_both(v):
        return on_left(v) + on_right(v)

    ready(w_x)
    ready(w_b)
    for m in range(8):
        two = bs[:, 128 * m : 128 * m + 128]
        both = jnp.concatenate([two * m_left, two * m_right], axis=0)
        bd[m] = both
        tab[16 + m] = nt(xs[4 + m], both).astype(BF)
    ready(w_lt)
    ready(w_gt)

    def upward():
        for lo in range(0, 31, 8):
            hi = min(lo + 8, 31)
            matrix = unpack(lambda j: filled(lt[lo:hi, 128 * j : 128 * j + 128]))
            for c in range(lo, hi):
                right = c < 30 and (c // 2) % 2 == 1
                v = matrix(c - lo)
                es[64 * c : 64 * c + 64, :] = on_right(v) if right else on_left(v)
        matrix = unpack(lambda j: filled(gt_in[:, 128 * j : 128 * j + 128]))
        for c in range(3):
            ge[c] = on_both(matrix(c))
        e_root = es[30 * 64 : 31 * 64, :]
        pair_down = nn(ge[half][:, :64], ge[2]).astype(BF)
        h_root = nn(e_root[:, :64], pair_down).astype(BF)
        hr[...] = h_root
        for lo, hi, n in ((16, 24, 4), (24, 28, 2), (28, 30, 1)):
            for i in range(n):
                kids = jnp.concatenate([tab[lo + 2 * i], tab[lo + 2 * i + 1]], axis=1)
                first = 2 * (lo - 16) + 4 * i
                tab[hi + i] = nn(kids, es[first * 64 : first * 64 + 256, :]).astype(BF)
        c_root = nn(tab[30], es[28 * 64 : 30 * 64, :]).astype(BF)
        tab[31] = c_root
        q = nn(c_root[:, :64], h_root)
        qb[...] = jnp.where(left, q[:32], q[32:]).astype(BF)
        ub[...] = nn(c_root[:, :64], e_root).astype(BF)

    def seen(l, first):
        mine = TOP_OFF[l] + lax.div(col, 2**l)
        total = jnp.zeros((64, 128), F32)
        for k in range(3):
            partner = jnp.where(k < top_count[mine], top_partner[k, mine], -1)
            target = jnp.where(left, first, first + 1)
            total = total + jnp.where(target == partner, gs[3 * l + k], 0.0)
        return total

    def prepare_top():
        wanted = [60 + lax.div(member, 4), 56 + lax.div(member, 2), 48 + member]
        wanted += [32 + 2 * member + i for i in range(2)] + [4 * member + i for i in range(4)]
        wanted += [TOP_OFF[l] + lax.div(col, 2**l) for l in range(5)]

        def pick(rows, n, clusters):
            at = iota((rows, n), 0)
            cluster = at * 0 - 1
            for i, c in enumerate(clusters):
                cluster = jnp.where(at == i, c, cluster)
            return jnp.where(iota((rows, n), 1) == cluster, 1.0, 0.0).astype(BF)

        rows = nn(pick(16, 62, wanted), tt[...])
        for lo in (0, 8):
            matrix = unpack(lambda j: rows[lo : lo + 8, 128 * j : 128 * j + 128])
            for c in range(lo, min(lo + 8, 14)):
                v = matrix(c - lo)
                et[64 * c : 64 * c + 64, :] = on_right(v) if c in (7, 8) else on_left(v) if c < 9 else on_both(v)
        ancestors = pick(8, 63, [TOP_OFF[l] + lax.div(col, 2**l) for l in range(6)])
        for k in range(3):
            rows = nn(ancestors, tc[k])
            matrix = unpack(lambda j: rows[:, 128 * j : 128 * j + 128])
            for l in range(6):
                ts[3 * l + k] = on_both(matrix(l))
        path = None
        for l in range(6):
            for k in range(3):
                s = ts[3 * l + k]
                gs[3 * l + k] = s.astype(F32) if l == 0 else nn(path[:, :64], s)
            if l < 5:
                step = et[(9 + l) * 64 : (10 + l) * 64, :]
                path = step if l == 0 else nn(path[:, :64], step).astype(BF)
        v = seen(5, 62)
        for i, l in enumerate((4, 3, 2)):
            v = nt(v[:, :64].astype(BF), et[64 * i : 64 * i + 64, :64]) + seen(l, wanted[i])[:, :64]
        v = nt(v.astype(BF), et[3 * 64 : 5 * 64, :64]) + seen(1, wanted[3])
        v = nt(v.astype(BF), et[5 * 64 : 9 * 64, :])
        v = v + jnp.concatenate([seen(0, wanted[5]), seen(0, wanted[7])], axis=1)
        zb[...] = v.astype(BF)

    upward()
    pl.semaphore_wait(barrier, jnp.where(source, 42, 15))

    c_q = copy(qb, p1.at[member], S_Q, S_Q + member, column_peer(z))

    @pl.when(jnp.logical_not(source))
    def _():
        c_q.start()

    c_u = [send(ub, gu.at[sub], S_U + d, sub_peers[d]) for d in range(1, 4)]
    gu[sub] = ub[...]
    c_xh = [
        send(xs.at[pl.ds(8, 4)], xs.at[pl.ds(0, 4)], S_XH, after),
        send(xs.at[pl.ds(4, 4)], xs.at[pl.ds(12, 4)], S_XH + 1, before),
    ]
    leaves_own, upper_own = tab.at[pl.ds(16, 8)], tab.at[pl.ds(24, 8)]
    c_leaves = [
        copy(leaves_own, tab.at[pl.ds(0, 8)], S_TAB, S_TAB, after),
        copy(leaves_own, tab.at[pl.ds(32, 8)], S_TAB + 1, S_TAB + 1, before),
    ]
    c_upper = [
        copy(upper_own, tab.at[pl.ds(8, 8)], S_TAB + 2, S_TAB + 2, after),
        copy(upper_own, tab.at[pl.ds(40, 8)], S_TAB + 3, S_TAB + 3, before),
    ]

    @pl.when(jnp.logical_not(source))
    def _():
        for cp in c_leaves + c_upper:
            cp.start()

    c_c = [
        pltpu.make_async_remote_copy(
            src_ref=p3.at[x], dst_ref=p3.at[x], send_sem=csem.at[d], recv_sem=rsem.at[S_C + x],
            device_id=plane_peers[d], device_id_type=MESH,
        )
        for d in range(1, 32)
    ]

    @pl.when(source)
    def _():
        p1[member] = qb[...]
        for m in range(8):

            @pl.when(member != m)
            def _(m=m):
                copy(qb, p1.at[m], S_Q, S_Q + m, col_peers[1]).wait_recv()

        total = p1[0].astype(F32)
        for m in range(1, 8):
            total = total + p1[m].astype(F32)
        p3[x] = total.astype(BF)
        for cp in c_c + c_leaves + c_upper:
            cp.start()

    ready(w_tt)
    ready(w_tc)
    ready(w_top)
    prepare_top()

    def widen(src, dst, lo, n):
        def step(i, carry):
            for h in range(8):
                at = lo + 8 * i + h
                v = src[at]
                r = half_swap(v)
                dst[2 * at] = jnp.concatenate([v * m_left, r * m_right], axis=0)
                dst[2 * at + 1] = jnp.concatenate([r * m_left, v * m_right], axis=0)
            return carry

        lax.fori_loop(0, n, step, 0)

    def spread(load, n):
        tiles = jnp.swapaxes(jnp.stack([load(j).astype(F32) for j in range(32)]), 0, 1)
        even, odd = [], []
        for k in range(0, n, 2):
            one, two = tiles[k], tiles[k + 1]
            even.append(jnp.where(left, one, half_swap(two)))
            odd.append(jnp.where(left, half_swap(one), two))
        rows = [jnp.concatenate(even, axis=1), jnp.concatenate(odd, axis=1)]
        return jnp.concatenate(rows, axis=0).astype(BF)

    def coupled(table, ids, w):
        pairs = [table[ids[k], 0:64, :] + table[ids[k + 1], 64:128, :] for k in range(0, len(ids), 2)]
        return nt(jnp.concatenate(pairs, axis=1), w)

    def in_order(one, two):
        return nn(jnp.concatenate([one, two], axis=1).astype(BF), pp[...])

    ready(w_nb)
    widen(xs, xbd, 4, 1)
    for cp in c_xh:
        cp.wait_recv()
    for at in (0, 12):
        for h in range(4):
            v = xs[at + h]
            r = half_swap(v)
            xbd[2 * (at + h)] = jnp.concatenate([v * m_left, r * m_right], axis=0)
            xbd[2 * (at + h) + 1] = jnp.concatenate([r * m_left, v * m_right], axis=0)

    def near_step(i, carry):
        weights = []
        for h in range(8):
            t = 8 * i + h
            weights.append(spread(lambda j: nb[t, :, 128 * j : 128 * j + 128], 8))
        parts = []
        for h in range(8):
            ids = [jnp.clip(near_list[k, 8 * i + h] - (b * 16 - 8), 0, 31) for k in range(8)]
            parts.append(coupled(xbd, ids, weights[h]))
        for h in range(4):
            nearp[4 * i + h] = in_order(parts[2 * h], parts[2 * h + 1])
        return carry

    lax.fori_loop(0, 2, near_step, 0)

    c_d = [copy(p4.at[member], p4.at[member], S_D + d, S_D + d, col_peers[d]) for d in range(1, 8)]
    for i in range(4):

        @pl.when(jnp.logical_not(source & (x == i)))
        def _(i=i):
            copy(p3.at[i], p3.at[i], S_C, S_C + i, col_peers[1]).wait_recv()

    have = []
    for i in (0, 2):
        up = p3[i] * m_left + half_swap(p3[i + 1]) * m_right
        down = half_swap(p3[i]) * m_left + p3[i + 1] * m_right
        have.append(jnp.concatenate([up, down], axis=0))
    d = nt(jnp.concatenate(have, axis=1), zb[...])
    p4[member] = jnp.concatenate([d[:32], d[32:]], axis=1).astype(BF)
    for cp in c_d:
        cp.start()

    for cp in c_u:
        cp.wait_recv()
    g0 = (gu[0].astype(F32) + gu[1].astype(F32)).astype(BF)
    g1 = (gu[2].astype(F32) + gu[3].astype(F32)).astype(BF)
    g2 = (nn(g0[:, :64], ge[0]) + nn(g1[:, :64], ge[1])).astype(BF)
    gt[3] = g0 + half_swap(g0)
    gt[4] = g1 + half_swap(g1)
    gt[5] = g2
    gt[9] = jnp.zeros((64, 128), BF)
    c_gt = [
        send(gt.at[pl.ds(3, 3)], gt.at[pl.ds(0, 3)], S_GT, g_after),
        send(gt.at[pl.ds(3, 3)], gt.at[pl.ds(6, 3)], S_GT + 1, g_before),
    ]

    ready(w_lc)

    def far_blocks(i, carry):
        for h in range(8):
            c = jnp.minimum(8 * i + h, 30)
            wf[8 * i + h] = spread(lambda j: lc[c, :, 128 * j : 128 * j + 128], 8)
        return carry

    lax.fori_loop(0, 4, far_blocks, 0)

    def far_step(i, carry):
        parts = []
        for h in range(8):
            c = jnp.minimum(8 * i + h, 30)
            count = jnp.where(8 * i + h < 31, local_count[c], 0)
            ids = []
            for k in range(8):
                e = jnp.clip(local_partner[k, c] - (b - 1) * 31, 0, 92)
                e = e + jnp.where(e >= 31, 1, 0) + jnp.where(e >= 62, 1, 0)
                ids.append(jnp.where(k < count, e, 63))
            parts.append(coupled(bdt, ids, wf[8 * i + h]))
        for h in range(4):
            far[4 * i + h] = in_order(parts[2 * h], parts[2 * h + 1])
        return carry

    widen(tab, bdt, 16, 2)
    for cp in c_leaves:
        cp.wait_recv()
    widen(tab, bdt, 0, 1)
    widen(tab, bdt, 32, 1)
    lax.fori_loop(0, 2, far_step, 0)

    ready(w_gc)
    for cp in c_gt:
        cp.wait_recv()
    found = []
    for c in range(3):
        w = spread(lambda j: gc[c, :, 128 * j : 128 * j + 128], 4)
        entries = []
        for k in range(4):
            e = jnp.clip(group_partner[c, k] - (leaf - 1) * 3, 0, 8)
            entries.append(gt[jnp.where(k < group_count[c], e, 9)])
        pairs = [entries[k] * m_left + entries[k + 1] * m_right for k in (0, 2)]
        found.append(nt(jnp.concatenate(pairs, axis=1), w))
    f01 = in_order(found[0], found[1])
    f2 = in_order(found[2], found[2])
    f_half = jnp.where(half == 0, f01, half_swap(f01))[:, :64]
    d_half = f_half + nt(f2[:, :64].astype(BF), ge[half][:, :64])

    for cp in c_upper:
        cp.wait_recv()
    widen(tab, bdt, 8, 1)
    widen(tab, bdt, 40, 1)
    lax.fori_loop(2, 4, far_step, 0)

    e_root = es[30 * 64 : 31 * 64, :]
    d_root = far[15][:, :64] + nt(d_half.astype(BF), e_root[:, :64])
    state = jnp.concatenate([d_root, nt(eye, hr[...][:, :64])], axis=0).astype(BF)
    nothing = jnp.zeros((64, 128), F32)

    def with_far(v, i):
        return (v + jnp.concatenate([far[i], nothing], axis=0)).astype(BF)

    states = [with_far(nt(state, es[28 * 64 : 30 * 64, :64]), 14)]
    for first, pair in ((24, 12), (16, 8), (0, 0)):
        lower_level = []
        for i, parents in enumerate(states):
            at = (first + 4 * i) * 64
            both = nt(parents, es[at : at + 256, :])
            lower_level.append(with_far(both[:, :128], pair + 2 * i))
            lower_level.append(with_far(both[:, 128:], pair + 2 * i + 1))
        states = lower_level
    for m in range(8):
        r = nn(states[m], bd[m])
        nearp[m] = nearp[m] + r[:64]
        vht[m] = r[64:].astype(BF)

    for cp in c_d:
        cp.wait_recv()
    total = p4[0].astype(F32)
    for m in range(1, 8):
        total = total + p4[m].astype(F32)
    d_col = jnp.concatenate([total[:, :64], total[:, 64:]], axis=0).astype(BF)
    for m in range(8):
        out[:, 128 * m : 128 * m + 128] = nearp[m] + nn(d_col, vht[m])

    for cp in c_u + c_xh + c_leaves + c_upper + c_gt + c_d:
        cp.wait_send()

    @pl.when(source)
    def _():
        for cp in c_c:
            cp.wait_send()

    @pl.when(jnp.logical_not(source))
    def _():
        c_q.wait_send()


def body(
    right_sides, leaf_basis, near_blocks, near_list, local_transfer, local_couple, local_partner, local_count,
    group_transfer, group_couple, group_partner, group_count, top_transfer, top_couple, top_partner, top_count,
):
    hbm = pl.BlockSpec(memory_space=pltpu.HBM)
    vm = pltpu.VMEM
    return pl.pallas_call(
        kernel,
        out_shape=jax.ShapeDtypeStruct((64, 1024), F32),
        in_specs=[hbm] * 16,
        out_specs=pl.BlockSpec(memory_space=pltpu.VMEM),
        scratch_shapes=[
            vm((16, 64, 128), BF),
            vm((64, 1024), BF),
            vm((16, 8, 4096), BF),
            vm((31, 4096), BF),
            vm((31, 8, 4096), BF),
            vm((3, 4096), BF),
            vm((3, 4, 4096), BF),
            vm((62, 4096), BF),
            vm((3, 63, 4096), BF),
            vm((31 * 64, 128), BF),
            vm((3, 64, 128), BF),
            vm((16 * 64, 128), BF),
            vm((18, 64, 128), BF),
            vm((32, 64, 512), BF),
            vm((8, 128, 128), BF),
            vm((48, 64, 128), BF),
            vm((96, 128, 128), BF),
            vm((32, 128, 128), BF),
            vm((128, 128), BF),
            vm((32, 128), BF),
            vm((64, 128), BF),
            vm((8, 32, 128), BF),
            vm((4, 32, 128), BF),
            vm((8, 32, 128), BF),
            vm((64, 128), BF),
            vm((4, 64, 128), BF),
            vm((10, 64, 128), BF),
            vm((18, 64, 128), F32),
            vm((64, 256), BF),
            vm((16, 64, 128), F32),
            vm((8, 64, 128), F32),
            vm((8, 64, 128), BF),
            pltpu.SMEM((8, 16), jnp.int32),
            pltpu.SMEM((8, 31), jnp.int32),
            pltpu.SMEM((31,), jnp.int32),
            pltpu.SMEM((3, 4), jnp.int32),
            pltpu.SMEM((3,), jnp.int32),
            pltpu.SMEM((3, 63), jnp.int32),
            pltpu.SMEM((63,), jnp.int32),
            pltpu.SemaphoreType.DMA((24,)),
            pltpu.SemaphoreType.DMA((N_SEM,)),
            pltpu.SemaphoreType.DMA((N_SEM,)),
            pltpu.SemaphoreType.DMA((32,)),
        ],
        compiler_params=pltpu.CompilerParams(
            collective_id=0, has_side_effects=True, vmem_limit_bytes=60 * 1024 * 1024
        ),
        name="h2",
    )(
        near_list.T, local_partner.T, local_count, group_partner, group_count, top_partner.T, top_count,
        right_sides, leaf_basis, near_blocks, local_transfer, local_couple, group_transfer, group_couple,
        top_transfer, jnp.transpose(top_couple, (1, 0, 2)),
    )


def solution(mesh):
    both = ("leaf", "sub")
    placed = (
        P(None, both), P(None, both), P(both, None, None), P(both, None), P(both, None), P(both, None, None),
        P(both, None), P(both), P("leaf", None), P("leaf", None, None), P("leaf", None), P("leaf"),
        P(), P(), P(), P(),
    )
    return jax.shard_map(body, mesh=mesh, in_specs=placed, out_specs=P(None, both), check_vma=False)
```

```python
import functools

import jax
import jax.numpy as jnp
from jax import lax
from jax.experimental import pallas as pl
from jax.experimental.pallas import tpu as pltpu
from jax.sharding import PartitionSpec as P

BF = jnp.bfloat16
F32 = jnp.float32
MESH = pl.DeviceIdType.MESH
TOP_OFF = (0, 32, 48, 56, 60, 62)
S_Q, S_C, S_D, S_U, S_XH, S_TAB, S_GT, N_SEM = 0, 8, 12, 20, 24, 26, 30, 32


def nt(a, b):
    return lax.dot_general(a, b, (((1,), (1,)), ((), ())), preferred_element_type=F32)


def nn(a, b):
    return jnp.dot(a, b, preferred_element_type=F32)


def half_swap(v):
    return pltpu.roll(v, 64, 1)


def iota(shape, dim):
    return lax.broadcasted_iota(jnp.int32, shape, dim)


def kernel(
    near_list_hbm, local_partner_hbm, local_count_hbm, group_partner_hbm, group_count_hbm, top_partner_hbm,
    top_count_hbm, x_hbm, basis_hbm, near_hbm, ltrans_hbm, lcouple_hbm, gtrans_hbm, gcouple_hbm, ttrans_hbm, tcouple_hbm,
    out,
    xs, bs, nb, lt, lc, gt_in, gc, tt, tc,
    es, ge, et, ts, wf, bd, tab, bdt, xbd, pp,
    qb, hr, p1, p3, p4, ub, gu, gt, gs, zb, far, nearp, vht,
    near_list, local_partner, local_count, group_partner, group_count, top_partner, top_count,
    lsem, ssem, rsem, csem,
):
    leaf = lax.axis_index("leaf")
    sub = lax.axis_index("sub")
    col, ylo = lax.div(leaf, 2), lax.rem(leaf, 2)
    z, x = lax.div(col, 4), lax.rem(col, 4)
    member = ylo * 4 + sub
    b = leaf * 4 + sub
    half = lax.div(sub, 2)

    source = member == z

    def column_peer(m):
        return (col * 2 + lax.div(m, 4), lax.rem(m, 4))

    def ring_peer(step):
        n = lax.rem(b + step, 256)
        return (lax.div(n, 4), lax.rem(n, 4))

    col_peers = [column_peer(lax.rem(member + d, 8)) for d in range(8)]
    plane_peers = [(lax.rem(col + d, 32) * 2 + ylo, sub) for d in range(32)]
    plane_sources = [((member * 4 + i) * 2 + ylo, sub) for i in range(4)]
    sub_peers = [(leaf, lax.rem(sub + d, 4)) for d in range(4)]
    after, before = ring_peer(1), ring_peer(255)
    g_after = (lax.rem(leaf + 1, 64), sub)
    g_before = (lax.rem(leaf + 63, 64), sub)

    local = []

    def fetch(src, dst):
        cp = pltpu.make_async_copy(src, dst, lsem.at[len(local)])
        cp.start()
        local.append(cp)
        return cp

    w_x = [fetch(x_hbm.at[:, pl.ds(128 * m, 128)], xs.at[4 + m]) for m in range(8)]
    w_b = [fetch(basis_hbm, bs)]
    w_lt = [fetch(ltrans_hbm, lt)]
    w_gt = [fetch(gtrans_hbm, gt_in)]
    w_tt = [fetch(ttrans_hbm, tt)]
    w_tc = [fetch(tcouple_hbm, tc)]
    w_top = [fetch(top_partner_hbm, top_partner), fetch(top_count_hbm, top_count)]
    w_nb = [fetch(near_hbm, nb), fetch(near_list_hbm, near_list)]
    w_lc = [fetch(lcouple_hbm, lc), fetch(local_partner_hbm, local_partner), fetch(local_count_hbm, local_count)]
    w_gc = [fetch(gcouple_hbm, gc), fetch(group_partner_hbm, group_partner), fetch(group_count_hbm, group_count)]

    def ready(copies):
        for cp in copies:
            cp.wait()

    barrier = pltpu.get_barrier_semaphore()
    def greet(peers):
        for peer in peers:
            pl.semaphore_signal(barrier, inc=1, device_id=peer, device_id_type=MESH)

    greet(col_peers[1:] + [after, before, g_after, g_before])

    @pl.when(source)
    def _():
        greet(plane_peers[1:])

    @pl.when(jnp.logical_not(source))
    def _():
        greet(plane_sources)

    def copy(src, dst, sent, got, peer):
        return pltpu.make_async_remote_copy(
            src_ref=src, dst_ref=dst, send_sem=ssem.at[sent], recv_sem=rsem.at[got],
            device_id=peer, device_id_type=MESH,
        )

    def send(src, dst, place, peer):
        cp = copy(src, dst, place, place, peer)
        cp.start()
        return cp

    lane = iota((1, 128), 1)
    left = lane < 64
    m_left = jnp.where(left, 1.0, 0.0).astype(BF)
    m_right = jnp.where(left, 0.0, 1.0).astype(BF)
    row, column = iota((128, 128), 0), iota((128, 128), 1)
    from_row = lax.div(row, 64) * 64 + 2 * lax.rem(row, 32) + lax.div(lax.rem(row, 64), 32)
    pp[...] = jnp.where(column == from_row, 1.0, 0.0).astype(BF)
    eye = jnp.where(iota((64, 64), 0) == iota((64, 64), 1), 1.0, 0.0).astype(BF)

    def unpack(load):
        parts = []
        for lo in (0, 16):
            tiles = []
            for j in range(lo, lo + 16):
                v = load(j)
                tiles += [v, half_swap(v)]
            parts.append(jnp.swapaxes(jnp.stack(tiles), 0, 1))
        return lambda c: jnp.concatenate([part[c] for part in parts], axis=0).astype(BF)

    def filled(v):
        v = v.astype(F32)
        if v.shape[0] == 8:
            return v
        return jnp.concatenate([v, jnp.zeros((8 - v.shape[0], 128), F32)], axis=0)

    def on_left(v):
        return v * m_left

    def on_right(v):
        return half_swap(v * m_left)

    def on_both(v):
        return on_left(v) + on_right(v)

    ready(w_x)
    ready(w_b)
    for m in range(8):
        two = bs[:, 128 * m : 128 * m + 128]
        both = jnp.concatenate([two * m_left, two * m_right], axis=0)
        bd[m] = both
        tab[16 + m] = nt(xs[4 + m], both).astype(BF)
    ready(w_lt)
    ready(w_gt)

    def upward():
        for lo in range(0, 31, 8):
            hi = min(lo + 8, 31)
            matrix = unpack(lambda j: filled(lt[lo:hi, 128 * j : 128 * j + 128]))
            for c in range(lo, hi):
                right = c < 30 and (c // 2) % 2 == 1
                v = matrix(c - lo)
                es[64 * c : 64 * c + 64, :] = on_right(v) if right else on_left(v)
        matrix = unpack(lambda j: filled(gt_in[:, 128 * j : 128 * j + 128]))
        for c in range(3):
            ge[c] = on_both(matrix(c))
        e_root = es[30 * 64 : 31 * 64, :]
        pair_down = nn(ge[half][:, :64], ge[2]).astype(BF)
        h_root = nn(e_root[:, :64], pair_down).astype(BF)
        hr[...] = h_root
        for lo, hi, n in ((16, 24, 4), (24, 28, 2), (28, 30, 1)):
            for i in range(n):
                kids = jnp.concatenate([tab[lo + 2 * i], tab[lo + 2 * i + 1]], axis=1)
                first = 2 * (lo - 16) + 4 * i
                tab[hi + i] = nn(kids, es[first * 64 : first * 64 + 256, :]).astype(BF)
        c_root = nn(tab[30], es[28 * 64 : 30 * 64, :]).astype(BF)
        tab[31] = c_root
        q = nn(c_root[:, :64], h_root)
        qb[...] = jnp.where(left, q[:32], q[32:]).astype(BF)
        ub[...] = nn(c_root[:, :64], e_root).astype(BF)

    def seen(l, first):
        mine = TOP_OFF[l] + lax.div(col, 2**l)
        total = jnp.zeros((64, 128), F32)
        for k in range(3):
            partner = jnp.where(k < top_count[mine], top_partner[k, mine], -1)
            target = jnp.where(left, first, first + 1)
            total = total + jnp.where(target == partner, gs[3 * l + k], 0.0)
        return total

    def prepare_top():
        wanted = [60 + lax.div(member, 4), 56 + lax.div(member, 2), 48 + member]
        wanted += [32 + 2 * member + i for i in range(2)] + [4 * member + i for i in range(4)]
        wanted += [TOP_OFF[l] + lax.div(col, 2**l) for l in range(5)]

        def pick(rows, n, clusters):
            at = iota((rows, n), 0)
            cluster = at * 0 - 1
            for i, c in enumerate(clusters):
                cluster = jnp.where(at == i, c, cluster)
            return jnp.where(iota((rows, n), 1) == cluster, 1.0, 0.0).astype(BF)

        rows = nn(pick(16, 62, wanted), tt[...])
        for lo in (0, 8):
            matrix = unpack(lambda j: rows[lo : lo + 8, 128 * j : 128 * j + 128])
            for c in range(lo, min(lo + 8, 14)):
                v = matrix(c - lo)
                et[64 * c : 64 * c + 64, :] = on_right(v) if c in (7, 8) else on_left(v) if c < 9 else on_both(v)
        ancestors = pick(8, 63, [TOP_OFF[l] + lax.div(col, 2**l) for l in range(6)])
        for k in range(3):
            rows = nn(ancestors, tc[k])
            matrix = unpack(lambda j: rows[:, 128 * j : 128 * j + 128])
            for l in range(6):
                ts[3 * l + k] = on_both(matrix(l))
        path = None
        for l in range(6):
            for k in range(3):
                s = ts[3 * l + k]
                gs[3 * l + k] = s.astype(F32) if l == 0 else nn(path[:, :64], s)
            if l < 5:
                step = et[(9 + l) * 64 : (10 + l) * 64, :]
                path = step if l == 0 else nn(path[:, :64], step).astype(BF)
        v = seen(5, 62)
        for i, l in enumerate((4, 3, 2)):
            v = nt(v[:, :64].astype(BF), et[64 * i : 64 * i + 64, :64]) + seen(l, wanted[i])[:, :64]
        v = nt(v.astype(BF), et[3 * 64 : 5 * 64, :64]) + seen(1, wanted[3])
        v = nt(v.astype(BF), et[5 * 64 : 9 * 64, :])
        v = v + jnp.concatenate([seen(0, wanted[5]), seen(0, wanted[7])], axis=1)
        zb[...] = v.astype(BF)

    upward()
    pl.semaphore_wait(barrier, jnp.where(source, 42, 15))

    c_q = copy(qb, p1.at[member], S_Q, S_Q + member, column_peer(z))

    @pl.when(jnp.logical_not(source))
    def _():
        c_q.start()

    c_u = [send(ub, gu.at[sub], S_U + d, sub_peers[d]) for d in range(1, 4)]
    gu[sub] = ub[...]
    c_xh = [
        send(xs.at[pl.ds(8, 4)], xs.at[pl.ds(0, 4)], S_XH, after),
        send(xs.at[pl.ds(4, 4)], xs.at[pl.ds(12, 4)], S_XH + 1, before),
    ]
    leaves_own, upper_own = tab.at[pl.ds(16, 8)], tab.at[pl.ds(24, 8)]
    c_leaves = [
        send(leaves_own, tab.at[pl.ds(0, 8)], S_TAB, after),
        send(leaves_own, tab.at[pl.ds(32, 8)], S_TAB + 1, before),
    ]
    c_upper = [
        send(upper_own, tab.at[pl.ds(8, 8)], S_TAB + 2, after),
        send(upper_own, tab.at[pl.ds(40, 8)], S_TAB + 3, before),
    ]

    ready(w_tt)
    ready(w_tc)
    ready(w_top)
    prepare_top()

    c_c = [
        pltpu.make_async_remote_copy(
            src_ref=p3.at[x], dst_ref=p3.at[x], send_sem=csem.at[d], recv_sem=rsem.at[S_C + x],
            device_id=plane_peers[d], device_id_type=MESH,
        )
        for d in range(1, 32)
    ]

    @pl.when(source)
    def _():
        p1[member] = qb[...]
        for m in range(8):

            @pl.when(member != m)
            def _(m=m):
                copy(qb, p1.at[m], S_Q, S_Q + m, col_peers[1]).wait_recv()

        total = p1[0].astype(F32)
        for m in range(1, 8):
            total = total + p1[m].astype(F32)
        p3[x] = total.astype(BF)
        for cp in c_c:
            cp.start()

    def widen(src, dst, lo, n):
        def step(i, carry):
            for h in range(8):
                at = lo + 8 * i + h
                v = src[at]
                r = half_swap(v)
                dst[2 * at] = jnp.concatenate([v * m_left, r * m_right], axis=0)
                dst[2 * at + 1] = jnp.concatenate([r * m_left, v * m_right], axis=0)
            return carry

        lax.fori_loop(0, n, step, 0)

    def spread(load, n):
        tiles = jnp.swapaxes(jnp.stack([load(j).astype(F32) for j in range(32)]), 0, 1)
        even, odd = [], []
        for k in range(0, n, 2):
            one, two = tiles[k], tiles[k + 1]
            even.append(jnp.where(left, one, half_swap(two)))
            odd.append(jnp.where(left, half_swap(one), two))
        rows = [jnp.concatenate(even, axis=1), jnp.concatenate(odd, axis=1)]
        return jnp.concatenate(rows, axis=0).astype(BF)

    def coupled(table, ids, w):
        pairs = [table[ids[k], 0:64, :] + table[ids[k + 1], 64:128, :] for k in range(0, len(ids), 2)]
        return nt(jnp.concatenate(pairs, axis=1), w)

    def in_order(one, two):
        return nn(jnp.concatenate([one, two], axis=1).astype(BF), pp[...])

    ready(w_nb)
    widen(xs, xbd, 4, 1)
    for cp in c_xh:
        cp.wait_recv()
    for at in (0, 12):
        for h in range(4):
            v = xs[at + h]
            r = half_swap(v)
            xbd[2 * (at + h)] = jnp.concatenate([v * m_left, r * m_right], axis=0)
            xbd[2 * (at + h) + 1] = jnp.concatenate([r * m_left, v * m_right], axis=0)

    def near_step(i, carry):
        weights = []
        for h in range(8):
            t = 8 * i + h
            weights.append(spread(lambda j: nb[t, :, 128 * j : 128 * j + 128], 8))
        parts = []
        for h in range(8):
            ids = [jnp.clip(near_list[k, 8 * i + h] - (b * 16 - 8), 0, 31) for k in range(8)]
            parts.append(coupled(xbd, ids, weights[h]))
        for h in range(4):
            nearp[4 * i + h] = in_order(parts[2 * h], parts[2 * h + 1])
        return carry

    lax.fori_loop(0, 2, near_step, 0)

    c_d = [copy(p4.at[member], p4.at[member], S_D + d, S_D + d, col_peers[d]) for d in range(1, 8)]
    for i in range(4):

        @pl.when(jnp.logical_not(source & (x == i)))
        def _(i=i):
            copy(p3.at[i], p3.at[i], S_C, S_C + i, col_peers[1]).wait_recv()

    have = []
    for i in (0, 2):
        up = p3[i] * m_left + half_swap(p3[i + 1]) * m_right
        down = half_swap(p3[i]) * m_left + p3[i + 1] * m_right
        have.append(jnp.concatenate([up, down], axis=0))
    d = nt(jnp.concatenate(have, axis=1), zb[...])
    p4[member] = jnp.concatenate([d[:32], d[32:]], axis=1).astype(BF)
    for cp in c_d:
        cp.start()

    for cp in c_u:
        cp.wait_recv()
    g0 = (gu[0].astype(F32) + gu[1].astype(F32)).astype(BF)
    g1 = (gu[2].astype(F32) + gu[3].astype(F32)).astype(BF)
    g2 = (nn(g0[:, :64], ge[0]) + nn(g1[:, :64], ge[1])).astype(BF)
    gt[3] = g0 + half_swap(g0)
    gt[4] = g1 + half_swap(g1)
    gt[5] = g2
    gt[9] = jnp.zeros((64, 128), BF)
    c_gt = [
        send(gt.at[pl.ds(3, 3)], gt.at[pl.ds(0, 3)], S_GT, g_after),
        send(gt.at[pl.ds(3, 3)], gt.at[pl.ds(6, 3)], S_GT + 1, g_before),
    ]

    ready(w_lc)

    def far_blocks(i, carry):
        for h in range(8):
            c = jnp.minimum(8 * i + h, 30)
            wf[8 * i + h] = spread(lambda j: lc[c, :, 128 * j : 128 * j + 128], 8)
        return carry

    lax.fori_loop(0, 4, far_blocks, 0)

    def far_step(i, carry):
        parts = []
        for h in range(8):
            c = jnp.minimum(8 * i + h, 30)
            count = jnp.where(8 * i + h < 31, local_count[c], 0)
            ids = []
            for k in range(8):
                e = jnp.clip(local_partner[k, c] - (b - 1) * 31, 0, 92)
                e = e + jnp.where(e >= 31, 1, 0) + jnp.where(e >= 62, 1, 0)
                ids.append(jnp.where(k < count, e, 63))
            parts.append(coupled(bdt, ids, wf[8 * i + h]))
        for h in range(4):
            far[4 * i + h] = in_order(parts[2 * h], parts[2 * h + 1])
        return carry

    widen(tab, bdt, 16, 2)
    for cp in c_leaves:
        cp.wait_recv()
    widen(tab, bdt, 0, 1)
    widen(tab, bdt, 32, 1)
    lax.fori_loop(0, 2, far_step, 0)

    ready(w_gc)
    for cp in c_gt:
        cp.wait_recv()
    found = []
    for c in range(3):
        w = spread(lambda j: gc[c, :, 128 * j : 128 * j + 128], 4)
        entries = []
        for k in range(4):
            e = jnp.clip(group_partner[c, k] - (leaf - 1) * 3, 0, 8)
            entries.append(gt[jnp.where(k < group_count[c], e, 9)])
        pairs = [entries[k] * m_left + entries[k + 1] * m_right for k in (0, 2)]
        found.append(nt(jnp.concatenate(pairs, axis=1), w))
    f01 = in_order(found[0], found[1])
    f2 = in_order(found[2], found[2])
    f_half = jnp.where(half == 0, f01, half_swap(f01))[:, :64]
    d_half = f_half + nt(f2[:, :64].astype(BF), ge[half][:, :64])

    for cp in c_upper:
        cp.wait_recv()
    widen(tab, bdt, 8, 1)
    widen(tab, bdt, 40, 1)
    lax.fori_loop(2, 4, far_step, 0)

    e_root = es[30 * 64 : 31 * 64, :]
    d_root = far[15][:, :64] + nt(d_half.astype(BF), e_root[:, :64])
    state = jnp.concatenate([d_root, nt(eye, hr[...][:, :64])], axis=0).astype(BF)
    nothing = jnp.zeros((64, 128), F32)

    def with_far(v, i):
        return (v + jnp.concatenate([far[i], nothing], axis=0)).astype(BF)

    states = [with_far(nt(state, es[28 * 64 : 30 * 64, :64]), 14)]
    for first, pair in ((24, 12), (16, 8), (0, 0)):
        lower_level = []
        for i, parents in enumerate(states):
            at = (first + 4 * i) * 64
            both = nt(parents, es[at : at + 256, :])
            lower_level.append(with_far(both[:, :128], pair + 2 * i))
            lower_level.append(with_far(both[:, 128:], pair + 2 * i + 1))
        states = lower_level
    for m in range(8):
        r = nn(states[m], bd[m])
        nearp[m] = nearp[m] + r[:64]
        vht[m] = r[64:].astype(BF)

    for cp in c_d:
        cp.wait_recv()
    total = p4[0].astype(F32)
    for m in range(1, 8):
        total = total + p4[m].astype(F32)
    d_col = jnp.concatenate([total[:, :64], total[:, 64:]], axis=0).astype(BF)
    for m in range(8):
        out[:, 128 * m : 128 * m + 128] = nearp[m] + nn(d_col, vht[m])

    for cp in c_u + c_xh + c_leaves + c_upper + c_gt + c_d:
        cp.wait_send()

    @pl.when(source)
    def _():
        for cp in c_c:
            cp.wait_send()

    @pl.when(jnp.logical_not(source))
    def _():
        c_q.wait_send()


def body(
    right_sides, leaf_basis, near_blocks, near_list, local_transfer, local_couple, local_partner, local_count,
    group_transfer, group_couple, group_partner, group_count, top_transfer, top_couple, top_partner, top_count,
):
    hbm = pl.BlockSpec(memory_space=pltpu.HBM)
    vm = pltpu.VMEM
    return pl.pallas_call(
        kernel,
        out_shape=jax.ShapeDtypeStruct((64, 1024), F32),
        in_specs=[hbm] * 16,
        out_specs=pl.BlockSpec(memory_space=pltpu.VMEM),
        scratch_shapes=[
            vm((16, 64, 128), BF),
            vm((64, 1024), BF),
            vm((16, 8, 4096), BF),
            vm((31, 4096), BF),
            vm((31, 8, 4096), BF),
            vm((3, 4096), BF),
            vm((3, 4, 4096), BF),
            vm((62, 4096), BF),
            vm((3, 63, 4096), BF),
            vm((31 * 64, 128), BF),
            vm((3, 64, 128), BF),
            vm((16 * 64, 128), BF),
            vm((18, 64, 128), BF),
            vm((32, 64, 512), BF),
            vm((8, 128, 128), BF),
            vm((48, 64, 128), BF),
            vm((96, 128, 128), BF),
            vm((32, 128, 128), BF),
            vm((128, 128), BF),
            vm((32, 128), BF),
            vm((64, 128), BF),
            vm((8, 32, 128), BF),
            vm((4, 32, 128), BF),
            vm((8, 32, 128), BF),
            vm((64, 128), BF),
            vm((4, 64, 128), BF),
            vm((10, 64, 128), BF),
            vm((18, 64, 128), F32),
            vm((64, 256), BF),
            vm((16, 64, 128), F32),
            vm((8, 64, 128), F32),
            vm((8, 64, 128), BF),
            pltpu.SMEM((8, 16), jnp.int32),
            pltpu.SMEM((8, 31), jnp.int32),
            pltpu.SMEM((31,), jnp.int32),
            pltpu.SMEM((3, 4), jnp.int32),
            pltpu.SMEM((3,), jnp.int32),
            pltpu.SMEM((3, 63), jnp.int32),
            pltpu.SMEM((63,), jnp.int32),
            pltpu.SemaphoreType.DMA((24,)),
            pltpu.SemaphoreType.DMA((N_SEM,)),
            pltpu.SemaphoreType.DMA((N_SEM,)),
            pltpu.SemaphoreType.DMA((32,)),
        ],
        compiler_params=pltpu.CompilerParams(
            collective_id=0, has_side_effects=True, vmem_limit_bytes=48 * 1024 * 1024
        ),
        name="h2",
    )(
        *[pltpu.with_memory_space_constraint(v, pltpu.HBM) for v in (
        near_list.T, local_partner.T, local_count, group_partner, group_count, top_partner.T, top_count,
        right_sides, leaf_basis, near_blocks, local_transfer, local_couple, group_transfer, group_couple,
        top_transfer, jnp.transpose(top_couple, (1, 0, 2)),
        )],
    )


def solution(mesh):
    both = ("leaf", "sub")
    placed = (
        P(None, both), P(None, both), P(both, None, None), P(both, None), P(both, None), P(both, None, None),
        P(both, None), P(both), P("leaf", None), P("leaf", None, None), P("leaf", None), P("leaf"),
        P(), P(), P(), P(),
    )
    return jax.shard_map(body, mesh=mesh, in_specs=placed, out_specs=P(None, both), check_vma=False)
```

```python
import functools

import jax
import jax.numpy as jnp
from jax import lax
from jax.experimental import pallas as pl
from jax.experimental.pallas import tpu as pltpu
from jax.sharding import PartitionSpec as P

BF = jnp.bfloat16
F32 = jnp.float32
MESH = pl.DeviceIdType.MESH
TOP_OFF = (0, 32, 48, 56, 60, 62)
S_Q, S_C, S_D, S_U, S_XH, S_TAB, S_GT, N_SEM = 0, 8, 12, 20, 24, 26, 30, 32


def nt(a, b):
    return lax.dot_general(a, b, (((1,), (1,)), ((), ())), preferred_element_type=F32)


def nn(a, b):
    return jnp.dot(a, b, preferred_element_type=F32)


def half_swap(v):
    return pltpu.roll(v, 64, 1)


def iota(shape, dim):
    return lax.broadcasted_iota(jnp.int32, shape, dim)


def kernel(
    near_list_hbm, local_partner_hbm, local_count_hbm, group_partner_hbm, group_count_hbm, top_partner_hbm,
    top_count_hbm, x_hbm, basis_hbm, near_hbm, ltrans_hbm, lcouple_hbm, gtrans_hbm, gcouple_hbm, ttrans_hbm, tcouple_hbm,
    out,
    xs, bs, nb, lt, lc, gt_in, gc, tt, tc,
    es, ge, et, ts, wf, bd, tab, bdt, xbd, pp,
    qb, hr, p1, p3, p4, ub, gu, gt, gs, zb, far, nearp, vht,
    near_list, local_partner, local_count, group_partner, group_count, top_partner, top_count,
    lsem, ssem, rsem, csem,
):
    leaf = lax.axis_index("leaf")
    sub = lax.axis_index("sub")
    col, ylo = lax.div(leaf, 2), lax.rem(leaf, 2)
    z, x = lax.div(col, 4), lax.rem(col, 4)
    member = ylo * 4 + sub
    b = leaf * 4 + sub
    half = lax.div(sub, 2)

    source = member == z

    def column_peer(m):
        return (col * 2 + lax.div(m, 4), lax.rem(m, 4))

    def ring_peer(step):
        n = lax.rem(b + step, 256)
        return (lax.div(n, 4), lax.rem(n, 4))

    col_peers = [column_peer(lax.rem(member + d, 8)) for d in range(8)]
    plane_peers = [(lax.rem(col + d, 32) * 2 + ylo, sub) for d in range(32)]
    plane_sources = [((member * 4 + i) * 2 + ylo, sub) for i in range(4)]
    sub_peers = [(leaf, lax.rem(sub + d, 4)) for d in range(4)]
    after, before = ring_peer(1), ring_peer(255)
    g_after = (lax.rem(leaf + 1, 64), sub)
    g_before = (lax.rem(leaf + 63, 64), sub)

    local = []

    def fetch(src, dst):
        cp = pltpu.make_async_copy(src, dst, lsem.at[len(local)])
        cp.start()
        local.append(cp)
        return cp

    w_x = [fetch(x_hbm.at[:, pl.ds(128 * m, 128)], xs.at[4 + m]) for m in range(8)]
    w_b = [fetch(basis_hbm, bs)]
    w_lt = [fetch(ltrans_hbm, lt)]
    w_gt = [fetch(gtrans_hbm, gt_in)]
    w_tt = [fetch(ttrans_hbm, tt)]
    w_tc = [fetch(tcouple_hbm, tc)]
    w_top = [fetch(top_partner_hbm, top_partner), fetch(top_count_hbm, top_count)]
    w_nb = [fetch(near_hbm, nb), fetch(near_list_hbm, near_list)]
    w_lc = [fetch(lcouple_hbm, lc), fetch(local_partner_hbm, local_partner), fetch(local_count_hbm, local_count)]
    w_gc = [fetch(gcouple_hbm, gc), fetch(group_partner_hbm, group_partner), fetch(group_count_hbm, group_count)]

    def ready(copies):
        for cp in copies:
            cp.wait()

    barrier = pltpu.get_barrier_semaphore()
    def greet(peers):
        for peer in peers:
            pl.semaphore_signal(barrier, inc=1, device_id=peer, device_id_type=MESH)

    greet(col_peers[1:] + [after, before, g_after, g_before])

    @pl.when(source)
    def _():
        greet(plane_peers[1:])

    @pl.when(jnp.logical_not(source))
    def _():
        greet(plane_sources)

    def copy(src, dst, sent, got, peer):
        return pltpu.make_async_remote_copy(
            src_ref=src, dst_ref=dst, send_sem=ssem.at[sent], recv_sem=rsem.at[got],
            device_id=peer, device_id_type=MESH,
        )

    def send(src, dst, place, peer):
        cp = copy(src, dst, place, place, peer)
        cp.start()
        return cp

    lane = iota((1, 128), 1)
    left = lane < 64
    m_left = jnp.where(left, 1.0, 0.0).astype(BF)
    m_right = jnp.where(left, 0.0, 1.0).astype(BF)
    row, column = iota((128, 128), 0), iota((128, 128), 1)
    from_row = lax.div(row, 64) * 64 + 2 * lax.rem(row, 32) + lax.div(lax.rem(row, 64), 32)
    pp[...] = jnp.where(column == from_row, 1.0, 0.0).astype(BF)
    eye = jnp.where(iota((64, 64), 0) == iota((64, 64), 1), 1.0, 0.0).astype(BF)

    def unpack(load):
        parts = []
        for lo in (0, 16):
            tiles = []
            for j in range(lo, lo + 16):
                v = load(j)
                tiles += [v, half_swap(v)]
            parts.append(jnp.swapaxes(jnp.stack(tiles), 0, 1))
        return lambda c: jnp.concatenate([part[c] for part in parts], axis=0).astype(BF)

    def filled(v):
        v = v.astype(F32)
        if v.shape[0] == 8:
            return v
        return jnp.concatenate([v, jnp.zeros((8 - v.shape[0], 128), F32)], axis=0)

    def on_left(v):
        return v * m_left

    def on_right(v):
        return half_swap(v * m_left)

    def on_both(v):
        return on_left(v) + on_right(v)

    ready(w_x)
    ready(w_b)
    for m in range(8):
        two = bs[:, 128 * m : 128 * m + 128]
        both = jnp.concatenate([two * m_left, two * m_right], axis=0)
        bd[m] = both
        tab[16 + m] = nt(xs[4 + m], both).astype(BF)
    ready(w_lt)
    ready(w_gt)

    def upward():
        for lo in range(0, 31, 8):
            hi = min(lo + 8, 31)
            matrix = unpack(lambda j: filled(lt[lo:hi, 128 * j : 128 * j + 128]))
            for c in range(lo, hi):
                right = c < 30 and (c // 2) % 2 == 1
                v = matrix(c - lo)
                es[64 * c : 64 * c + 64, :] = on_right(v) if right else on_left(v)
        matrix = unpack(lambda j: filled(gt_in[:, 128 * j : 128 * j + 128]))
        for c in range(3):
            ge[c] = on_both(matrix(c))
        e_root = es[30 * 64 : 31 * 64, :]
        pair_down = nn(ge[half][:, :64], ge[2]).astype(BF)
        h_root = nn(e_root[:, :64], pair_down).astype(BF)
        hr[...] = h_root
        for lo, hi, n in ((16, 24, 4), (24, 28, 2), (28, 30, 1)):
            for i in range(n):
                kids = jnp.concatenate([tab[lo + 2 * i], tab[lo + 2 * i + 1]], axis=1)
                first = 2 * (lo - 16) + 4 * i
                tab[hi + i] = nn(kids, es[first * 64 : first * 64 + 256, :]).astype(BF)
        c_root = nn(tab[30], es[28 * 64 : 30 * 64, :]).astype(BF)
        tab[31] = c_root
        q = nn(c_root[:, :64], h_root)
        qb[...] = jnp.where(left, q[:32], q[32:]).astype(BF)
        ub[...] = nn(c_root[:, :64], e_root).astype(BF)

    def seen(l, first):
        mine = TOP_OFF[l] + lax.div(col, 2**l)
        total = jnp.zeros((64, 128), F32)
        for k in range(3):
            partner = jnp.where(k < top_count[mine], top_partner[k, mine], -1)
            target = jnp.where(left, first, first + 1)
            total = total + jnp.where(target == partner, gs[3 * l + k], 0.0)
        return total

    def prepare_top():
        wanted = [60 + lax.div(member, 4), 56 + lax.div(member, 2), 48 + member]
        wanted += [32 + 2 * member + i for i in range(2)] + [4 * member + i for i in range(4)]
        wanted += [TOP_OFF[l] + lax.div(col, 2**l) for l in range(5)]

        def pick(rows, n, clusters):
            at = iota((rows, n), 0)
            cluster = at * 0 - 1
            for i, c in enumerate(clusters):
                cluster = jnp.where(at == i, c, cluster)
            return jnp.where(iota((rows, n), 1) == cluster, 1.0, 0.0).astype(BF)

        rows = nn(pick(16, 62, wanted), tt[...])
        for lo in (0, 8):
            matrix = unpack(lambda j: rows[lo : lo + 8, 128 * j : 128 * j + 128])
            for c in range(lo, min(lo + 8, 14)):
                v = matrix(c - lo)
                et[64 * c : 64 * c + 64, :] = on_right(v) if c in (7, 8) else on_left(v) if c < 9 else on_both(v)
        ancestors = pick(8, 63, [TOP_OFF[l] + lax.div(col, 2**l) for l in range(6)])
        for k in range(3):
            rows = nn(ancestors, tc[k])
            matrix = unpack(lambda j: rows[:, 128 * j : 128 * j + 128])
            for l in range(6):
                ts[3 * l + k] = on_both(matrix(l))
        path = None
        for l in range(6):
            for k in range(3):
                s = ts[3 * l + k]
                gs[3 * l + k] = s.astype(F32) if l == 0 else nn(path[:, :64], s)
            if l < 5:
                step = et[(9 + l) * 64 : (10 + l) * 64, :]
                path = step if l == 0 else nn(path[:, :64], step).astype(BF)
        v = seen(5, 62)
        for i, l in enumerate((4, 3, 2)):
            v = nt(v[:, :64].astype(BF), et[64 * i : 64 * i + 64, :64]) + seen(l, wanted[i])[:, :64]
        v = nt(v.astype(BF), et[3 * 64 : 5 * 64, :64]) + seen(1, wanted[3])
        v = nt(v.astype(BF), et[5 * 64 : 9 * 64, :])
        v = v + jnp.concatenate([seen(0, wanted[5]), seen(0, wanted[7])], axis=1)
        zb[...] = v.astype(BF)

    upward()
    pl.semaphore_wait(barrier, jnp.where(source, 42, 15))

    c_q = copy(qb, p1.at[member], S_Q, S_Q + member, column_peer(z))

    @pl.when(jnp.logical_not(source))
    def _():
        c_q.start()

    c_u = [send(ub, gu.at[sub], S_U + d, sub_peers[d]) for d in range(1, 4)]
    gu[sub] = ub[...]

    def exchange(ref, to_after, to_before, n, from_before, from_after, place):
        copies = []
        for turn in range(2):
            back = lax.rem(sub, 2) == 1 - turn
            cp = copy(
                ref.at[pl.ds(jnp.where(back, to_before, to_after), n)],
                ref.at[pl.ds(jnp.where(back, from_after, from_before), n)],
                place + turn,
                place + jnp.where(back, 1, 0),
                tuple(jnp.where(back, a, c) for a, c in zip(before, after)),
            )
            cp.start()
            copies.append(cp)
        return copies

    c_xh = exchange(xs, 8, 4, 4, 0, 12, S_XH)
    c_leaves = exchange(tab, 16, 16, 8, 0, 32, S_TAB)
    c_upper = exchange(tab, 24, 24, 8, 8, 40, S_TAB + 2)

    ready(w_tt)
    ready(w_tc)
    ready(w_top)
    prepare_top()

    c_c = [
        pltpu.make_async_remote_copy(
            src_ref=p3.at[x], dst_ref=p3.at[x], send_sem=csem.at[d], recv_sem=rsem.at[S_C + x],
            device_id=plane_peers[d], device_id_type=MESH,
        )
        for d in range(1, 32)
    ]

    @pl.when(source)
    def _():
        p1[member] = qb[...]
        for m in range(8):

            @pl.when(member != m)
            def _(m=m):
                copy(qb, p1.at[m], S_Q, S_Q + m, col_peers[1]).wait_recv()

        total = p1[0].astype(F32)
        for m in range(1, 8):
            total = total + p1[m].astype(F32)
        p3[x] = total.astype(BF)
        for cp in c_c:
            cp.start()

    def widen(src, dst, lo, n):
        def step(i, carry):
            for h in range(8):
                at = lo + 8 * i + h
                v = src[at]
                r = half_swap(v)
                dst[2 * at] = jnp.concatenate([v * m_left, r * m_right], axis=0)
                dst[2 * at + 1] = jnp.concatenate([r * m_left, v * m_right], axis=0)
            return carry

        lax.fori_loop(0, n, step, 0)

    def spread(load, n):
        tiles = jnp.swapaxes(jnp.stack([load(j).astype(F32) for j in range(32)]), 0, 1)
        even, odd = [], []
        for k in range(0, n, 2):
            one, two = tiles[k], tiles[k + 1]
            even.append(jnp.where(left, one, half_swap(two)))
            odd.append(jnp.where(left, half_swap(one), two))
        rows = [jnp.concatenate(even, axis=1), jnp.concatenate(odd, axis=1)]
        return jnp.concatenate(rows, axis=0).astype(BF)

    def coupled(table, ids, w):
        pairs = [table[ids[k], 0:64, :] + table[ids[k + 1], 64:128, :] for k in range(0, len(ids), 2)]
        return nt(jnp.concatenate(pairs, axis=1), w)

    def in_order(one, two):
        return nn(jnp.concatenate([one, two], axis=1).astype(BF), pp[...])

    ready(w_nb)
    widen(xs, xbd, 4, 1)
    for cp in c_xh:
        cp.wait_recv()
    for at in (0, 12):
        for h in range(4):
            v = xs[at + h]
            r = half_swap(v)
            xbd[2 * (at + h)] = jnp.concatenate([v * m_left, r * m_right], axis=0)
            xbd[2 * (at + h) + 1] = jnp.concatenate([r * m_left, v * m_right], axis=0)

    def near_step(i, carry):
        weights = []
        for h in range(8):
            t = 8 * i + h
            weights.append(spread(lambda j: nb[t, :, 128 * j : 128 * j + 128], 8))
        parts = []
        for h in range(8):
            ids = [jnp.clip(near_list[k, 8 * i + h] - (b * 16 - 8), 0, 31) for k in range(8)]
            parts.append(coupled(xbd, ids, weights[h]))
        for h in range(4):
            nearp[4 * i + h] = in_order(parts[2 * h], parts[2 * h + 1])
        return carry

    lax.fori_loop(0, 2, near_step, 0)

    c_d = [copy(p4.at[member], p4.at[member], S_D + d, S_D + d, col_peers[d]) for d in range(1, 8)]
    for i in range(4):

        @pl.when(jnp.logical_not(source & (x == i)))
        def _(i=i):
            copy(p3.at[i], p3.at[i], S_C, S_C + i, col_peers[1]).wait_recv()

    have = []
    for i in (0, 2):
        up = p3[i] * m_left + half_swap(p3[i + 1]) * m_right
        down = half_swap(p3[i]) * m_left + p3[i + 1] * m_right
        have.append(jnp.concatenate([up, down], axis=0))
    d = nt(jnp.concatenate(have, axis=1), zb[...])
    p4[member] = jnp.concatenate([d[:32], d[32:]], axis=1).astype(BF)
    for cp in c_d:
        cp.start()

    for cp in c_u:
        cp.wait_recv()
    g0 = (gu[0].astype(F32) + gu[1].astype(F32)).astype(BF)
    g1 = (gu[2].astype(F32) + gu[3].astype(F32)).astype(BF)
    g2 = (nn(g0[:, :64], ge[0]) + nn(g1[:, :64], ge[1])).astype(BF)
    gt[3] = g0 + half_swap(g0)
    gt[4] = g1 + half_swap(g1)
    gt[5] = g2
    gt[9] = jnp.zeros((64, 128), BF)
    c_gt = [
        send(gt.at[pl.ds(3, 3)], gt.at[pl.ds(0, 3)], S_GT, g_after),
        send(gt.at[pl.ds(3, 3)], gt.at[pl.ds(6, 3)], S_GT + 1, g_before),
    ]

    ready(w_lc)

    def far_blocks(i, carry):
        for h in range(8):
            c = jnp.minimum(8 * i + h, 30)
            wf[8 * i + h] = spread(lambda j: lc[c, :, 128 * j : 128 * j + 128], 8)
        return carry

    lax.fori_loop(0, 4, far_blocks, 0)

    def far_step(i, carry):
        parts = []
        for h in range(8):
            c = jnp.minimum(8 * i + h, 30)
            count = jnp.where(8 * i + h < 31, local_count[c], 0)
            ids = []
            for k in range(8):
                e = jnp.clip(local_partner[k, c] - (b - 1) * 31, 0, 92)
                e = e + jnp.where(e >= 31, 1, 0) + jnp.where(e >= 62, 1, 0)
                ids.append(jnp.where(k < count, e, 63))
            parts.append(coupled(bdt, ids, wf[8 * i + h]))
        for h in range(4):
            far[4 * i + h] = in_order(parts[2 * h], parts[2 * h + 1])
        return carry

    widen(tab, bdt, 16, 2)
    for cp in c_leaves:
        cp.wait_recv()
    widen(tab, bdt, 0, 1)
    widen(tab, bdt, 32, 1)
    lax.fori_loop(0, 2, far_step, 0)

    ready(w_gc)
    for cp in c_gt:
        cp.wait_recv()
    found = []
    for c in range(3):
        w = spread(lambda j: gc[c, :, 128 * j : 128 * j + 128], 4)
        entries = []
        for k in range(4):
            e = jnp.clip(group_partner[c, k] - (leaf - 1) * 3, 0, 8)
            entries.append(gt[jnp.where(k < group_count[c], e, 9)])
        pairs = [entries[k] * m_left + entries[k + 1] * m_right for k in (0, 2)]
        found.append(nt(jnp.concatenate(pairs, axis=1), w))
    f01 = in_order(found[0], found[1])
    f2 = in_order(found[2], found[2])
    f_half = jnp.where(half == 0, f01, half_swap(f01))[:, :64]
    d_half = f_half + nt(f2[:, :64].astype(BF), ge[half][:, :64])

    for cp in c_upper:
        cp.wait_recv()
    widen(tab, bdt, 8, 1)
    widen(tab, bdt, 40, 1)
    lax.fori_loop(2, 4, far_step, 0)

    e_root = es[30 * 64 : 31 * 64, :]
    d_root = far[15][:, :64] + nt(d_half.astype(BF), e_root[:, :64])
    state = jnp.concatenate([d_root, nt(eye, hr[...][:, :64])], axis=0).astype(BF)
    nothing = jnp.zeros((64, 128), F32)

    def with_far(v, i):
        return (v + jnp.concatenate([far[i], nothing], axis=0)).astype(BF)

    states = [with_far(nt(state, es[28 * 64 : 30 * 64, :64]), 14)]
    for first, pair in ((24, 12), (16, 8), (0, 0)):
        lower_level = []
        for i, parents in enumerate(states):
            at = (first + 4 * i) * 64
            both = nt(parents, es[at : at + 256, :])
            lower_level.append(with_far(both[:, :128], pair + 2 * i))
            lower_level.append(with_far(both[:, 128:], pair + 2 * i + 1))
        states = lower_level
    for m in range(8):
        r = nn(states[m], bd[m])
        nearp[m] = nearp[m] + r[:64]
        vht[m] = r[64:].astype(BF)

    for cp in c_d:
        cp.wait_recv()
    total = p4[0].astype(F32)
    for m in range(1, 8):
        total = total + p4[m].astype(F32)
    d_col = jnp.concatenate([total[:, :64], total[:, 64:]], axis=0).astype(BF)
    for m in range(8):
        out[:, 128 * m : 128 * m + 128] = nearp[m] + nn(d_col, vht[m])

    for cp in c_u + c_xh + c_leaves + c_upper + c_gt + c_d:
        cp.wait_send()

    @pl.when(source)
    def _():
        for cp in c_c:
            cp.wait_send()

    @pl.when(jnp.logical_not(source))
    def _():
        c_q.wait_send()


def body(
    right_sides, leaf_basis, near_blocks, near_list, local_transfer, local_couple, local_partner, local_count,
    group_transfer, group_couple, group_partner, group_count, top_transfer, top_couple, top_partner, top_count,
):
    hbm = pl.BlockSpec(memory_space=pltpu.HBM)
    vm = pltpu.VMEM
    return pl.pallas_call(
        kernel,
        out_shape=jax.ShapeDtypeStruct((64, 1024), F32),
        in_specs=[hbm] * 16,
        out_specs=pl.BlockSpec(memory_space=pltpu.VMEM),
        scratch_shapes=[
            vm((16, 64, 128), BF),
            vm((64, 1024), BF),
            vm((16, 8, 4096), BF),
            vm((31, 4096), BF),
            vm((31, 8, 4096), BF),
            vm((3, 4096), BF),
            vm((3, 4, 4096), BF),
            vm((62, 4096), BF),
            vm((3, 63, 4096), BF),
            vm((31 * 64, 128), BF),
            vm((3, 64, 128), BF),
            vm((16 * 64, 128), BF),
            vm((18, 64, 128), BF),
            vm((32, 64, 512), BF),
            vm((8, 128, 128), BF),
            vm((48, 64, 128), BF),
            vm((96, 128, 128), BF),
            vm((32, 128, 128), BF),
            vm((128, 128), BF),
            vm((32, 128), BF),
            vm((64, 128), BF),
            vm((8, 32, 128), BF),
            vm((4, 32, 128), BF),
            vm((8, 32, 128), BF),
            vm((64, 128), BF),
            vm((4, 64, 128), BF),
            vm((10, 64, 128), BF),
            vm((18, 64, 128), F32),
            vm((64, 256), BF),
            vm((16, 64, 128), F32),
            vm((8, 64, 128), F32),
            vm((8, 64, 128), BF),
            pltpu.SMEM((8, 16), jnp.int32),
            pltpu.SMEM((8, 31), jnp.int32),
            pltpu.SMEM((31,), jnp.int32),
            pltpu.SMEM((3, 4), jnp.int32),
            pltpu.SMEM((3,), jnp.int32),
            pltpu.SMEM((3, 63), jnp.int32),
            pltpu.SMEM((63,), jnp.int32),
            pltpu.SemaphoreType.DMA((24,)),
            pltpu.SemaphoreType.DMA((N_SEM,)),
            pltpu.SemaphoreType.DMA((N_SEM,)),
            pltpu.SemaphoreType.DMA((32,)),
        ],
        compiler_params=pltpu.CompilerParams(
            collective_id=0, has_side_effects=True, vmem_limit_bytes=48 * 1024 * 1024
        ),
        name="h2",
    )(
        *[pltpu.with_memory_space_constraint(v, pltpu.HBM) for v in (
        near_list.T, local_partner.T, local_count, group_partner, group_count, top_partner.T, top_count,
        right_sides, leaf_basis, near_blocks, local_transfer, local_couple, group_transfer, group_couple,
        top_transfer, jnp.transpose(top_couple, (1, 0, 2)),
        )],
    )


def solution(mesh):
    both = ("leaf", "sub")
    placed = (
        P(None, both), P(None, both), P(both, None, None), P(both, None), P(both, None), P(both, None, None),
        P(both, None), P(both), P("leaf", None), P("leaf", None, None), P("leaf", None), P("leaf"),
        P(), P(), P(), P(),
    )
    return jax.shard_map(body, mesh=mesh, in_specs=placed, out_specs=P(None, both), check_vma=False)
```

```python
import functools

import jax
import jax.numpy as jnp
from jax import lax
from jax.experimental import pallas as pl
from jax.experimental.pallas import tpu as pltpu
from jax.sharding import PartitionSpec as P

BF = jnp.bfloat16
F32 = jnp.float32
MESH = pl.DeviceIdType.MESH
TOP_OFF = (0, 32, 48, 56, 60, 62)
S_Q, S_C, S_D, S_U, S_XH, S_TAB, S_GT, N_SEM = 0, 8, 12, 20, 24, 26, 30, 32


def nt(a, b):
    return lax.dot_general(a, b, (((1,), (1,)), ((), ())), preferred_element_type=F32)


def nn(a, b):
    return jnp.dot(a, b, preferred_element_type=F32)


def half_swap(v):
    return pltpu.roll(v, 64, 1)


def iota(shape, dim):
    return lax.broadcasted_iota(jnp.int32, shape, dim)


def kernel(
    near_list_hbm, local_partner_hbm, local_count_hbm, group_partner_hbm, group_count_hbm, top_partner_hbm,
    top_count_hbm, x_hbm, basis_hbm, near_hbm, ltrans_hbm, lcouple_hbm, gtrans_hbm, gcouple_hbm, ttrans_hbm, tcouple_hbm,
    out,
    xs, bs, nb, lt, lc, gt_in, gc, tt, tc,
    es, ge, et, ts, wf, bd, tab, bdt, xbd, pp,
    qb, hr, p1, p3, p4, ub, gu, gt, gs, zb, far, nearp, vht,
    near_list, local_partner, local_count, group_partner, group_count, top_partner, top_count,
    lsem, ssem, rsem, csem,
):
    leaf = lax.axis_index("leaf")
    sub = lax.axis_index("sub")
    col, ylo = lax.div(leaf, 2), lax.rem(leaf, 2)
    z, x = lax.div(col, 4), lax.rem(col, 4)
    member = ylo * 4 + sub
    b = leaf * 4 + sub
    half = lax.div(sub, 2)

    source = member == z

    def column_peer(m):
        return (col * 2 + lax.div(m, 4), lax.rem(m, 4))

    def ring_peer(step):
        n = lax.rem(b + step, 256)
        return (lax.div(n, 4), lax.rem(n, 4))

    col_peers = [column_peer(lax.rem(member + d, 8)) for d in range(8)]
    plane_peers = [(lax.rem(col + d, 32) * 2 + ylo, sub) for d in range(32)]
    plane_sources = [((member * 4 + i) * 2 + ylo, sub) for i in range(4)]
    sub_peers = [(leaf, lax.rem(sub + d, 4)) for d in range(4)]
    after, before = ring_peer(1), ring_peer(255)
    g_after = (lax.rem(leaf + 1, 64), sub)
    g_before = (lax.rem(leaf + 63, 64), sub)

    local = []

    def fetch(src, dst):
        cp = pltpu.make_async_copy(src, dst, lsem.at[len(local)])
        cp.start()
        local.append(cp)
        return cp

    w_x = [fetch(x_hbm.at[:, pl.ds(128 * m, 128)], xs.at[4 + m]) for m in range(8)]
    w_b = [fetch(basis_hbm, bs)]
    w_lt = [fetch(ltrans_hbm, lt)]
    w_gt = [fetch(gtrans_hbm, gt_in)]
    w_tt = [fetch(ttrans_hbm, tt)]
    w_tc = [fetch(tcouple_hbm, tc)]
    w_top = [fetch(top_partner_hbm, top_partner), fetch(top_count_hbm, top_count)]
    w_nb = [fetch(near_hbm, nb), fetch(near_list_hbm, near_list)]
    w_lc = [fetch(lcouple_hbm, lc), fetch(local_partner_hbm, local_partner), fetch(local_count_hbm, local_count)]
    w_gc = [fetch(gcouple_hbm, gc), fetch(group_partner_hbm, group_partner), fetch(group_count_hbm, group_count)]

    def ready(copies):
        for cp in copies:
            cp.wait()

    barrier = pltpu.get_barrier_semaphore()
    def greet(peers):
        for peer in peers:
            pl.semaphore_signal(barrier, inc=1, device_id=peer, device_id_type=MESH)

    greet(col_peers[1:] + [after, before, g_after, g_before])

    @pl.when(source)
    def _():
        greet(plane_peers[1:])

    @pl.when(jnp.logical_not(source))
    def _():
        greet(plane_sources)

    def copy(src, dst, sent, got, peer):
        return pltpu.make_async_remote_copy(
            src_ref=src, dst_ref=dst, send_sem=ssem.at[sent], recv_sem=rsem.at[got],
            device_id=peer, device_id_type=MESH,
        )

    def send(src, dst, place, peer):
        cp = copy(src, dst, place, place, peer)
        cp.start()
        return cp

    lane = iota((1, 128), 1)
    left = lane < 64
    m_left = jnp.where(left, 1.0, 0.0).astype(BF)
    m_right = jnp.where(left, 0.0, 1.0).astype(BF)
    row, column = iota((128, 128), 0), iota((128, 128), 1)
    from_row = lax.div(row, 64) * 64 + 2 * lax.rem(row, 32) + lax.div(lax.rem(row, 64), 32)
    pp[...] = jnp.where(column == from_row, 1.0, 0.0).astype(BF)
    eye = jnp.where(iota((64, 64), 0) == iota((64, 64), 1), 1.0, 0.0).astype(BF)

    def unpack(load):
        parts = []
        for lo in (0, 16):
            tiles = []
            for j in range(lo, lo + 16):
                v = load(j)
                tiles += [v, half_swap(v)]
            parts.append(jnp.swapaxes(jnp.stack(tiles), 0, 1))
        return lambda c: jnp.concatenate([part[c] for part in parts], axis=0).astype(BF)

    def filled(v):
        v = v.astype(F32)
        if v.shape[0] == 8:
            return v
        return jnp.concatenate([v, jnp.zeros((8 - v.shape[0], 128), F32)], axis=0)

    def on_left(v):
        return v * m_left

    def on_right(v):
        return half_swap(v * m_left)

    def on_both(v):
        return on_left(v) + on_right(v)

    ready(w_x)
    ready(w_b)
    for m in range(8):
        two = bs[:, 128 * m : 128 * m + 128]
        both = jnp.concatenate([two * m_left, two * m_right], axis=0)
        bd[m] = both
        tab[16 + m] = nt(xs[4 + m], both).astype(BF)
    ready(w_lt)
    ready(w_gt)

    def upward():
        for lo in range(0, 31, 8):
            hi = min(lo + 8, 31)
            matrix = unpack(lambda j: filled(lt[lo:hi, 128 * j : 128 * j + 128]))
            for c in range(lo, hi):
                right = c < 30 and (c // 2) % 2 == 1
                v = matrix(c - lo)
                es[64 * c : 64 * c + 64, :] = on_right(v) if right else on_left(v)
        matrix = unpack(lambda j: filled(gt_in[:, 128 * j : 128 * j + 128]))
        for c in range(3):
            ge[c] = on_both(matrix(c))
        e_root = es[30 * 64 : 31 * 64, :]
        pair_down = nn(ge[half][:, :64], ge[2]).astype(BF)
        h_root = nn(e_root[:, :64], pair_down).astype(BF)
        hr[...] = h_root
        for lo, hi, n in ((16, 24, 4), (24, 28, 2), (28, 30, 1)):
            for i in range(n):
                kids = jnp.concatenate([tab[lo + 2 * i], tab[lo + 2 * i + 1]], axis=1)
                first = 2 * (lo - 16) + 4 * i
                tab[hi + i] = nn(kids, es[first * 64 : first * 64 + 256, :]).astype(BF)
        c_root = nn(tab[30], es[28 * 64 : 30 * 64, :]).astype(BF)
        tab[31] = c_root
        q = nn(c_root[:, :64], h_root)
        qb[...] = jnp.where(left, q[:32], q[32:]).astype(BF)
        ub[...] = nn(c_root[:, :64], e_root).astype(BF)

    def seen(l, first):
        mine = TOP_OFF[l] + lax.div(col, 2**l)
        total = jnp.zeros((64, 128), F32)
        for k in range(3):
            partner = jnp.where(k < top_count[mine], top_partner[k, mine], -1)
            target = jnp.where(left, first, first + 1)
            total = total + jnp.where(target == partner, gs[3 * l + k], 0.0)
        return total

    def prepare_top():
        wanted = [60 + lax.div(member, 4), 56 + lax.div(member, 2), 48 + member]
        wanted += [32 + 2 * member + i for i in range(2)] + [4 * member + i for i in range(4)]
        wanted += [TOP_OFF[l] + lax.div(col, 2**l) for l in range(5)]

        def pick(rows, n, clusters):
            at = iota((rows, n), 0)
            cluster = at * 0 - 1
            for i, c in enumerate(clusters):
                cluster = jnp.where(at == i, c, cluster)
            return jnp.where(iota((rows, n), 1) == cluster, 1.0, 0.0).astype(BF)

        rows = nn(pick(16, 62, wanted), tt[...])
        for lo in (0, 8):
            matrix = unpack(lambda j: rows[lo : lo + 8, 128 * j : 128 * j + 128])
            for c in range(lo, min(lo + 8, 14)):
                v = matrix(c - lo)
                et[64 * c : 64 * c + 64, :] = on_right(v) if c in (7, 8) else on_left(v) if c < 9 else on_both(v)
        ancestors = pick(8, 63, [TOP_OFF[l] + lax.div(col, 2**l) for l in range(6)])
        for k in range(3):
            rows = nn(ancestors, tc[k])
            matrix = unpack(lambda j: rows[:, 128 * j : 128 * j + 128])
            for l in range(6):
                ts[3 * l + k] = on_both(matrix(l))
        path = None
        for l in range(6):
            for k in range(3):
                s = ts[3 * l + k]
                gs[3 * l + k] = s.astype(F32) if l == 0 else nn(path[:, :64], s)
            if l < 5:
                step = et[(9 + l) * 64 : (10 + l) * 64, :]
                path = step if l == 0 else nn(path[:, :64], step).astype(BF)
        v = seen(5, 62)
        for i, l in enumerate((4, 3, 2)):
            v = nt(v[:, :64].astype(BF), et[64 * i : 64 * i + 64, :64]) + seen(l, wanted[i])[:, :64]
        v = nt(v.astype(BF), et[3 * 64 : 5 * 64, :64]) + seen(1, wanted[3])
        v = nt(v.astype(BF), et[5 * 64 : 9 * 64, :])
        v = v + jnp.concatenate([seen(0, wanted[5]), seen(0, wanted[7])], axis=1)
        zb[...] = v.astype(BF)

    upward()
    pl.semaphore_wait(barrier, jnp.where(source, 42, 15))

    c_q = copy(qb, p1.at[member], S_Q, S_Q + member, column_peer(z))

    @pl.when(jnp.logical_not(source))
    def _():
        c_q.start()

    c_u = [send(ub, gu.at[sub], S_U + d, sub_peers[d]) for d in range(1, 4)]
    gu[sub] = ub[...]
    c_xh = [
        send(xs.at[pl.ds(8, 4)], xs.at[pl.ds(0, 4)], S_XH, after),
        send(xs.at[pl.ds(4, 4)], xs.at[pl.ds(12, 4)], S_XH + 1, before),
    ]
    leaves_own, upper_own = tab.at[pl.ds(16, 8)], tab.at[pl.ds(24, 8)]
    c_leaves = [
        send(leaves_own, tab.at[pl.ds(0, 8)], S_TAB, after),
        send(leaves_own, tab.at[pl.ds(32, 8)], S_TAB + 1, before),
    ]
    c_upper = [
        send(upper_own, tab.at[pl.ds(8, 8)], S_TAB + 2, after),
        send(upper_own, tab.at[pl.ds(40, 8)], S_TAB + 3, before),
    ]

    ready(w_tt)
    ready(w_tc)
    ready(w_top)
    prepare_top()

    c_c = [
        pltpu.make_async_remote_copy(
            src_ref=p3.at[x], dst_ref=p3.at[x], send_sem=csem.at[d], recv_sem=rsem.at[S_C + x],
            device_id=plane_peers[d], device_id_type=MESH,
        )
        for d in range(1, 32)
    ]

    @pl.when(source)
    def _():
        p1[member] = qb[...]
        for m in range(8):

            @pl.when(member != m)
            def _(m=m):
                copy(qb, p1.at[m], S_Q, S_Q + m, col_peers[1]).wait_recv()

        total = p1[0].astype(F32)
        for m in range(1, 8):
            total = total + p1[m].astype(F32)
        p3[x] = total.astype(BF)
        for cp in c_c:
            cp.start()

    def widen(src, dst, lo, n):
        def step(i, carry):
            for h in range(8):
                at = lo + 8 * i + h
                v = src[at]
                r = half_swap(v)
                dst[2 * at] = jnp.concatenate([v * m_left, r * m_right], axis=0)
                dst[2 * at + 1] = jnp.concatenate([r * m_left, v * m_right], axis=0)
            return carry

        lax.fori_loop(0, n, step, 0)

    def spread(load, n):
        tiles = jnp.swapaxes(jnp.stack([load(j).astype(F32) for j in range(32)]), 0, 1)
        even, odd = [], []
        for k in range(0, n, 2):
            one, two = tiles[k], tiles[k + 1]
            even.append(jnp.where(left, one, half_swap(two)))
            odd.append(jnp.where(left, half_swap(one), two))
        rows = [jnp.concatenate(even, axis=1), jnp.concatenate(odd, axis=1)]
        return jnp.concatenate(rows, axis=0).astype(BF)

    def coupled(table, ids, w):
        pairs = [table[ids[k], 0:64, :] + table[ids[k + 1], 64:128, :] for k in range(0, len(ids), 2)]
        return nt(jnp.concatenate(pairs, axis=1), w)

    def in_order(one, two):
        return nn(jnp.concatenate([one, two], axis=1).astype(BF), pp[...])

    c_d = [copy(p4.at[member], p4.at[member], S_D + d, S_D + d, col_peers[d]) for d in range(1, 8)]
    for i in range(4):

        @pl.when(jnp.logical_not(source & (x == i)))
        def _(i=i):
            copy(p3.at[i], p3.at[i], S_C, S_C + i, col_peers[1]).wait_recv()

    have = []
    for i in (0, 2):
        up = p3[i] * m_left + half_swap(p3[i + 1]) * m_right
        down = half_swap(p3[i]) * m_left + p3[i + 1] * m_right
        have.append(jnp.concatenate([up, down], axis=0))
    d = nt(jnp.concatenate(have, axis=1), zb[...])
    p4[member] = jnp.concatenate([d[:32], d[32:]], axis=1).astype(BF)
    for cp in c_d:
        cp.start()

    for cp in c_u:
        cp.wait_recv()
    g0 = (gu[0].astype(F32) + gu[1].astype(F32)).astype(BF)
    g1 = (gu[2].astype(F32) + gu[3].astype(F32)).astype(BF)
    g2 = (nn(g0[:, :64], ge[0]) + nn(g1[:, :64], ge[1])).astype(BF)
    gt[3] = g0 + half_swap(g0)
    gt[4] = g1 + half_swap(g1)
    gt[5] = g2
    gt[9] = jnp.zeros((64, 128), BF)
    c_gt = [
        send(gt.at[pl.ds(3, 3)], gt.at[pl.ds(0, 3)], S_GT, g_after),
        send(gt.at[pl.ds(3, 3)], gt.at[pl.ds(6, 3)], S_GT + 1, g_before),
    ]

    ready(w_nb)
    widen(xs, xbd, 4, 1)
    for cp in c_xh:
        cp.wait_recv()
    for at in (0, 12):
        for h in range(4):
            v = xs[at + h]
            r = half_swap(v)
            xbd[2 * (at + h)] = jnp.concatenate([v * m_left, r * m_right], axis=0)
            xbd[2 * (at + h) + 1] = jnp.concatenate([r * m_left, v * m_right], axis=0)

    def near_step(i, carry):
        weights = []
        for h in range(8):
            t = 8 * i + h
            weights.append(spread(lambda j: nb[t, :, 128 * j : 128 * j + 128], 8))
        parts = []
        for h in range(8):
            ids = [jnp.clip(near_list[k, 8 * i + h] - (b * 16 - 8), 0, 31) for k in range(8)]
            parts.append(coupled(xbd, ids, weights[h]))
        for h in range(4):
            nearp[4 * i + h] = in_order(parts[2 * h], parts[2 * h + 1])
        return carry

    lax.fori_loop(0, 2, near_step, 0)

    ready(w_lc)

    def far_blocks(i, carry):
        for h in range(8):
            c = jnp.minimum(8 * i + h, 30)
            wf[8 * i + h] = spread(lambda j: lc[c, :, 128 * j : 128 * j + 128], 8)
        return carry

    lax.fori_loop(0, 4, far_blocks, 0)

    def far_step(i, carry):
        parts = []
        for h in range(8):
            c = jnp.minimum(8 * i + h, 30)
            count = jnp.where(8 * i + h < 31, local_count[c], 0)
            ids = []
            for k in range(8):
                e = jnp.clip(local_partner[k, c] - (b - 1) * 31, 0, 92)
                e = e + jnp.where(e >= 31, 1, 0) + jnp.where(e >= 62, 1, 0)
                ids.append(jnp.where(k < count, e, 63))
            parts.append(coupled(bdt, ids, wf[8 * i + h]))
        for h in range(4):
            far[4 * i + h] = in_order(parts[2 * h], parts[2 * h + 1])
        return carry

    widen(tab, bdt, 16, 2)
    for cp in c_leaves:
        cp.wait_recv()
    widen(tab, bdt, 0, 1)
    widen(tab, bdt, 32, 1)
    lax.fori_loop(0, 2, far_step, 0)

    ready(w_gc)
    for cp in c_gt:
        cp.wait_recv()
    found = []
    for c in range(3):
        w = spread(lambda j: gc[c, :, 128 * j : 128 * j + 128], 4)
        entries = []
        for k in range(4):
            e = jnp.clip(group_partner[c, k] - (leaf - 1) * 3, 0, 8)
            entries.append(gt[jnp.where(k < group_count[c], e, 9)])
        pairs = [entries[k] * m_left + entries[k + 1] * m_right for k in (0, 2)]
        found.append(nt(jnp.concatenate(pairs, axis=1), w))
    f01 = in_order(found[0], found[1])
    f2 = in_order(found[2], found[2])
    f_half = jnp.where(half == 0, f01, half_swap(f01))[:, :64]
    d_half = f_half + nt(f2[:, :64].astype(BF), ge[half][:, :64])

    for cp in c_upper:
        cp.wait_recv()
    widen(tab, bdt, 8, 1)
    widen(tab, bdt, 40, 1)
    lax.fori_loop(2, 4, far_step, 0)

    e_root = es[30 * 64 : 31 * 64, :]
    d_root = far[15][:, :64] + nt(d_half.astype(BF), e_root[:, :64])
    state = jnp.concatenate([d_root, nt(eye, hr[...][:, :64])], axis=0).astype(BF)
    nothing = jnp.zeros((64, 128), F32)

    def with_far(v, i):
        return (v + jnp.concatenate([far[i], nothing], axis=0)).astype(BF)

    states = [with_far(nt(state, es[28 * 64 : 30 * 64, :64]), 14)]
    for first, pair in ((24, 12), (16, 8), (0, 0)):
        lower_level = []
        for i, parents in enumerate(states):
            at = (first + 4 * i) * 64
            both = nt(parents, es[at : at + 256, :])
            lower_level.append(with_far(both[:, :128], pair + 2 * i))
            lower_level.append(with_far(both[:, 128:], pair + 2 * i + 1))
        states = lower_level
    for m in range(8):
        r = nn(states[m], bd[m])
        nearp[m] = nearp[m] + r[:64]
        vht[m] = r[64:].astype(BF)

    for cp in c_d:
        cp.wait_recv()
    total = p4[0].astype(F32)
    for m in range(1, 8):
        total = total + p4[m].astype(F32)
    d_col = jnp.concatenate([total[:, :64], total[:, 64:]], axis=0).astype(BF)
    for m in range(8):
        out[:, 128 * m : 128 * m + 128] = nearp[m] + nn(d_col, vht[m])

    for cp in c_u + c_xh + c_leaves + c_upper + c_gt + c_d:
        cp.wait_send()

    @pl.when(source)
    def _():
        for cp in c_c:
            cp.wait_send()

    @pl.when(jnp.logical_not(source))
    def _():
        c_q.wait_send()


def body(
    right_sides, leaf_basis, near_blocks, near_list, local_transfer, local_couple, local_partner, local_count,
    group_transfer, group_couple, group_partner, group_count, top_transfer, top_couple, top_partner, top_count,
):
    hbm = pl.BlockSpec(memory_space=pltpu.HBM)
    vm = pltpu.VMEM
    return pl.pallas_call(
        kernel,
        out_shape=jax.ShapeDtypeStruct((64, 1024), F32),
        in_specs=[hbm] * 16,
        out_specs=pl.BlockSpec(memory_space=pltpu.VMEM),
        scratch_shapes=[
            vm((16, 64, 128), BF),
            vm((64, 1024), BF),
            vm((16, 8, 4096), BF),
            vm((31, 4096), BF),
            vm((31, 8, 4096), BF),
            vm((3, 4096), BF),
            vm((3, 4, 4096), BF),
            vm((62, 4096), BF),
            vm((3, 63, 4096), BF),
            vm((31 * 64, 128), BF),
            vm((3, 64, 128), BF),
            vm((16 * 64, 128), BF),
            vm((18, 64, 128), BF),
            vm((32, 64, 512), BF),
            vm((8, 128, 128), BF),
            vm((48, 64, 128), BF),
            vm((96, 128, 128), BF),
            vm((32, 128, 128), BF),
            vm((128, 128), BF),
            vm((32, 128), BF),
            vm((64, 128), BF),
            vm((8, 32, 128), BF),
            vm((4, 32, 128), BF),
            vm((8, 32, 128), BF),
            vm((64, 128), BF),
            vm((4, 64, 128), BF),
            vm((10, 64, 128), BF),
            vm((18, 64, 128), F32),
            vm((64, 256), BF),
            vm((16, 64, 128), F32),
            vm((8, 64, 128), F32),
            vm((8, 64, 128), BF),
            pltpu.SMEM((8, 16), jnp.int32),
            pltpu.SMEM((8, 31), jnp.int32),
            pltpu.SMEM((31,), jnp.int32),
            pltpu.SMEM((3, 4), jnp.int32),
            pltpu.SMEM((3,), jnp.int32),
            pltpu.SMEM((3, 63), jnp.int32),
            pltpu.SMEM((63,), jnp.int32),
            pltpu.SemaphoreType.DMA((24,)),
            pltpu.SemaphoreType.DMA((N_SEM,)),
            pltpu.SemaphoreType.DMA((N_SEM,)),
            pltpu.SemaphoreType.DMA((32,)),
        ],
        compiler_params=pltpu.CompilerParams(
            collective_id=0, has_side_effects=True, vmem_limit_bytes=48 * 1024 * 1024
        ),
        name="h2",
    )(
        *[pltpu.with_memory_space_constraint(v, pltpu.HBM) for v in (
        near_list.T, local_partner.T, local_count, group_partner, group_count, top_partner.T, top_count,
        right_sides, leaf_basis, near_blocks, local_transfer, local_couple, group_transfer, group_couple,
        top_transfer, jnp.transpose(top_couple, (1, 0, 2)),
        )],
    )


def solution(mesh):
    both = ("leaf", "sub")
    placed = (
        P(None, both), P(None, both), P(both, None, None), P(both, None), P(both, None), P(both, None, None),
        P(both, None), P(both), P("leaf", None), P("leaf", None, None), P("leaf", None), P("leaf"),
        P(), P(), P(), P(),
    )
    return jax.shard_map(body, mesh=mesh, in_specs=placed, out_specs=P(None, both), check_vma=False)
```
